512 devices in a mesh: dp: 32 (over x_hi, z, core), cuts: 16 (over x_lo, y).
Axes of the slice: x: 4 (x_hi: 2, x_lo: 2; x = x_hi * 2 + x_lo), y: 8, z: 8, core: 2. Of those that a mesh axis runs over, the one named last changes fastest.
Arguments:
- tokens: bfloat16 [4096, 2048], P('dp', 'cuts'), may hold values from -6 to 6
- cotangent: bfloat16 [4096, 2048], P('dp', 'cuts'), may hold values from -6 to 6
- gates: float32 [4096, 2], P('dp'), may hold values from 0.1 to 1
- routes: int32 [4096, 2], P('dp'), may hold values from 0 to 31, all different within a row; in each aligned block of 128 rows (0 to 127, 128 to 255, ...) at most 12 rows name the same one
- w_in: bfloat16 [32, 2048, 4096], P('dp', None, 'cuts'), may hold values from -0.125 to 0.125
- w_out: bfloat16 [32, 4096, 2048], P('dp', 'cuts'), may hold values from -0.09375 to 0.09375
Outputs:
- mixed: bfloat16 [4096, 2048], P('dp', 'cuts')
- token_grad: bfloat16 [4096, 2048], P('dp', 'cuts')
- grad_in: bfloat16 [32, 2048, 4096], P('dp', None, 'cuts')
- grad_out: bfloat16 [32, 4096, 2048], P('dp', 'cuts')
The draws below stay inside these ranges and needn't reach their ends.
Inputs may be any that keep to these rules, and one draw needn't show every extreme that they name: `routes`: each row names 2 different experts. Within the rows of one device (aligned blocks of 128 rows) no expert is named by more than 12 rows, a bound that some block reaches.
All inputs are finite; a program needn't handle non-finite values.
Results may differ from the reference program's by a relative error of at most 0.024.
Values may be sent and summed in bfloat16 or wider, within the bound.
No kernel may reach another device: no remote copies, remote signals or barrier semaphores. Data moves between devices by JAX's collectives and lax.ppermute only.
A program may use at most 64 MiB of HBM per device.

```python
import math
import jax
import jax.numpy as jnp
import numpy as np
from jax import lax

D = 2048
FF = 4096
TOP = 2
TOK_DEV = 128
EXPERTS = 32
CAP = 12
TOKENS = 4096
N_DP = 32
N_CUTS = 16


def steps_of(rng, extent, split, smallest, top_value):
    def one(axis_at, blocks):
        steps = jax.random.uniform(jax.random.fold_in(jax.random.fold_in(rng, 6), axis_at), (blocks,), jnp.float32, smallest / len(split), top_value / len(split))
        return jnp.repeat(jnp.exp(steps), extent[axis_at] // blocks).reshape((-1,) + (1,) * (len(extent) - axis_at - 1))

    gain = one(*split[0])
    for cut in split[1:]:
        gain = gain * one(*cut)
    return gain


def assign_block(stream_key, own, number, rows, count, top, most, skew):
    ranking = jax.random.permutation(stream_key, count)
    crowded, usual = shares(count, rows * top, most, skew, True), shares(count, rows * top, most, skew, False)
    places = jnp.arange(count)

    def named(lengths, rotation):
        used = int((lengths > 0).sum())
        fixed = max(1, used // 4)
        passed = fixed + (places - fixed + rotation * (used - fixed)) % max(1, count - fixed)
        return jnp.zeros((count,), jnp.int32).at[ranking[jnp.where(places < fixed, places, passed)]].set(jnp.asarray(lengths, jnp.int32))

    lengths = jnp.where(number % 4 == 0, named(crowded, number // 4), named(usual, number - number // 4 - 1))
    mixed = jax.random.permutation(jax.random.fold_in(own, 3), count)
    giver, taker = mixed[0:count // 2 * 2:2], mixed[1:count // 2 * 2:2]
    margin = jnp.minimum(lengths[giver] - 1, most - lengths[taker]) // 2
    margin = jnp.where((giver == ranking[0]) | (taker == ranking[0]) | (lengths[taker] == 0), 0, jnp.maximum(margin, 0))
    passed = jax.random.randint(jax.random.fold_in(own, 4), (count // 2,), 0, 1 << 20) % (margin + 1)
    lengths = lengths.at[giver].add(-passed).at[taker].add(passed)
    items = jnp.searchsorted(jnp.cumsum(lengths), jnp.arange(rows * top), side="right").astype(jnp.int32)
    grid = items.reshape(top, rows).T
    grid = grid[jax.random.permutation(jax.random.fold_in(own, 1), rows)]
    rotation = jax.random.randint(jax.random.fold_in(own, 2), (rows, 1), 0, top)
    return jnp.take_along_axis(grid, (jnp.arange(top)[None, :] + rotation) % top, axis=1)


def shares(count, total, bound, lean, full):
    loads = [(1 << 20) // math.isqrt(rank ** lean) + 1 for rank in range(1, count + 1)]
    largest = bound if full else min(bound, max(-(-total // count), total * loads[0] // sum(loads)))
    least = 1 if total - largest >= count - 1 else 0
    holding, rest = [largest] + [least] * (count - 1), total - largest - least * (count - 1)
    while rest > 0:
        free = [i for i in range(1, count) if holding[i] < largest] or [i for i in range(1, count) if holding[i] < bound]
        whole, remaining = sum([loads[i] for i in free]), rest
        for i in free:
            more = min(bound - holding[i], max(1, remaining * loads[i] // whole), rest)
            holding[i] = holding[i] + more
            rest = rest - more
    return np.array(holding)


def centred(key, extent, spread, bound, shards=(), held_as=jnp.bfloat16):
    values = spread * jax.random.normal(key, extent, jnp.float32)
    if shards:
        values = values * steps_of(key, extent, shards, -0.22, 0.18)
    return jnp.clip(values, -bound, bound).astype(held_as)


def setup_inputs(seed: int = 0) -> dict:
    keys = jax.random.split(jax.random.key(seed), 7)
    tokens = centred(keys[0], (TOKENS, D), 1.0, 6.0, ((0, 32), (1, 16)))
    cotangent = centred(keys[1], (TOKENS, D), 1.0, 6.0, ((0, 32), (1, 16)))
    gates = jnp.clip(0.1 + 0.9 * jax.random.uniform(keys[2], (TOKENS, TOP), jnp.float32) ** steps_of(keys[2], (TOKENS, TOP), ((0, 32),), -0.2, 0.2), 0.1, 1.0)
    routes_keys = jax.random.split(jax.random.fold_in(keys[3], 1), TOKENS // TOK_DEV)
    routes_turns = jax.random.permutation(jax.random.fold_in(keys[3], 3), TOKENS // TOK_DEV)
    routes = jax.vmap(lambda own, number: assign_block(jax.random.fold_in(keys[3], 2), own, number, TOK_DEV, EXPERTS, TOP, CAP, 2))(routes_keys, routes_turns).reshape((TOKENS, TOP))
    w_in = centred(keys[4], (EXPERTS, D, FF), D ** -0.5, 0.125, ((0, 32), (2, 16)))
    w_out = centred(keys[5], (EXPERTS, FF, D), FF ** -0.5, 0.09375, ((0, 32), (1, 16)))
    return dict(tokens=tokens, cotangent=cotangent, gates=gates, routes=routes, w_in=w_in, w_out=w_out)


def gelu_parts(pre):
    coef = math.sqrt(2.0 / math.pi)
    inner = coef * (pre + 0.044715 * pre * pre * pre)
    tangent = jnp.tanh(inner)
    value = 0.5 * pre * (1.0 + tangent)
    slope = 0.5 * (1.0 + tangent) + 0.5 * pre * (1.0 - tangent * tangent) * coef * (1.0 + 3.0 * 0.044715 * pre * pre)
    return (value, slope)

def reference(tokens, cotangent, gates, routes, w_in, w_out):
    slots = N_DP * CAP
    rows_all = TOKENS * TOP
    blocks = routes.reshape(N_DP, TOK_DEV * TOP)
    onehot = (blocks[:, :, None] == jnp.arange(EXPERTS, dtype=jnp.int32)[None, None, :]).astype(jnp.int32)
    before = jnp.cumsum(onehot, axis=1) - onehot
    position = lax.optimization_barrier(jnp.sum(before * onehot, axis=2))
    source = jnp.arange(N_DP, dtype=jnp.int32)[:, None]
    target = (blocks * slots + source * CAP + position).reshape(-1).astype(jnp.int32)
    owner = jnp.full((EXPERTS * slots,), rows_all, jnp.int32).at[target].set(jnp.arange(rows_all, dtype=jnp.int32))
    weights = gates.reshape(-1, 1)
    rep_x = jnp.concatenate([jnp.repeat(tokens, TOP, axis=0), jnp.zeros((1, D), jnp.bfloat16)], axis=0)
    scaled = (weights * jnp.repeat(cotangent, TOP, axis=0).astype(jnp.float32)).astype(jnp.bfloat16)
    rep_g = jnp.concatenate([scaled, jnp.zeros((1, D), jnp.bfloat16)], axis=0)
    buf_x = rep_x[owner].reshape(EXPERTS, slots, D)
    buf_g = rep_g[owner].reshape(EXPERTS, slots, D)
    group = FF // N_CUTS

    def expert_pass(items):
        rows_x, rows_g, first, second = items
        pre = jnp.dot(rows_x, first, preferred_element_type=jnp.float32)
        value, slope = gelu_parts(pre)
        active = value.astype(jnp.bfloat16)
        backed = jnp.dot(rows_g, second.T, preferred_element_type=jnp.float32)
        dpre = (backed * slope).astype(jnp.bfloat16)
        pieces = jnp.einsum('rcf,cfd->rcd', active.reshape(slots, N_CUTS, group).astype(jnp.float32), second.reshape(N_CUTS, group, D).astype(jnp.float32))
        out_sum = lax.optimization_barrier(pieces.astype(jnp.bfloat16)).astype(jnp.float32).sum(axis=1)
        gpieces = jnp.einsum('rcf,dcf->rcd', dpre.reshape(slots, N_CUTS, group).astype(jnp.float32), first.reshape(D, N_CUTS, group).astype(jnp.float32))
        back_sum = lax.optimization_barrier(gpieces.astype(jnp.bfloat16)).astype(jnp.float32).sum(axis=1)
        grad_first = jnp.dot(rows_x.T, dpre, preferred_element_type=jnp.float32).astype(jnp.bfloat16)
        grad_second = jnp.dot(active.T, rows_g, preferred_element_type=jnp.float32).astype(jnp.bfloat16)
        return (out_sum, back_sum, grad_first, grad_second)
    out_all, back_all, grad_in, grad_out = lax.map(expert_pass, (buf_x, buf_g, w_in, w_out))
    picked_out = out_all.reshape(EXPERTS * slots, D)[target]
    picked_back = back_all.reshape(EXPERTS * slots, D)[target]
    mixed = (weights * picked_out).reshape(TOKENS, TOP, D).sum(axis=1).astype(jnp.bfloat16)
    token_grad = picked_back.reshape(TOKENS, TOP, D).sum(axis=1).astype(jnp.bfloat16)
    return (mixed, token_grad, grad_in, grad_out)
```

```python
import functools
import math

import jax
import jax.numpy as jnp
from jax import lax
from jax.experimental import pallas as pl
from jax.experimental.pallas import tpu as pltpu
from jax.sharding import PartitionSpec as P

BF16 = jnp.bfloat16
F32 = jnp.float32
HALVES = 2
PAD = 8


def gelu_parts(pre):
    coef = math.sqrt(2.0 / math.pi)
    inner = coef * (pre + 0.044715 * pre * pre * pre)
    tangent = jnp.tanh(inner)
    value = 0.5 * pre * (1.0 + tangent)
    slope = 0.5 * (1.0 + tangent) + 0.5 * pre * (1.0 - tangent * tangent) * coef * (
        1.0 + 3.0 * 0.044715 * pre * pre
    )
    return (value, slope)


def dot(left, right, dims=((1,), (0,))):
    return lax.dot_general(left, right, (dims, ((), ())), preferred_element_type=F32)


def iota(shape, axis):
    return lax.broadcasted_iota(jnp.int32, shape, axis)


def place_kernel(experts, cap, routes_ref, gates_ref, tok_ref, cot_ref, sent_ref, rows_ref):
    tok_rows, width = tok_ref.shape
    routes = routes_ref[...]
    first, second = routes[0:1, :], routes[1:2, :]
    names = iota((experts, tok_rows), 0)
    hit0, hit1 = names == first, names == second
    either = jnp.where(hit0 | hit1, 1.0, 0.0).astype(BF16)
    earlier = iota((tok_rows, tok_rows), 0) < iota((tok_rows, tok_rows), 1)
    count = dot(either, jnp.where(earlier, 1.0, 0.0).astype(BF16))
    half_cap = cap // HALVES

    def row_of(hit, expert):
        position = jnp.sum(jnp.where(hit, count, 0.0), axis=0, keepdims=True).astype(jnp.int32)
        upper = jnp.where(position >= half_cap, 1, 0)
        return (expert * HALVES + upper) * PAD + position - upper * half_cap

    row0, row1 = row_of(hit0, first), row_of(hit1, second)
    rows_ref[0:1, :] = row0
    rows_ref[1:2, :] = row1
    chunks = experts * HALVES
    slot = iota((chunks * PAD, tok_rows), 0)
    at0, at1 = slot == row0, slot == row1
    gates = gates_ref[...]
    gate = jnp.sum(
        jnp.where(at0, gates[0:1, :], 0.0) + jnp.where(at1, gates[1:2, :], 0.0),
        axis=1,
        keepdims=True,
    )
    select = jnp.where(at0 | at1, 1.0, 0.0).astype(BF16)
    both = dot(select, jnp.concatenate([tok_ref[...], cot_ref[...]], axis=1))
    held_x = both[:, :width].reshape(chunks, PAD, width)
    held_g = (both[:, width:] * gate).reshape(chunks, PAD, width)
    sent_ref[...] = jnp.concatenate([held_x, held_g], axis=1).astype(BF16)


def packing(sources, used):
    shape = (sources * used, sources * PAD)
    at = iota(shape, 1)
    inner = lax.bitwise_and(at, PAD - 1)
    outer = lax.shift_right_logical(at, 3)
    hit = (iota(shape, 0) == outer * used + inner) & (inner < used)
    return jnp.where(hit, 1.0, 0.0).astype(BF16)


def pack_kernel(sources, used, recv_ref, out_ref):
    width = recv_ref.shape[2]
    pick = packing(sources, used)
    held = recv_ref[...].astype(F32).reshape(sources, HALVES, 2, PAD, width)
    rows = sources * used
    for kind in range(2):
        for part in range(HALVES):
            piece = held[:, part, kind].reshape(sources * PAD, width).astype(BF16)
            start = (kind * HALVES + part) * rows
            out_ref[start : start + rows, :] = dot(pick, piece).astype(BF16)


def sum_kernel(sources, used, recv_ref, out_ref):
    groups, _, width = recv_ref.shape
    pick = packing(sources, used)
    rows = sources * used
    kinds = []
    for kind in range(2):
        parts = []
        for part in range(HALVES):
            start = (kind * HALVES + part) * rows
            total = recv_ref[0, start : start + rows, :].astype(F32)
            for group in range(1, groups):
                total = total + recv_ref[group, start : start + rows, :].astype(F32)
            spread = dot(pick, total.astype(BF16), ((0,), (0,)))
            parts.append(spread.reshape(sources, 1, PAD, width))
        kinds.append(jnp.concatenate(parts, axis=1))
    whole = jnp.concatenate(kinds, axis=2)
    out_ref[...] = whole.reshape(sources * HALVES, 2 * PAD, width).astype(BF16)


def expert_kernel(
    recv_ref, in0_ref, in1_ref, out0_ref, out1_ref, ret_ref, x_ref, g_ref, act_ref, dpre_ref
):
    peers, all_rows, width = recv_ref.shape
    rows = all_rows // (2 * HALVES)
    for kind, ref in ((0, x_ref), (1, g_ref)):
        for part in range(HALVES):
            start = (kind * HALVES + part) * rows
            for peer in range(peers):
                at = (part * peers + peer) * width
                ref[:, at : at + width] = recv_ref[peer, start : start + rows, :]
    ins, outs = (in0_ref, in1_ref), (out0_ref, out1_ref)
    acts, dpres = [], []
    for group in range(2):
        pre = dot(x_ref[...], ins[group][...])
        value, slope = gelu_parts(pre)
        backed = dot(g_ref[...], outs[group][...], ((1,), (1,)))
        acts.append(value.astype(BF16))
        dpres.append((backed * slope).astype(BF16))
        act_ref[group] = acts[group]
        dpre_ref[group] = dpres[group]
    for part in range(HALVES):
        for pair in range(peers // 2):
            at = (part * peers + 2 * pair) * width
            cols = slice(at, at + 2 * width)
            given = dot(acts[0], outs[0][:, cols]) + dot(acts[1], outs[1][:, cols])
            back = dot(dpres[0], ins[0][cols, :], ((1,), (1,))) + dot(
                dpres[1], ins[1][cols, :], ((1,), (1,))
            )
            for kind, block in ((0, given), (1, back)):
                block = block.astype(BF16)
                start = (kind * HALVES + part) * rows
                ret_ref[2 * pair, start : start + rows, :] = block[:, :width]
                ret_ref[2 * pair + 1, start : start + rows, :] = block[:, width:]


def combine_kernel(rows_ref, gates_ref, home_ref, mixed_ref, grad_ref):
    chunks, _, width = home_ref.shape
    tok_rows = mixed_ref.shape[0]
    held = home_ref[...].astype(F32)
    given = held[:, :PAD].reshape(chunks * PAD, width).astype(BF16)
    back = held[:, PAD:].reshape(chunks * PAD, width).astype(BF16)
    slot = iota((chunks * PAD, tok_rows), 0)
    at0, at1 = slot == rows_ref[0:1, :], slot == rows_ref[1:2, :]
    diagonal = iota((tok_rows, tok_rows), 0) == iota((tok_rows, tok_rows), 1)

    def mask(hit):
        return jnp.where(hit, 1.0, 0.0).astype(BF16)

    def column(row):
        return jnp.sum(jnp.where(diagonal, row, 0.0), axis=1, keepdims=True)

    over_rows = ((0,), (0,))
    mixed = column(gates_ref[0:1, :]) * dot(mask(at0), given, over_rows) + column(
        gates_ref[1:2, :]
    ) * dot(mask(at1), given, over_rows)
    mixed_ref[...] = mixed.astype(BF16)
    grad_ref[...] = dot(mask(at0 | at1), back, over_rows).astype(BF16)


def call(kernel, shapes, flops, moved, *args):
    return pl.pallas_call(
        kernel,
        out_shape=shapes,
        cost_estimate=pl.CostEstimate(flops=flops, bytes_accessed=moved, transcendentals=0),
        compiler_params=pltpu.CompilerParams(vmem_limit_bytes=40 * 1024 * 1024),
    )(*args)


def struct(*shape, dtype=BF16):
    return jax.ShapeDtypeStruct(shape, dtype)


def body(tokens, cotangent, gates, routes, w_in, w_out):
    experts = lax.axis_size("dp")
    cuts = lax.axis_size("cuts")
    peers = cuts // HALVES
    tok_rows, width = tokens.shape
    chosen = routes.shape[1]
    cap = 3 * chosen * tok_rows // (2 * experts)
    used = cap // HALVES
    chunks = experts * HALVES
    rows = experts * used
    model = width * cuts
    swap = [(c, (c + peers) % cuts) for c in range(cuts)]
    line = [[h * peers + y for y in range(peers)] for h in range(HALVES)]
    plane = [
        [d * cuts + h * peers + y for d in range(experts) for h in range(HALVES)]
        for y in range(peers)
    ]

    def to_partner(value):
        return lax.ppermute(value, "cuts", swap)

    def over_plane(value):
        return lax.all_to_all(value, ("dp", "cuts"), 0, 0, tiled=True, axis_index_groups=plane)

    def over_line(value):
        return lax.all_to_all(value, "cuts", 0, 0, tiled=True, axis_index_groups=line)

    in_own, out_own = w_in[0], w_out[0]
    hidden = in_own.shape[1]
    in_other, out_other = to_partner(in_own), to_partner(out_own)
    routes_t, gates_t = routes.T, gates.T

    sent, places = call(
        functools.partial(place_kernel, experts, cap),
        (struct(chunks, 2 * PAD, width), struct(chosen, tok_rows, dtype=jnp.int32)),
        4 * chunks * PAD * tok_rows * width,
        8 * chunks * PAD * width,
        routes_t,
        gates_t,
        tokens,
        cotangent,
    )
    recv = over_plane(sent)
    packed = call(
        functools.partial(pack_kernel, experts, used),
        struct(4 * rows, width),
        8 * rows * experts * PAD * width,
        8 * rows * 4 * width,
        recv,
    )
    lined = over_line(jnp.broadcast_to(packed[None], (peers, 4 * rows, width)))
    ret, held_x, held_g, active, dpre = call(
        expert_kernel,
        (
            struct(peers, 4 * rows, width),
            struct(rows, model),
            struct(rows, model),
            struct(2, rows, hidden),
            struct(2, rows, hidden),
        ),
        16 * rows * model * hidden,
        24 * rows * model,
        lined,
        in_own,
        in_other,
        out_own,
        out_other,
    )
    returned = over_line(ret)
    over_rows = ((0,), (0,))
    sent_in = to_partner(dot(held_x, dpre[1], over_rows).astype(BF16))
    sent_out = to_partner(dot(active[1], held_g, over_rows).astype(BF16))
    summed = call(
        functools.partial(sum_kernel, experts, used),
        struct(chunks, 2 * PAD, width),
        8 * rows * experts * PAD * width,
        8 * rows * peers * width,
        returned,
    )
    home = over_plane(summed)
    grad_in = (dot(held_x, dpre[0], over_rows) + sent_in.astype(F32)).astype(BF16)[None]
    grad_out = (dot(active[0], held_g, over_rows) + sent_out.astype(F32)).astype(BF16)[None]
    mixed, token_grad = call(
        combine_kernel,
        (struct(tok_rows, width), struct(tok_rows, width)),
        6 * chunks * PAD * tok_rows * width,
        8 * chunks * PAD * width,
        places,
        gates_t,
        home,
    )
    return (mixed, token_grad, grad_in, grad_out)


def solution(mesh):
    in_specs = (
        P("dp", "cuts"),
        P("dp", "cuts"),
        P("dp", None),
        P("dp", None),
        P("dp", None, "cuts"),
        P("dp", "cuts", None),
    )
    out_specs = (P("dp", "cuts"), P("dp", "cuts"), P("dp", None, "cuts"), P("dp", "cuts", None))
    return jax.shard_map(body, mesh=mesh, in_specs=in_specs, out_specs=out_specs, check_vma=False)
```

```python
import functools
import math

import jax
import jax.numpy as jnp
from jax import lax
from jax.experimental import pallas as pl
from jax.experimental.pallas import tpu as pltpu
from jax.sharding import PartitionSpec as P

BF16 = jnp.bfloat16
F32 = jnp.float32
HALVES = 2
PAD = 8


def gelu_parts(pre):
    coef = math.sqrt(2.0 / math.pi)
    inner = coef * (pre + 0.044715 * pre * pre * pre)
    tangent = jnp.tanh(inner)
    value = 0.5 * pre * (1.0 + tangent)
    slope = 0.5 * (1.0 + tangent) + 0.5 * pre * (1.0 - tangent * tangent) * coef * (
        1.0 + 3.0 * 0.044715 * pre * pre
    )
    return (value, slope)


def dot(left, right, dims=((1,), (0,))):
    return lax.dot_general(left, right, (dims, ((), ())), preferred_element_type=F32)


def iota(shape, axis):
    return lax.broadcasted_iota(jnp.int32, shape, axis)


def place_kernel(experts, cap, routes_in, gates_in, tok_in, cot_in, sent_ref, rows_ref, *scratch):
    routes_ref, gates_ref, both_ref, sems = scratch
    tok_rows, width = tok_in.shape
    copies = [
        pltpu.make_async_copy(routes_in, routes_ref, sems.at[0]),
        pltpu.make_async_copy(gates_in, gates_ref, sems.at[1]),
        pltpu.make_async_copy(tok_in, both_ref.at[:, pl.ds(0, width)], sems.at[2]),
        pltpu.make_async_copy(cot_in, both_ref.at[:, pl.ds(width, width)], sems.at[3]),
    ]
    for copy in copies:
        copy.start()
    copies[0].wait()
    routes = routes_ref[...]
    first, second = routes[0:1, :], routes[1:2, :]
    names = iota((experts, tok_rows), 0)
    hit0, hit1 = names == first, names == second
    either = jnp.where(hit0 | hit1, 1.0, 0.0).astype(BF16)
    earlier = iota((tok_rows, tok_rows), 0) < iota((tok_rows, tok_rows), 1)
    count = dot(either, jnp.where(earlier, 1.0, 0.0).astype(BF16))
    half_cap = cap // HALVES

    def row_of(hit, expert):
        position = jnp.sum(jnp.where(hit, count, 0.0), axis=0, keepdims=True).astype(jnp.int32)
        upper = jnp.where(position >= half_cap, 1, 0)
        return (expert * HALVES + upper) * PAD + position - upper * half_cap

    row0, row1 = row_of(hit0, first), row_of(hit1, second)
    rows_ref[0:1, :] = row0
    rows_ref[1:2, :] = row1
    chunks = experts * HALVES
    slot = iota((chunks * PAD, tok_rows), 0)
    at0, at1 = slot == row0, slot == row1
    copies[1].wait()
    gates = gates_ref[...]
    gate = jnp.sum(
        jnp.where(at0, gates[0:1, :], 0.0) + jnp.where(at1, gates[1:2, :], 0.0),
        axis=1,
        keepdims=True,
    )
    select = jnp.where(at0 | at1, 1.0, 0.0).astype(BF16)
    copies[2].wait()
    copies[3].wait()
    both = dot(select, both_ref[...])
    held_x = both[:, :width].reshape(chunks, PAD, width)
    held_g = (both[:, width:] * gate).reshape(chunks, PAD, width)
    sent_ref[...] = jnp.concatenate([held_x, held_g], axis=1).astype(BF16)


def packing(sources, used):
    shape = (sources * used, sources * PAD)
    at = iota(shape, 1)
    inner = lax.bitwise_and(at, PAD - 1)
    outer = lax.shift_right_logical(at, 3)
    hit = (iota(shape, 0) == outer * used + inner) & (inner < used)
    return jnp.where(hit, 1.0, 0.0).astype(BF16)


def pack_kernel(sources, used, recv_ref, x_out, g_out, x_ref, g_ref, sems):
    width = recv_ref.shape[2]
    pick = packing(sources, used)
    held = recv_ref[...].astype(F32).reshape(sources, HALVES, 2, PAD, width)
    rows = sources * used
    copies = []
    for kind, ref, out in ((0, x_ref, x_out), (1, g_ref, g_out)):
        for part in range(HALVES):
            piece = held[:, part, kind].reshape(sources * PAD, width).astype(BF16)
            ref[part * rows : (part + 1) * rows, :] = dot(pick, piece).astype(BF16)
        for peer in range(out.shape[0]):
            copies.append(pltpu.make_async_copy(ref, out.at[peer], sems.at[kind, peer]))
            copies[-1].start()
    for copy in copies:
        copy.wait()


def sum_kernel(sources, used, given_ref, back_ref, out_ref):
    groups, _, width = given_ref.shape
    pick = packing(sources, used)
    rows = sources * used
    kinds = []
    for ref in (given_ref, back_ref):
        parts = []
        for part in range(HALVES):
            start = part * rows
            total = ref[0, start : start + rows, :].astype(F32)
            for group in range(1, groups):
                total = total + ref[group, start : start + rows, :].astype(F32)
            spread = dot(pick, total.astype(BF16), ((0,), (0,)))
            parts.append(spread.reshape(sources, 1, PAD, width))
        kinds.append(jnp.concatenate(parts, axis=1))
    whole = jnp.concatenate(kinds, axis=2)
    out_ref[...] = whole.reshape(sources * HALVES, 2 * PAD, width).astype(BF16)


def fetch_rows(recv, held_ref, sems):
    peers, both_rows, width = recv.shape
    rows = both_rows // HALVES
    copies = []
    for part in range(HALVES):
        for peer in range(peers):
            at = (part * peers + peer) * width
            copies.append(
                pltpu.make_async_copy(
                    recv.at[peer, pl.ds(part * rows, rows), :],
                    held_ref.at[:, pl.ds(at, width)],
                    sems.at[part * peers + peer],
                )
            )
            copies[-1].start()
    return copies


def fetch_weights(own, head, tail, other, refs, sems):
    in0_ref, in1_ref, out0_ref, out1_ref = refs
    cut = head.shape[0]
    return {
        "in0": [pltpu.make_async_copy(own[0], in0_ref, sems.at[0])],
        "in1": [
            pltpu.make_async_copy(head, in1_ref.at[pl.ds(0, cut), :], sems.at[1]),
            pltpu.make_async_copy(tail, in1_ref.at[pl.ds(cut, tail.shape[0]), :], sems.at[2]),
        ],
        "out0": [pltpu.make_async_copy(own[1], out0_ref, sems.at[3])],
        "out1": [pltpu.make_async_copy(other, out1_ref, sems.at[4])],
    }


def send_blocks(ret_ref, ret_out, sems, product):
    peers, both_rows, width = ret_ref.shape
    rows = both_rows // HALVES
    copies = []
    for part in range(HALVES):
        at_rows = pl.ds(part * rows, rows)
        for pair in range(peers // 2):
            at = (part * peers + 2 * pair) * width
            block = product(slice(at, at + 2 * width)).astype(BF16)
            for side in range(2):
                peer = 2 * pair + side
                ret_ref[peer, at_rows, :] = block[:, side * width : (side + 1) * width]
                copies.append(
                    pltpu.make_async_copy(
                        ret_ref.at[peer, at_rows, :],
                        ret_out.at[peer, at_rows, :],
                        sems.at[part * peers + peer],
                    )
                )
                copies[-1].start()
    return copies


def forward_kernel(
    recv, in_own, in_head, in_tail, out_own, out_other, ret_out, x_out, act_ref, slope_ref, *scratch
):
    x_ref, in0, in1, out0, out1, ret_ref, row_sems, weight_sems, ret_sems, x_sem = scratch
    rows = fetch_rows(recv, x_ref, row_sems)
    weights = fetch_weights(
        (in_own, out_own), in_head, in_tail, out_other, (in0, in1, out0, out1), weight_sems
    )
    for name in ("in0", "in1", "out0", "out1"):
        for copy in weights[name]:
            copy.start()
    for copy in rows:
        copy.wait()
    kept = pltpu.make_async_copy(x_ref, x_out, x_sem.at[0])
    kept.start()
    acts = []
    for group, (name, ref) in enumerate((("in0", in0), ("in1", in1))):
        for copy in weights[name]:
            copy.wait()
        value, slope = gelu_parts(dot(x_ref[...], ref[...]))
        acts.append(value.astype(BF16))
        act_ref[group] = acts[group]
        slope_ref[group] = slope
    for name in ("out0", "out1"):
        for copy in weights[name]:
            copy.wait()
    sent = send_blocks(
        ret_ref,
        ret_out,
        ret_sems,
        lambda cols: dot(acts[0], out0[:, cols]) + dot(acts[1], out1[:, cols]),
    )
    for copy in sent + [kept]:
        copy.wait()


def backward_kernel(
    recv, in_own, in_head, in_tail, out_own, out_other, slope_ref, ret_out, g_out, dpre_ref, *scratch
):
    g_ref, in0, in1, out0, out1, ret_ref, row_sems, weight_sems, ret_sems, g_sem = scratch
    rows = fetch_rows(recv, g_ref, row_sems)
    weights = fetch_weights(
        (in_own, out_own), in_head, in_tail, out_other, (in0, in1, out0, out1), weight_sems
    )
    for name in ("out0", "out1", "in0", "in1"):
        for copy in weights[name]:
            copy.start()
    for copy in rows:
        copy.wait()
    kept = pltpu.make_async_copy(g_ref, g_out, g_sem.at[0])
    kept.start()
    dpres = []
    by_last = ((1,), (1,))
    for group, (name, ref) in enumerate((("out0", out0), ("out1", out1))):
        for copy in weights[name]:
            copy.wait()
        backed = dot(g_ref[...], ref[...], by_last)
        dpres.append((backed * slope_ref[group]).astype(BF16))
        dpre_ref[group] = dpres[group]
    for name in ("in0", "in1"):
        for copy in weights[name]:
            copy.wait()
    sent = send_blocks(
        ret_ref,
        ret_out,
        ret_sems,
        lambda cols: dot(dpres[0], in0[cols, :], by_last) + dot(dpres[1], in1[cols, :], by_last),
    )
    for copy in sent + [kept]:
        copy.wait()


def combine_kernel(rows_ref, gates_ref, home_ref, mixed_ref, grad_ref):
    chunks, _, width = home_ref.shape
    tok_rows = mixed_ref.shape[0]
    held = home_ref[...].astype(F32)
    given = held[:, :PAD].reshape(chunks * PAD, width).astype(BF16)
    back = held[:, PAD:].reshape(chunks * PAD, width).astype(BF16)
    slot = iota((chunks * PAD, tok_rows), 0)
    at0, at1 = slot == rows_ref[0:1, :], slot == rows_ref[1:2, :]
    diagonal = iota((tok_rows, tok_rows), 0) == iota((tok_rows, tok_rows), 1)

    def mask(hit):
        return jnp.where(hit, 1.0, 0.0).astype(BF16)

    def column(row):
        return jnp.sum(jnp.where(diagonal, row, 0.0), axis=1, keepdims=True)

    over_rows = ((0,), (0,))
    mixed = column(gates_ref[0:1, :]) * dot(mask(at0), given, over_rows) + column(
        gates_ref[1:2, :]
    ) * dot(mask(at1), given, over_rows)
    mixed_ref[...] = mixed.astype(BF16)
    grad_ref[...] = dot(mask(at0 | at1), back, over_rows).astype(BF16)


def call(kernel, shapes, cost, places, limit, scratch, *args):
    ins, outs = places
    flops, moved = cost
    return pl.pallas_call(
        kernel,
        out_shape=shapes,
        in_specs=[pl.BlockSpec(memory_space=place) for place in ins],
        out_specs=tuple(pl.BlockSpec(memory_space=place) for place in outs),
        scratch_shapes=scratch,
        cost_estimate=pl.CostEstimate(flops=flops, bytes_accessed=moved, transcendentals=0),
        compiler_params=pltpu.CompilerParams(vmem_limit_bytes=limit * 1024 * 1024),
    )(*args)


def struct(*shape, dtype=BF16):
    return jax.ShapeDtypeStruct(shape, dtype)


def body(tokens, cotangent, gates, routes, w_in, w_out):
    experts = lax.axis_size("dp")
    cuts = lax.axis_size("cuts")
    peers = cuts // HALVES
    tok_rows, width = tokens.shape
    chosen = routes.shape[1]
    cap = 3 * chosen * tok_rows // (2 * experts)
    used = cap // HALVES
    chunks = experts * HALVES
    rows = experts * used
    both_rows = HALVES * rows
    model = width * cuts
    near, far = pltpu.VMEM, pltpu.HBM
    dma = pltpu.SemaphoreType.DMA
    swap = [(c, (c + peers) % cuts) for c in range(cuts)]
    line = [[h * peers + y for y in range(peers)] for h in range(HALVES)]
    plane = [
        [d * cuts + h * peers + y for d in range(experts) for h in range(HALVES)]
        for y in range(peers)
    ]

    def to_partner(value):
        return lax.ppermute(value, "cuts", swap)

    def over_plane(value):
        return lax.all_to_all(value, ("dp", "cuts"), 0, 0, tiled=True, axis_index_groups=plane)

    def over_line(value):
        return lax.all_to_all(value, "cuts", 0, 0, tiled=True, axis_index_groups=line)

    in_own, out_own = w_in[0], w_out[0]
    hidden = in_own.shape[1]
    cut = model * 3 // 4
    in_head = to_partner(in_own[:cut])
    in_tail, out_other = to_partner(in_own[cut:]), to_partner(out_own)
    routes_t, gates_t = routes.T, gates.T

    sent, places = call(
        functools.partial(place_kernel, experts, cap),
        (struct(chunks, 2 * PAD, width), struct(chosen, tok_rows, dtype=jnp.int32)),
        (4 * chunks * PAD * tok_rows * width, 8 * chunks * PAD * width),
        ([far] * 4, [near] * 2),
        16,
        [
            pltpu.VMEM((chosen, tok_rows), jnp.int32),
            pltpu.VMEM((chosen, tok_rows), F32),
            pltpu.VMEM((tok_rows, 2 * width), BF16),
            dma((4,)),
        ],
        routes_t,
        gates_t,
        tokens,
        cotangent,
    )
    recv = over_plane(sent)
    spread_x, spread_g = call(
        functools.partial(pack_kernel, experts, used),
        (struct(peers, both_rows, width), struct(peers, both_rows, width)),
        (8 * rows * experts * PAD * width, 8 * both_rows * peers * width),
        ([near], [far] * 2),
        16,
        [
            pltpu.VMEM((both_rows, width), BF16),
            pltpu.VMEM((both_rows, width), BF16),
            dma((2, peers)),
        ],
        recv,
    )
    spread_x, spread_g, in_head = lax.optimization_barrier((spread_x, spread_g, in_head))
    lined_x, lined_g = over_line(spread_x), over_line(spread_g)
    blocks = [
        pltpu.VMEM((rows, model), BF16),
        pltpu.VMEM((model, hidden), BF16),
        pltpu.VMEM((model, hidden), BF16),
        pltpu.VMEM((hidden, model), BF16),
        pltpu.VMEM((hidden, model), BF16),
        pltpu.VMEM((peers, both_rows, width), BF16),
        dma((cuts,)),
        dma((5,)),
        dma((cuts,)),
        dma((1,)),
    ]
    work = (8 * rows * model * hidden, 4 * rows * model + 8 * model * hidden)
    given, held_x, active, slope = call(
        forward_kernel,
        (
            struct(peers, both_rows, width),
            struct(rows, model),
            struct(2, rows, hidden),
            struct(2, rows, hidden, dtype=F32),
        ),
        work,
        ([far] * 6, [far, far, near, near]),
        32,
        blocks,
        lined_x,
        in_own,
        in_head,
        in_tail,
        out_own,
        out_other,
    )
    back_given = over_line(given)
    back, held_g, dpre = call(
        backward_kernel,
        (
            struct(peers, both_rows, width),
            struct(rows, model),
            struct(2, rows, hidden),
        ),
        work,
        ([far] * 6 + [near], [far, far, near]),
        32,
        blocks,
        lined_g,
        in_own,
        in_head,
        in_tail,
        out_own,
        out_other,
        slope,
    )
    back_back = over_line(back)
    over_rows = ((0,), (0,))
    sent_in = to_partner(dot(held_x, dpre[1], over_rows).astype(BF16))
    sent_out = to_partner(dot(active[1], held_g, over_rows).astype(BF16))
    summed = call(
        functools.partial(sum_kernel, experts, used),
        (struct(chunks, 2 * PAD, width),),
        (8 * rows * experts * PAD * width, 8 * rows * peers * width),
        ([near] * 2, [near]),
        16,
        [],
        back_given,
        back_back,
    )[0]
    home = over_plane(summed)
    grad_in = (dot(held_x, dpre[0], over_rows) + sent_in.astype(F32)).astype(BF16)[None]
    grad_out = (dot(active[0], held_g, over_rows) + sent_out.astype(F32)).astype(BF16)[None]
    mixed, token_grad = call(
        combine_kernel,
        (struct(tok_rows, width), struct(tok_rows, width)),
        (6 * chunks * PAD * tok_rows * width, 8 * chunks * PAD * width),
        ([near] * 3, [near] * 2),
        16,
        [],
        places,
        gates_t,
        home,
    )
    return (mixed, token_grad, grad_in, grad_out)


def solution(mesh):
    in_specs = (
        P("dp", "cuts"),
        P("dp", "cuts"),
        P("dp", None),
        P("dp", None),
        P("dp", None, "cuts"),
        P("dp", "cuts", None),
    )
    out_specs = (P("dp", "cuts"), P("dp", "cuts"), P("dp", None, "cuts"), P("dp", "cuts", None))
    return jax.shard_map(body, mesh=mesh, in_specs=in_specs, out_specs=out_specs, check_vma=False)
```

```python
import functools
import math

import jax
import jax.numpy as jnp
from jax import lax
from jax.experimental import pallas as pl
from jax.experimental.pallas import tpu as pltpu
from jax.sharding import PartitionSpec as P

BF16 = jnp.bfloat16
F32 = jnp.float32
HALVES = 2
PAD = 8


def gelu_parts(pre):
    coef = math.sqrt(2.0 / math.pi)
    inner = coef * (pre + 0.044715 * pre * pre * pre)
    tangent = jnp.tanh(inner)
    value = 0.5 * pre * (1.0 + tangent)
    slope = 0.5 * (1.0 + tangent) + 0.5 * pre * (1.0 - tangent * tangent) * coef * (
        1.0 + 3.0 * 0.044715 * pre * pre
    )
    return (value, slope)


def dot(left, right, dims=((1,), (0,))):
    return lax.dot_general(left, right, (dims, ((), ())), preferred_element_type=F32)


def iota(shape, axis):
    return lax.broadcasted_iota(jnp.int32, shape, axis)


def place_kernel(experts, cap, routes_in, gates_in, tok_in, cot_in, sent_ref, rows_ref, *scratch):
    routes_ref, gates_ref, both_ref, sems = scratch
    tok_rows, width = tok_in.shape
    copies = [
        pltpu.make_async_copy(routes_in, routes_ref, sems.at[0]),
        pltpu.make_async_copy(gates_in, gates_ref, sems.at[1]),
        pltpu.make_async_copy(tok_in, both_ref.at[:, pl.ds(0, width)], sems.at[2]),
        pltpu.make_async_copy(cot_in, both_ref.at[:, pl.ds(width, width)], sems.at[3]),
    ]
    for copy in copies:
        copy.start()
    copies[0].wait()
    routes = routes_ref[...]
    first, second = routes[0:1, :], routes[1:2, :]
    names = iota((experts, tok_rows), 0)
    hit0, hit1 = names == first, names == second
    either = jnp.where(hit0 | hit1, 1.0, 0.0).astype(BF16)
    earlier = iota((tok_rows, tok_rows), 0) < iota((tok_rows, tok_rows), 1)
    count = dot(either, jnp.where(earlier, 1.0, 0.0).astype(BF16))
    half_cap = cap // HALVES

    def row_of(hit, expert):
        position = jnp.sum(jnp.where(hit, count, 0.0), axis=0, keepdims=True).astype(jnp.int32)
        upper = jnp.where(position >= half_cap, 1, 0)
        return (expert * HALVES + upper) * PAD + position - upper * half_cap

    row0, row1 = row_of(hit0, first), row_of(hit1, second)
    rows_ref[0:1, :] = row0
    rows_ref[1:2, :] = row1
    chunks = experts * HALVES
    slot = iota((chunks * PAD, tok_rows), 0)
    at0, at1 = slot == row0, slot == row1
    copies[1].wait()
    gates = gates_ref[...]
    gate = jnp.sum(
        jnp.where(at0, gates[0:1, :], 0.0) + jnp.where(at1, gates[1:2, :], 0.0),
        axis=1,
        keepdims=True,
    )
    select = jnp.where(at0 | at1, 1.0, 0.0).astype(BF16)
    copies[2].wait()
    copies[3].wait()
    both = dot(select, both_ref[...])
    held_x = both[:, :width].reshape(chunks, PAD, width)
    held_g = (both[:, width:] * gate).reshape(chunks, PAD, width)
    sent_ref[...] = jnp.concatenate([held_x, held_g], axis=1).astype(BF16)


def packing(sources, used):
    shape = (sources * used, sources * PAD)
    at = iota(shape, 1)
    inner = lax.bitwise_and(at, PAD - 1)
    outer = lax.shift_right_logical(at, 3)
    hit = (iota(shape, 0) == outer * used + inner) & (inner < used)
    return jnp.where(hit, 1.0, 0.0).astype(BF16)


def pack_kernel(sources, used, recv_ref, out, held_ref, sems):
    width = recv_ref.shape[2]
    pick = packing(sources, used)
    held = recv_ref[...].astype(F32).reshape(sources, HALVES, 2, PAD, width)
    rows = sources * used
    copies = []
    for kind in range(2):
        for part in range(HALVES):
            piece = held[:, part, kind].reshape(sources * PAD, width).astype(BF16)
            start = (kind * HALVES + part) * rows
            held_ref[start : start + rows, :] = dot(pick, piece).astype(BF16)
        at = pl.ds(kind * HALVES * rows, HALVES * rows)
        for peer in range(out.shape[0]):
            copies.append(
                pltpu.make_async_copy(held_ref.at[at, :], out.at[peer, at, :], sems.at[kind, peer])
            )
            copies[-1].start()
    for copy in copies:
        copy.wait()


def sum_kernel(sources, used, recv_ref, out_ref):
    groups, _, width = recv_ref.shape
    pick = packing(sources, used)
    rows = sources * used
    kinds = []
    for kind in range(2):
        parts = []
        for part in range(HALVES):
            start = (kind * HALVES + part) * rows
            total = recv_ref[0, start : start + rows, :].astype(F32)
            for group in range(1, groups):
                total = total + recv_ref[group, start : start + rows, :].astype(F32)
            spread = dot(pick, total.astype(BF16), ((0,), (0,)))
            parts.append(spread.reshape(sources, 1, PAD, width))
        kinds.append(jnp.concatenate(parts, axis=1))
    whole = jnp.concatenate(kinds, axis=2)
    out_ref[...] = whole.reshape(sources * HALVES, 2 * PAD, width).astype(BF16)


def expert_kernel(
    recv, in_own, in_head, in_tail, out_own, out_other, ret_out, x_out, g_out, act_ref, dpre_ref, *scratch
):
    x_ref, g_ref, in0, in1, out0, out1, ret_ref, row_sems, weight_sems, ret_sems, kept_sems = scratch
    peers, all_rows, width = recv.shape
    rows = all_rows // (2 * HALVES)
    cut = in_head.shape[0]

    def fetch_rows(kind, ref):
        copies = []
        for part in range(HALVES):
            start = (kind * HALVES + part) * rows
            for peer in range(peers):
                index = part * peers + peer
                copies.append(
                    pltpu.make_async_copy(
                        recv.at[peer, pl.ds(start, rows), :],
                        ref.at[:, pl.ds(index * width, width)],
                        row_sems.at[kind, index],
                    )
                )
                copies[-1].start()
        return copies

    rows_x = fetch_rows(0, x_ref)
    load_in = [
        [pltpu.make_async_copy(in_own, in0, weight_sems.at[0])],
        [
            pltpu.make_async_copy(in_head, in1.at[pl.ds(0, cut), :], weight_sems.at[1]),
            pltpu.make_async_copy(
                in_tail, in1.at[pl.ds(cut, in1.shape[0] - cut), :], weight_sems.at[2]
            ),
        ],
    ]
    load_out = [
        [pltpu.make_async_copy(out_own, out0, weight_sems.at[3])],
        [pltpu.make_async_copy(out_other, out1, weight_sems.at[4])],
    ]
    for copies in load_in:
        for copy in copies:
            copy.start()
    rows_g = fetch_rows(1, g_ref)
    for copies in load_out:
        for copy in copies:
            copy.start()
    sent = []

    def send(kind, product):
        for part in range(HALVES):
            at_rows = pl.ds((kind * HALVES + part) * rows, rows)
            for pair in range(peers // 2):
                at = (part * peers + 2 * pair) * width
                block = product(slice(at, at + 2 * width)).astype(BF16)
                for side in range(2):
                    peer = 2 * pair + side
                    ret_ref[peer, at_rows, :] = block[:, side * width : (side + 1) * width]
                    sent.append(
                        pltpu.make_async_copy(
                            ret_ref.at[peer, at_rows, :],
                            ret_out.at[peer, at_rows, :],
                            ret_sems.at[kind, part * peers + peer],
                        )
                    )
                    sent[-1].start()

    def keep(ref, out, index):
        sent.append(pltpu.make_async_copy(ref, out, kept_sems.at[index]))
        sent[-1].start()

    by_last = ((1,), (1,))
    for copy in rows_x:
        copy.wait()
    keep(x_ref, x_out, 0)
    acts, slopes, dpres = [], [], []
    for group, ref in enumerate((in0, in1)):
        for copy in load_in[group]:
            copy.wait()
        value, slope = gelu_parts(dot(x_ref[...], ref[...]))
        acts.append(value.astype(BF16))
        slopes.append(slope)
        act_ref[group] = acts[group]
    for copy in rows_g:
        copy.wait()
    keep(g_ref, g_out, 1)
    for group, ref in enumerate((out0, out1)):
        for copy in load_out[group]:
            copy.wait()
        dpres.append((dot(g_ref[...], ref[...], by_last) * slopes[group]).astype(BF16))
        dpre_ref[group] = dpres[group]
    send(0, lambda cols: dot(acts[0], out0[:, cols]) + dot(acts[1], out1[:, cols]))
    send(
        1,
        lambda cols: dot(dpres[0], in0[cols, :], by_last) + dot(dpres[1], in1[cols, :], by_last),
    )
    for copy in sent:
        copy.wait()


def combine_kernel(rows_ref, gates_ref, home_ref, mixed_ref, grad_ref):
    chunks, _, width = home_ref.shape
    tok_rows = mixed_ref.shape[0]
    held = home_ref[...].astype(F32)
    given = held[:, :PAD].reshape(chunks * PAD, width).astype(BF16)
    back = held[:, PAD:].reshape(chunks * PAD, width).astype(BF16)
    slot = iota((chunks * PAD, tok_rows), 0)
    at0, at1 = slot == rows_ref[0:1, :], slot == rows_ref[1:2, :]
    diagonal = iota((tok_rows, tok_rows), 0) == iota((tok_rows, tok_rows), 1)

    def mask(hit):
        return jnp.where(hit, 1.0, 0.0).astype(BF16)

    def column(row):
        return jnp.sum(jnp.where(diagonal, row, 0.0), axis=1, keepdims=True)

    over_rows = ((0,), (0,))
    mixed = column(gates_ref[0:1, :]) * dot(mask(at0), given, over_rows) + column(
        gates_ref[1:2, :]
    ) * dot(mask(at1), given, over_rows)
    mixed_ref[...] = mixed.astype(BF16)
    grad_ref[...] = dot(mask(at0 | at1), back, over_rows).astype(BF16)


def call(kernel, shapes, cost, places, limit, scratch, *args):
    ins, outs = places
    flops, moved = cost
    return pl.pallas_call(
        kernel,
        out_shape=shapes,
        in_specs=[pl.BlockSpec(memory_space=place) for place in ins],
        out_specs=tuple(pl.BlockSpec(memory_space=place) for place in outs),
        scratch_shapes=scratch,
        cost_estimate=pl.CostEstimate(flops=flops, bytes_accessed=moved, transcendentals=0),
        compiler_params=pltpu.CompilerParams(vmem_limit_bytes=limit * 1024 * 1024),
    )(*args)


def struct(*shape, dtype=BF16):
    return jax.ShapeDtypeStruct(shape, dtype)


def body(tokens, cotangent, gates, routes, w_in, w_out):
    experts = lax.axis_size("dp")
    cuts = lax.axis_size("cuts")
    peers = cuts // HALVES
    tok_rows, width = tokens.shape
    chosen = routes.shape[1]
    cap = 3 * chosen * tok_rows // (2 * experts)
    used = cap // HALVES
    chunks = experts * HALVES
    rows = experts * used
    both_rows = HALVES * rows
    model = width * cuts
    near, far = pltpu.VMEM, pltpu.HBM
    dma = pltpu.SemaphoreType.DMA
    swap = [(c, (c + peers) % cuts) for c in range(cuts)]
    line = [[h * peers + y for y in range(peers)] for h in range(HALVES)]
    plane = [
        [d * cuts + h * peers + y for d in range(experts) for h in range(HALVES)]
        for y in range(peers)
    ]

    def to_partner(value):
        return lax.ppermute(value, "cuts", swap)

    def over_plane(value):
        return lax.all_to_all(value, ("dp", "cuts"), 0, 0, tiled=True, axis_index_groups=plane)

    def over_line(value):
        return lax.all_to_all(value, "cuts", 0, 0, tiled=True, axis_index_groups=line)

    in_own, out_own = w_in[0], w_out[0]
    hidden = in_own.shape[1]
    cut = model * 3 // 4
    in_head = to_partner(in_own[:cut])
    in_tail, out_other = to_partner(in_own[cut:]), to_partner(out_own)
    routes_t, gates_t = routes.T, gates.T

    sent, places = call(
        functools.partial(place_kernel, experts, cap),
        (struct(chunks, 2 * PAD, width), struct(chosen, tok_rows, dtype=jnp.int32)),
        (4 * chunks * PAD * tok_rows * width, 8 * chunks * PAD * width),
        ([far] * 4, [near] * 2),
        16,
        [
            pltpu.VMEM((chosen, tok_rows), jnp.int32),
            pltpu.VMEM((chosen, tok_rows), F32),
            pltpu.VMEM((tok_rows, 2 * width), BF16),
            dma((4,)),
        ],
        routes_t,
        gates_t,
        tokens,
        cotangent,
    )
    recv = over_plane(sent)
    spread = call(
        functools.partial(pack_kernel, experts, used),
        (struct(peers, 4 * rows, width),),
        (8 * rows * experts * PAD * width, 8 * both_rows * peers * width),
        ([near], [far]),
        56,
        [pltpu.VMEM((4 * rows, width), BF16), dma((2, peers))],
        recv,
    )[0]
    spread, in_head = lax.optimization_barrier((spread, in_head))
    lined = over_line(spread)
    ret, held_x, held_g, active, dpre = call(
        expert_kernel,
        (
            struct(peers, 4 * rows, width),
            struct(rows, model),
            struct(rows, model),
            struct(2, rows, hidden),
            struct(2, rows, hidden),
        ),
        (16 * rows * model * hidden, 12 * rows * model + 8 * model * hidden),
        ([far] * 6, [far] * 3 + [near] * 2),
        60,
        [
            pltpu.VMEM((rows, model), BF16),
            pltpu.VMEM((rows, model), BF16),
            pltpu.VMEM((model, hidden), BF16),
            pltpu.VMEM((model, hidden), BF16),
            pltpu.VMEM((hidden, model), BF16),
            pltpu.VMEM((hidden, model), BF16),
            pltpu.VMEM((peers, 4 * rows, width), BF16),
            dma((2, cuts)),
            dma((5,)),
            dma((2, cuts)),
            dma((2,)),
        ],
        lined,
        in_own,
        in_head,
        in_tail,
        out_own,
        out_other,
    )
    returned = over_line(ret)
    over_rows = ((0,), (0,))
    sent_in = to_partner(dot(held_x, dpre[1], over_rows).astype(BF16))
    sent_out = to_partner(dot(active[1], held_g, over_rows).astype(BF16))
    summed = call(
        functools.partial(sum_kernel, experts, used),
        (struct(chunks, 2 * PAD, width),),
        (8 * rows * experts * PAD * width, 8 * rows * peers * width),
        ([near], [near]),
        16,
        [],
        returned,
    )[0]
    home = over_plane(summed)
    grad_in = (dot(held_x, dpre[0], over_rows) + sent_in.astype(F32)).astype(BF16)[None]
    grad_out = (dot(active[0], held_g, over_rows) + sent_out.astype(F32)).astype(BF16)[None]
    mixed, token_grad = call(
        combine_kernel,
        (struct(tok_rows, width), struct(tok_rows, width)),
        (6 * chunks * PAD * tok_rows * width, 8 * chunks * PAD * width),
        ([near] * 3, [near] * 2),
        16,
        [],
        places,
        gates_t,
        home,
    )
    return (mixed, token_grad, grad_in, grad_out)


def solution(mesh):
    in_specs = (
        P("dp", "cuts"),
        P("dp", "cuts"),
        P("dp", None),
        P("dp", None),
        P("dp", None, "cuts"),
        P("dp", "cuts", None),
    )
    out_specs = (P("dp", "cuts"), P("dp", "cuts"), P("dp", None, "cuts"), P("dp", "cuts", None))
    return jax.shard_map(body, mesh=mesh, in_specs=in_specs, out_specs=out_specs, check_vma=False)
```

```python
import functools
import math

import jax
import jax.numpy as jnp
from jax import lax
from jax.experimental import pallas as pl
from jax.experimental.pallas import tpu as pltpu
from jax.sharding import PartitionSpec as P

BF16 = jnp.bfloat16
F32 = jnp.float32
HALVES = 2
FOUR = 4


def gelu_parts(pre):
    coef = math.sqrt(2.0 / math.pi)
    inner = coef * (pre + 0.044715 * pre * pre * pre)
    tangent = jnp.tanh(inner)
    value = 0.5 * pre * (1.0 + tangent)
    slope = 0.5 * (1.0 + tangent) + 0.5 * pre * (1.0 - tangent * tangent) * coef * (
        1.0 + 3.0 * 0.044715 * pre * pre
    )
    return (value, slope)


def dot(left, right, dims=((1,), (0,))):
    return lax.dot_general(left, right, (dims, ((), ())), preferred_element_type=F32)


def iota(shape, axis):
    return lax.broadcasted_iota(jnp.int32, shape, axis)


def mask(hit):
    return jnp.where(hit, 1.0, 0.0).astype(BF16)


def place_kernel(experts, cap, routes_in, gates_in, tok_in, cot_in, sent, rows_ref, *scratch):
    routes_ref, gates_ref, tok_ref, cot_ref, held_ref, sems, sent_sems = scratch
    tok_rows = tok_in.shape[0]
    copies = [
        pltpu.make_async_copy(routes_in, routes_ref, sems.at[0]),
        pltpu.make_async_copy(gates_in, gates_ref, sems.at[1]),
        pltpu.make_async_copy(tok_in, tok_ref, sems.at[2]),
        pltpu.make_async_copy(cot_in, cot_ref, sems.at[3]),
    ]
    for copy in copies:
        copy.start()
    copies[0].wait()
    routes = routes_ref[...]
    first, second = routes[0:1, :], routes[1:2, :]
    names = iota((experts, tok_rows), 0)
    hit0, hit1 = names == first, names == second
    either = jnp.where(hit0 | hit1, 1.0, 0.0).astype(BF16)
    earlier = iota((tok_rows, tok_rows), 0) < iota((tok_rows, tok_rows), 1)
    count = dot(either, jnp.where(earlier, 1.0, 0.0).astype(BF16))
    used = cap // HALVES

    def row_of(hit, expert):
        position = jnp.sum(jnp.where(hit, count, 0.0), axis=0, keepdims=True).astype(jnp.int32)
        upper = jnp.where(position >= used, 1, 0)
        return (expert * HALVES + upper) * cap + position - upper * used

    row0, row1 = row_of(hit0, first), row_of(hit1, second)
    rows_ref[0:1, :] = row0
    rows_ref[1:2, :] = row1
    slot = iota((experts * HALVES * cap, tok_rows), 0)
    at_x = (slot == row0) | (slot == row1)
    at0, at1 = slot == row0 + used, slot == row1 + used
    copies[1].wait()
    gates = gates_ref[...]
    gate = jnp.sum(
        jnp.where(at0, gates[0:1, :], 0.0) + jnp.where(at1, gates[1:2, :], 0.0),
        axis=1,
        keepdims=True,
    )
    copies[2].wait()
    copies[3].wait()
    held_x = dot(mask(at_x), tok_ref[...])
    held_g = dot(mask(at0 | at1), cot_ref[...]) * gate
    held_ref[...] = (held_x + held_g).astype(BF16)
    copies = [
        pltpu.make_async_copy(held_ref, sent.at[index], sent_sems.at[index])
        for index in range(sent.shape[0])
    ]
    for copy in copies:
        copy.start()
    for copy in copies:
        copy.wait()


def sorted_row(at, used, sources):
    group = 4 * used
    scale = -(-(1 << 16) // group)
    source = lax.shift_right_logical(at * scale, 16)
    inner = at - source * group
    block = lax.shift_right_logical(inner * -(-(1 << 16) // used), 16)
    return block * (sources * used) + source * used + inner - block * used


def expert_kernel(used, odd_ref, own, low, high, in_own, in_other, out_own, out_head, out_tail, *rest):
    ret_own, ret_low, ret_high, x_out, g_out, act_ref, dpre_ref = rest[:7]
    recv_ref, pick_ref, spread_ref, x_ref, g_ref, in0, in1, out0, out1, held_ref, ret_ref = rest[7:18]
    recv_sems, weight_sems, ret_sems, kept_sems = rest[18:]
    classes, all_rows, width = own.shape
    peers = 2 * classes
    rows = all_rows // 4
    sources = rows // used
    side = classes // 2
    cut = out_head.shape[0]
    odd = odd_ref[0]

    def columns(index, other):
        place = 2 * index + (1 - odd if other else odd)
        return pl.ds(pl.multiple_of(place * width, width), width)

    moves = [(own, q, columns(q, False)) for q in range(classes)]
    moves += [(low, q, columns(q, True)) for q in range(side)]
    moves += [(high, q, columns(q + side, True)) for q in range(side)]
    arrive = [
        pltpu.make_async_copy(ref.at[q], recv_ref.at[:, cols], recv_sems.at[index])
        for index, (ref, q, cols) in enumerate(moves)
    ]
    load_in = [
        pltpu.make_async_copy(in_own, in0, weight_sems.at[0]),
        pltpu.make_async_copy(in_other, in1, weight_sems.at[1]),
    ]
    load_out = [
        [pltpu.make_async_copy(out_own, out0, weight_sems.at[2])],
        [
            pltpu.make_async_copy(out_head, out1.at[pl.ds(0, cut), :], weight_sems.at[3]),
            pltpu.make_async_copy(
                out_tail, out1.at[pl.ds(cut, out1.shape[0] - cut), :], weight_sems.at[4]
            ),
        ],
    ]
    for copy in arrive + load_in + load_out[0] + load_out[1]:
        copy.start()
    shape = (all_rows, all_rows)
    pick_ref[...] = mask(iota(shape, 0) == sorted_row(iota((1, all_rows), 1), used, sources))
    spread_ref[...] = mask(iota(shape, 1) == sorted_row(iota((all_rows, 1), 0), used, sources))
    for copy in arrive:
        copy.wait()
    for pair in range(classes):
        cols = slice(pair * 2 * width, (pair + 1) * 2 * width)
        block = dot(pick_ref[...], recv_ref[:, cols]).astype(BF16)
        for part in range(HALVES):
            at = (part * peers + 2 * pair) * width
            start = part * 2 * rows
            x_ref[:, at : at + 2 * width] = block[start : start + rows, :]
            g_ref[:, at : at + 2 * width] = block[start + rows : start + 2 * rows, :]
    kept = [
        pltpu.make_async_copy(x_ref, x_out, kept_sems.at[0]),
        pltpu.make_async_copy(g_ref, g_out, kept_sems.at[1]),
    ]
    for copy in kept:
        copy.start()

    by_last = ((1,), (1,))
    acts, slopes, dpres = [], [], []
    for group, ref in enumerate((in0, in1)):
        load_in[group].wait()
        value, slope = gelu_parts(dot(x_ref[...], ref[...]))
        acts.append(value.astype(BF16))
        slopes.append(slope)
        act_ref[group] = acts[group]
    for group, ref in enumerate((out0, out1)):
        for copy in load_out[group]:
            copy.wait()
        dpres.append((dot(g_ref[...], ref[...], by_last) * slopes[group]).astype(BF16))
        dpre_ref[group] = dpres[group]
    for pair in range(classes):
        for part in range(HALVES):
            at = (part * peers + 2 * pair) * width
            cols = slice(at, at + 2 * width)
            given = dot(acts[0], out0[:, cols]) + dot(acts[1], out1[:, cols])
            back = dot(dpres[0], in0[cols, :], by_last) + dot(dpres[1], in1[cols, :], by_last)
            start = part * 2 * rows
            held_ref[start : start + rows, :] = given.astype(BF16)
            held_ref[start + rows : start + 2 * rows, :] = back.astype(BF16)
        ret_ref[:, pair * 2 * width : (pair + 1) * 2 * width] = dot(
            spread_ref[...], held_ref[...]
        ).astype(BF16)
    moves = [(ret_own, q, columns(q, False)) for q in range(classes)]
    moves += [(ret_low, q, columns(q, True)) for q in range(side)]
    moves += [(ret_high, q, columns(q + side, True)) for q in range(side)]
    leave = [
        pltpu.make_async_copy(ret_ref.at[:, cols], ref.at[q], ret_sems.at[index])
        for index, (ref, q, cols) in enumerate(moves)
    ]
    for copy in leave:
        copy.start()
    for copy in leave + kept:
        copy.wait()


def add_kernel(own_ref, low_ref, high_ref, out_ref):
    side = low_ref.shape[0]
    for index in range(own_ref.shape[0]):
        ref = low_ref.at[index] if index < side else high_ref.at[index - side]
        out_ref[index] = (own_ref[index].astype(F32) + ref[...].astype(F32)).astype(BF16)


def combine_kernel(used, rows_ref, gates_ref, home_ref, mixed_ref, grad_ref):
    groups, all_rows, _ = home_ref.shape
    tok_rows = mixed_ref.shape[0]
    slot = iota((all_rows, tok_rows), 0)
    row0, row1 = rows_ref[0:1, :], rows_ref[1:2, :]
    diagonal = iota((tok_rows, tok_rows), 0) == iota((tok_rows, tok_rows), 1)

    def column(row):
        return jnp.sum(jnp.where(diagonal, row, 0.0), axis=1, keepdims=True)

    def picked(hit):
        chosen = mask(hit)
        return sum(dot(chosen, home_ref[group], ((0,), (0,))) for group in range(groups))

    mixed = column(gates_ref[0:1, :]) * picked(slot == row0) + column(
        gates_ref[1:2, :]
    ) * picked(slot == row1)
    mixed_ref[...] = mixed.astype(BF16)
    grad_ref[...] = picked((slot == row0 + used) | (slot == row1 + used)).astype(BF16)


def call(kernel, shapes, cost, places, limit, scratch, *args):
    ins, outs = places
    flops, moved = cost
    return pl.pallas_call(
        kernel,
        out_shape=shapes,
        in_specs=[pl.BlockSpec(memory_space=place) for place in ins],
        out_specs=tuple(pl.BlockSpec(memory_space=place) for place in outs),
        scratch_shapes=scratch,
        cost_estimate=pl.CostEstimate(flops=flops, bytes_accessed=moved, transcendentals=0),
        compiler_params=pltpu.CompilerParams(vmem_limit_bytes=limit * 1024 * 1024),
    )(*args)


def struct(*shape, dtype=BF16):
    return jax.ShapeDtypeStruct(shape, dtype)


def body(tokens, cotangent, gates, routes, w_in, w_out):
    experts = lax.axis_size("dp")
    cuts = lax.axis_size("cuts")
    peers = cuts // HALVES
    classes = peers // 2
    side = classes // 2
    tok_rows, width = tokens.shape
    chosen = routes.shape[1]
    cap = 3 * chosen * tok_rows // (2 * experts)
    used = cap // HALVES
    rows = experts * used
    all_rows = 4 * rows
    model = width * cuts
    near, far = pltpu.VMEM, pltpu.HBM
    dma = pltpu.SemaphoreType.DMA
    swap = [(c, (c + peers) % cuts) for c in range(cuts)]
    up = [(c, c // peers * peers + (c + 1) % peers) for c in range(cuts)]
    down = [(d, c) for c, d in up]
    spread = [
        [d * cuts + h * peers + y for y in range(odd, peers, 2) for d in range(experts) for h in range(HALVES)]
        for odd in range(2)
    ]

    def to_partner(value):
        return lax.ppermute(value, "cuts", swap)

    def over_spread(value):
        pieces = value.reshape(classes * all_rows // FOUR, FOUR, width)
        pieces = lax.all_to_all(pieces, ("dp", "cuts"), 0, 0, tiled=True, axis_index_groups=spread)
        return pieces.reshape(classes, all_rows, width)

    in_own, out_own = w_in[0], w_out[0]
    hidden = in_own.shape[1]
    cut = hidden // 4
    in_other, out_head = to_partner(in_own), to_partner(out_own[:cut])
    routes_t, gates_t = routes.T, gates.T
    odd = (lax.axis_index("cuts") % 2).astype(jnp.int32).reshape(1)

    sent, places = call(
        functools.partial(place_kernel, experts, cap),
        (struct(classes, all_rows, width), struct(chosen, tok_rows, dtype=jnp.int32)),
        (4 * all_rows * tok_rows * width, 4 * classes * all_rows * width),
        ([far] * 4, [far, near]),
        56,
        [
            pltpu.VMEM((chosen, tok_rows), jnp.int32),
            pltpu.VMEM((chosen, tok_rows), F32),
            pltpu.VMEM((tok_rows, width), BF16),
            pltpu.VMEM((tok_rows, width), BF16),
            pltpu.VMEM((all_rows, width), BF16),
            dma((4,)),
            dma((classes,)),
        ],
        routes_t,
        gates_t,
        tokens,
        cotangent,
    )
    recv = over_spread(sent)
    recv, in_other, out_head, out_own_late = lax.optimization_barrier(
        (recv, in_other, out_head, out_own)
    )
    low = lax.ppermute(recv[:side], "cuts", up)
    high = lax.ppermute(recv[side:], "cuts", down)
    out_tail = to_partner(out_own_late[cut:])
    ret_own, ret_low, ret_high, held_x, held_g, active, dpre = call(
        functools.partial(expert_kernel, used),
        (
            struct(classes, all_rows, width),
            struct(side, all_rows, width),
            struct(classes - side, all_rows, width),
            struct(rows, model),
            struct(rows, model),
            struct(2, rows, hidden),
            struct(2, rows, hidden),
        ),
        (16 * rows * model * hidden, 12 * rows * model + 8 * model * hidden),
        ([pltpu.SMEM] + [far] * 8, [far] * 5 + [near] * 2),
        60,
        [
            pltpu.VMEM((all_rows, peers * width), BF16),
            pltpu.VMEM((all_rows, all_rows), BF16),
            pltpu.VMEM((all_rows, all_rows), BF16),
            pltpu.VMEM((rows, model), BF16),
            pltpu.VMEM((rows, model), BF16),
            pltpu.VMEM((model, hidden), BF16),
            pltpu.VMEM((model, hidden), BF16),
            pltpu.VMEM((hidden, model), BF16),
            pltpu.VMEM((hidden, model), BF16),
            pltpu.VMEM((all_rows, 2 * width), BF16),
            pltpu.VMEM((all_rows, peers * width), BF16),
            dma((peers,)),
            dma((5,)),
            dma((peers,)),
            dma((2,)),
        ],
        odd,
        recv,
        low,
        high,
        in_own,
        in_other,
        out_own,
        out_head,
        out_tail,
    )
    from_low = lax.ppermute(ret_low, "cuts", up)
    from_high = lax.ppermute(ret_high, "cuts", down)
    over_rows = ((0,), (0,))
    sent_in = to_partner(dot(held_x, dpre[1], over_rows).astype(BF16))
    sent_out = to_partner(dot(active[1], held_g, over_rows).astype(BF16))
    summed = call(
        add_kernel,
        (struct(classes, all_rows, width),),
        (classes * all_rows * width, 6 * classes * all_rows * width),
        ([near] * 3, [near]),
        16,
        [],
        ret_own,
        from_low,
        from_high,
    )[0]
    home = over_spread(summed)
    grad_in = (dot(held_x, dpre[0], over_rows) + sent_in.astype(F32)).astype(BF16)[None]
    grad_out = (dot(active[0], held_g, over_rows) + sent_out.astype(F32)).astype(BF16)[None]
    mixed, token_grad = call(
        functools.partial(combine_kernel, used),
        (struct(tok_rows, width), struct(tok_rows, width)),
        (6 * classes * all_rows * tok_rows * width, 2 * classes * all_rows * width),
        ([near] * 3, [near] * 2),
        16,
        [],
        places,
        gates_t,
        home,
    )
    return (mixed, token_grad, grad_in, grad_out)


def solution(mesh):
    in_specs = (
        P("dp", "cuts"),
        P("dp", "cuts"),
        P("dp", None),
        P("dp", None),
        P("dp", None, "cuts"),
        P("dp", "cuts", None),
    )
    out_specs = (P("dp", "cuts"), P("dp", "cuts"), P("dp", None, "cuts"), P("dp", "cuts", None))
    return jax.shard_map(body, mesh=mesh, in_specs=in_specs, out_specs=out_specs, check_vma=False)
```

```python
import functools
import math

import jax
import jax.numpy as jnp
from jax import lax
from jax.experimental import pallas as pl
from jax.experimental.pallas import tpu as pltpu
from jax.sharding import PartitionSpec as P

BF16 = jnp.bfloat16
F32 = jnp.float32
HALVES = 2
EARLY = (1, 2)
FOUR = 4


def gelu_parts(pre):
    coef = math.sqrt(2.0 / math.pi)
    inner = coef * (pre + 0.044715 * pre * pre * pre)
    tangent = jnp.tanh(inner)
    value = 0.5 * pre * (1.0 + tangent)
    slope = 0.5 * (1.0 + tangent) + 0.5 * pre * (1.0 - tangent * tangent) * coef * (
        1.0 + 3.0 * 0.044715 * pre * pre
    )
    return (value, slope)


def dot(left, right, dims=((1,), (0,))):
    return lax.dot_general(left, right, (dims, ((), ())), preferred_element_type=F32)


def iota(shape, axis):
    return lax.broadcasted_iota(jnp.int32, shape, axis)


def mask(hit):
    return jnp.where(hit, 1.0, 0.0).astype(BF16)


def weight_blocks(hidden, model, width):
    blocks = [(0, at, model) for at in range(0, hidden, width)]
    return blocks + [(1, at, hidden) for at in range(0, model, width)]


def split_blocks(hidden, model, width):
    blocks = weight_blocks(hidden, model, width)
    count = hidden // width + model // width * EARLY[0] // EARLY[1]
    parts = []
    for part in (blocks[:count], blocks[count:]):
        at, placed = 0, []
        for which, first, rows in part:
            placed.append((which, first, at, rows))
            at += rows
        parts.append((placed, at))
    return parts


def place_kernel(experts, cap, routes_in, gates_in, tok_in, cot_in, in_own, out_own, *refs):
    sent, rows_ref, early, late = refs[:4]
    scratch = refs[4:]
    routes_ref, gates_ref, tok_ref, cot_ref, held_ref, sems, sent_sems, weight_sems = scratch
    tok_rows, width = tok_in.shape
    copies = [
        pltpu.make_async_copy(routes_in, routes_ref, sems.at[0]),
        pltpu.make_async_copy(gates_in, gates_ref, sems.at[1]),
        pltpu.make_async_copy(tok_in, tok_ref, sems.at[2]),
        pltpu.make_async_copy(cot_in, cot_ref, sems.at[3]),
    ]
    for copy in copies:
        copy.start()
    weights = []
    for (placed, _), out in zip(split_blocks(*reversed(in_own.shape), width), (early, late)):
        for which, first, at, rows in placed:
            source = (in_own, out_own)[which].at[:, pl.ds(first, width)]
            weights.append(
                pltpu.make_async_copy(
                    source, out.at[pl.ds(at, rows), :], weight_sems.at[len(weights)]
                )
            )
            weights[-1].start()
    copies[0].wait()
    routes = routes_ref[...]
    first, second = routes[0:1, :], routes[1:2, :]
    names = iota((experts, tok_rows), 0)
    hit0, hit1 = names == first, names == second
    either = jnp.where(hit0 | hit1, 1.0, 0.0).astype(BF16)
    earlier = iota((tok_rows, tok_rows), 0) < iota((tok_rows, tok_rows), 1)
    count = dot(either, jnp.where(earlier, 1.0, 0.0).astype(BF16))
    used = cap // HALVES

    def row_of(hit, expert):
        position = jnp.sum(jnp.where(hit, count, 0.0), axis=0, keepdims=True).astype(jnp.int32)
        upper = jnp.where(position >= used, 1, 0)
        return (expert * HALVES + upper) * cap + position - upper * used

    row0, row1 = row_of(hit0, first), row_of(hit1, second)
    rows_ref[0:1, :] = row0
    rows_ref[1:2, :] = row1
    slot = iota((experts * HALVES * cap, tok_rows), 0)
    at_x = (slot == row0) | (slot == row1)
    at0, at1 = slot == row0 + used, slot == row1 + used
    copies[1].wait()
    gates = gates_ref[...]
    gate = jnp.sum(
        jnp.where(at0, gates[0:1, :], 0.0) + jnp.where(at1, gates[1:2, :], 0.0),
        axis=1,
        keepdims=True,
    )
    copies[2].wait()
    copies[3].wait()
    held_x = dot(mask(at_x), tok_ref[...])
    held_g = dot(mask(at0 | at1), cot_ref[...]) * gate
    held_ref[...] = (held_x + held_g).astype(BF16)
    copies = [
        pltpu.make_async_copy(held_ref, sent.at[index], sent_sems.at[index])
        for index in range(sent.shape[0])
    ]
    for copy in copies:
        copy.start()
    for copy in copies + weights:
        copy.wait()


def sorted_row(at, used, sources):
    group = 4 * used
    scale = -(-(1 << 16) // group)
    source = lax.shift_right_logical(at * scale, 16)
    inner = at - source * group
    block = lax.shift_right_logical(inner * -(-(1 << 16) // used), 16)
    return block * (sources * used) + source * used + inner - block * used


def expert_kernel(used, odd_ref, own, low, high, in_own, out_own, early, late, *rest):
    ret_own, ret_low, ret_high, x_out, g_out, act_ref, dpre_ref = rest[:7]
    recv_ref, pick_ref, spread_ref, x_ref, g_ref, in0, in1, out0, out1, held_ref, ret_ref = rest[7:18]
    recv_sems, weight_sems, ret_sems, kept_sems = rest[18:]
    classes, all_rows, width = own.shape
    peers = 2 * classes
    rows = all_rows // 4
    sources = rows // used
    side = classes // 2
    odd = odd_ref[0]

    def columns(index, other):
        place = 2 * index + (1 - odd if other else odd)
        return pl.ds(pl.multiple_of(place * width, width), width)

    moves = [(own, q, columns(q, False)) for q in range(classes)]
    moves += [(low, q, columns(q, True)) for q in range(side)]
    moves += [(high, q, columns(q + side, True)) for q in range(side)]
    arrive = [
        pltpu.make_async_copy(ref.at[q], recv_ref.at[:, cols], recv_sems.at[index])
        for index, (ref, q, cols) in enumerate(moves)
    ]
    load_in = [[pltpu.make_async_copy(in_own, in0, weight_sems.at[0])], []]
    load_out = [[pltpu.make_async_copy(out_own, out0, weight_sems.at[1])], []]
    for (placed, _), source in zip(split_blocks(*reversed(in0.shape), width), (early, late)):
        for which, first, at, size in placed:
            target = (in1, out1)[which].at[:, pl.ds(first, width)]
            index = 2 + len(load_in[1]) + len(load_out[1])
            (load_in, load_out)[which][1].append(
                pltpu.make_async_copy(
                    source.at[pl.ds(at, size), :], target, weight_sems.at[index]
                )
            )
    for copy in arrive + load_in[0] + load_in[1] + load_out[0] + load_out[1]:
        copy.start()
    shape = (all_rows, all_rows)
    pick_ref[...] = mask(iota(shape, 0) == sorted_row(iota((1, all_rows), 1), used, sources))
    spread_ref[...] = mask(iota(shape, 1) == sorted_row(iota((all_rows, 1), 0), used, sources))
    for copy in arrive:
        copy.wait()
    for pair in range(classes):
        cols = slice(pair * 2 * width, (pair + 1) * 2 * width)
        block = dot(pick_ref[...], recv_ref[:, cols]).astype(BF16)
        for part in range(HALVES):
            at = (part * peers + 2 * pair) * width
            start = part * 2 * rows
            x_ref[:, at : at + 2 * width] = block[start : start + rows, :]
            g_ref[:, at : at + 2 * width] = block[start + rows : start + 2 * rows, :]
    kept = [
        pltpu.make_async_copy(x_ref, x_out, kept_sems.at[0]),
        pltpu.make_async_copy(g_ref, g_out, kept_sems.at[1]),
    ]
    for copy in kept:
        copy.start()

    by_last = ((1,), (1,))
    acts, slopes, dpres = [], [], []
    for group, ref in enumerate((in0, in1)):
        for copy in load_in[group]:
            copy.wait()
        value, slope = gelu_parts(dot(x_ref[...], ref[...]))
        acts.append(value.astype(BF16))
        slopes.append(slope)
        act_ref[group] = acts[group]
    for group, ref in enumerate((out0, out1)):
        for copy in load_out[group]:
            copy.wait()
        dpres.append((dot(g_ref[...], ref[...], by_last) * slopes[group]).astype(BF16))
        dpre_ref[group] = dpres[group]
    leave = []
    for pair in range(classes):
        for part in range(HALVES):
            at = (part * peers + 2 * pair) * width
            cols = slice(at, at + 2 * width)
            given = dot(acts[0], out0[:, cols]) + dot(acts[1], out1[:, cols])
            back = dot(dpres[0], in0[cols, :], by_last) + dot(dpres[1], in1[cols, :], by_last)
            start = part * 2 * rows
            held_ref[start : start + rows, :] = given.astype(BF16)
            held_ref[start + rows : start + 2 * rows, :] = back.astype(BF16)
        ret_ref[:, pair * 2 * width : (pair + 1) * 2 * width] = dot(
            spread_ref[...], held_ref[...]
        ).astype(BF16)
        other = ret_low.at[pair] if pair < side else ret_high.at[pair - side]
        leave.append(
            pltpu.make_async_copy(
                ret_ref.at[:, columns(pair, False)], ret_own.at[pair], ret_sems.at[2 * pair]
            )
        )
        leave.append(
            pltpu.make_async_copy(
                ret_ref.at[:, columns(pair, True)], other, ret_sems.at[2 * pair + 1]
            )
        )
        leave[-2].start()
        leave[-1].start()
    for copy in leave + kept:
        copy.wait()


def partner_kernel(x_ref, g_ref, act_ref, dpre_ref, out_ref):
    over_rows = ((0,), (0,))
    model = x_ref.shape[1]
    hidden, width = dpre_ref.shape[2], out_ref.shape[1]
    for at in range(0, model, hidden):
        part = dot(x_ref[:, at : at + hidden], dpre_ref[1], over_rows).astype(BF16)
        for index in range(hidden // width):
            start = index * model + at
            out_ref[start : start + hidden, :] = part[:, index * width : (index + 1) * width]
        part = dot(act_ref[1], g_ref[:, at : at + hidden], over_rows).astype(BF16)
        for index in range(hidden // width):
            start = hidden // width * model + (at // width + index) * hidden
            out_ref[start : start + hidden, :] = part[:, index * width : (index + 1) * width]


def gradient_kernel(x_ref, g_ref, act_ref, dpre_ref, sent_ref, grad_in_ref, grad_out_ref):
    over_rows = ((0,), (0,))
    model = x_ref.shape[1]
    hidden, width = dpre_ref.shape[2], sent_ref.shape[1]
    for at in range(0, model, hidden):
        part = dot(x_ref[:, at : at + hidden], dpre_ref[0], over_rows)
        for index in range(hidden // width):
            start = index * model + at
            cols = slice(index * width, (index + 1) * width)
            grad_in_ref[0, at : at + hidden, cols] = (
                part[:, cols] + sent_ref[start : start + hidden, :].astype(F32)
            ).astype(BF16)
        part = dot(act_ref[0], g_ref[:, at : at + hidden], over_rows)
        for index in range(hidden // width):
            start = hidden // width * model + (at // width + index) * hidden
            cols = slice(index * width, (index + 1) * width)
            grad_out_ref[0, :, at + index * width : at + (index + 1) * width] = (
                part[:, cols] + sent_ref[start : start + hidden, :].astype(F32)
            ).astype(BF16)


def add_kernel(own_ref, low_ref, high_ref, out_ref):
    side = low_ref.shape[0]
    for index in range(own_ref.shape[0]):
        ref = low_ref.at[index] if index < side else high_ref.at[index - side]
        out_ref[index] = (own_ref[index].astype(F32) + ref[...].astype(F32)).astype(BF16)


def combine_kernel(used, rows_ref, gates_ref, home_ref, mixed_ref, grad_ref):
    groups, all_rows, _ = home_ref.shape
    tok_rows = mixed_ref.shape[0]
    slot = iota((all_rows, tok_rows), 0)
    row0, row1 = rows_ref[0:1, :], rows_ref[1:2, :]
    diagonal = iota((tok_rows, tok_rows), 0) == iota((tok_rows, tok_rows), 1)

    def column(row):
        return jnp.sum(jnp.where(diagonal, row, 0.0), axis=1, keepdims=True)

    def picked(hit):
        chosen = mask(hit)
        return sum(dot(chosen, home_ref[group], ((0,), (0,))) for group in range(groups))

    mixed = column(gates_ref[0:1, :]) * picked(slot == row0) + column(
        gates_ref[1:2, :]
    ) * picked(slot == row1)
    mixed_ref[...] = mixed.astype(BF16)
    grad_ref[...] = picked((slot == row0 + used) | (slot == row1 + used)).astype(BF16)


def call(kernel, shapes, cost, places, limit, scratch, *args):
    ins, outs = places
    flops, moved = cost
    return pl.pallas_call(
        kernel,
        out_shape=shapes,
        in_specs=[pl.BlockSpec(memory_space=place) for place in ins],
        out_specs=tuple(pl.BlockSpec(memory_space=place) for place in outs),
        scratch_shapes=scratch,
        cost_estimate=pl.CostEstimate(flops=flops, bytes_accessed=moved, transcendentals=0),
        compiler_params=pltpu.CompilerParams(vmem_limit_bytes=limit * 1024 * 1024),
    )(*args)


def struct(*shape, dtype=BF16):
    return jax.ShapeDtypeStruct(shape, dtype)


def body(tokens, cotangent, gates, routes, w_in, w_out):
    experts = lax.axis_size("dp")
    cuts = lax.axis_size("cuts")
    peers = cuts // HALVES
    classes = peers // 2
    side = classes // 2
    tok_rows, width = tokens.shape
    chosen = routes.shape[1]
    cap = 3 * chosen * tok_rows // (2 * experts)
    used = cap // HALVES
    rows = experts * used
    all_rows = 4 * rows
    model = width * cuts
    near, far = pltpu.VMEM, pltpu.HBM
    dma = pltpu.SemaphoreType.DMA
    swap = [(c, (c + peers) % cuts) for c in range(cuts)]
    up = [(c, c // peers * peers + (c + 1) % peers) for c in range(cuts)]
    down = [(d, c) for c, d in up]
    spread = [
        [d * cuts + h * peers + y for y in range(odd, peers, 2) for d in range(experts) for h in range(HALVES)]
        for odd in range(2)
    ]

    def to_partner(value):
        return lax.ppermute(value, "cuts", swap)

    def over_spread(value):
        pieces = value.reshape(classes * all_rows // FOUR, FOUR, width)
        pieces = lax.all_to_all(pieces, ("dp", "cuts"), 0, 0, tiled=True, axis_index_groups=spread)
        return pieces.reshape(classes, all_rows, width)

    in_own, out_own = w_in[0], w_out[0]
    hidden = in_own.shape[1]
    blocks = hidden // width + cuts
    early_rows, late_rows = (part[1] for part in split_blocks(hidden, model, width))
    routes_t, gates_t = routes.T, gates.T
    odd = (lax.axis_index("cuts") % 2).astype(jnp.int32).reshape(1)

    sent, places, early, late = call(
        functools.partial(place_kernel, experts, cap),
        (
            struct(classes, all_rows, width),
            struct(chosen, tok_rows, dtype=jnp.int32),
            struct(early_rows, width),
            struct(late_rows, width),
        ),
        (4 * all_rows * tok_rows * width, 4 * classes * all_rows * width),
        ([far] * 6, [far, near, far, far]),
        56,
        [
            pltpu.VMEM((chosen, tok_rows), jnp.int32),
            pltpu.VMEM((chosen, tok_rows), F32),
            pltpu.VMEM((tok_rows, width), BF16),
            pltpu.VMEM((tok_rows, width), BF16),
            pltpu.VMEM((all_rows, width), BF16),
            dma((4,)),
            dma((classes,)),
            dma((blocks,)),
        ],
        routes_t,
        gates_t,
        tokens,
        cotangent,
        in_own,
        out_own,
    )
    early = to_partner(early)
    recv = over_spread(sent)
    recv, early, late = lax.optimization_barrier((recv, early, late))
    low = lax.ppermute(recv[:side], "cuts", up)
    high = lax.ppermute(recv[side:], "cuts", down)
    late = to_partner(late)
    ret_own, ret_low, ret_high, held_x, held_g, active, dpre = call(
        functools.partial(expert_kernel, used),
        (
            struct(classes, all_rows, width),
            struct(side, all_rows, width),
            struct(classes - side, all_rows, width),
            struct(rows, model),
            struct(rows, model),
            struct(2, rows, hidden),
            struct(2, rows, hidden),
        ),
        (16 * rows * model * hidden, 12 * rows * model + 8 * model * hidden),
        ([pltpu.SMEM] + [far] * 7, [far] * 5 + [near] * 2),
        60,
        [
            pltpu.VMEM((all_rows, peers * width), BF16),
            pltpu.VMEM((all_rows, all_rows), BF16),
            pltpu.VMEM((all_rows, all_rows), BF16),
            pltpu.VMEM((rows, model), BF16),
            pltpu.VMEM((rows, model), BF16),
            pltpu.VMEM((model, hidden), BF16),
            pltpu.VMEM((model, hidden), BF16),
            pltpu.VMEM((hidden, model), BF16),
            pltpu.VMEM((hidden, model), BF16),
            pltpu.VMEM((all_rows, 2 * width), BF16),
            pltpu.VMEM((all_rows, peers * width), BF16),
            dma((peers,)),
            dma((2 + blocks,)),
            dma((peers,)),
            dma((2,)),
        ],
        odd,
        recv,
        low,
        high,
        in_own,
        out_own,
        early,
        late,
    )
    from_low = lax.ppermute(ret_low, "cuts", up)
    from_high = lax.ppermute(ret_high, "cuts", down)
    sent_grads = call(
        partner_kernel,
        (struct(early_rows + late_rows, width),),
        (8 * rows * model * hidden, 8 * model * hidden),
        ([near] * 4, [near]),
        24,
        [],
        held_x,
        held_g,
        active,
        dpre,
    )[0]
    sent_grads = to_partner(sent_grads)
    summed = call(
        add_kernel,
        (struct(classes, all_rows, width),),
        (classes * all_rows * width, 6 * classes * all_rows * width),
        ([near] * 3, [near]),
        16,
        [],
        ret_own,
        from_low,
        from_high,
    )[0]
    home = over_spread(summed)
    grad_in, grad_out = call(
        gradient_kernel,
        (struct(1, model, hidden), struct(1, hidden, model)),
        (8 * rows * model * hidden, 16 * model * hidden),
        ([near] * 5, [near] * 2),
        32,
        [],
        held_x,
        held_g,
        active,
        dpre,
        sent_grads,
    )
    mixed, token_grad = call(
        functools.partial(combine_kernel, used),
        (struct(tok_rows, width), struct(tok_rows, width)),
        (6 * classes * all_rows * tok_rows * width, 2 * classes * all_rows * width),
        ([near] * 3, [near] * 2),
        16,
        [],
        places,
        gates_t,
        home,
    )
    return (mixed, token_grad, grad_in, grad_out)


def solution(mesh):
    in_specs = (
        P("dp", "cuts"),
        P("dp", "cuts"),
        P("dp", None),
        P("dp", None),
        P("dp", None, "cuts"),
        P("dp", "cuts", None),
    )
    out_specs = (P("dp", "cuts"), P("dp", "cuts"), P("dp", None, "cuts"), P("dp", "cuts", None))
    return jax.shard_map(body, mesh=mesh, in_specs=in_specs, out_specs=out_specs, check_vma=False)
```

```python
import functools
import math

import jax
import jax.numpy as jnp
from jax import lax
from jax.experimental import pallas as pl
from jax.experimental.pallas import tpu as pltpu
from jax.sharding import PartitionSpec as P

BF16 = jnp.bfloat16
F32 = jnp.float32
HALVES = 2
EARLY = (1, 2)
GROUP = 8
FOUR = 4


def gelu_parts(pre):
    coef = math.sqrt(2.0 / math.pi)
    inner = coef * (pre + 0.044715 * pre * pre * pre)
    tangent = jnp.tanh(inner)
    value = 0.5 * pre * (1.0 + tangent)
    slope = 0.5 * (1.0 + tangent) + 0.5 * pre * (1.0 - tangent * tangent) * coef * (
        1.0 + 3.0 * 0.044715 * pre * pre
    )
    return (value, slope)


def dot(left, right, dims=((1,), (0,))):
    return lax.dot_general(left, right, (dims, ((), ())), preferred_element_type=F32)


def iota(shape, axis):
    return lax.broadcasted_iota(jnp.int32, shape, axis)


def mask(hit):
    return jnp.where(hit, 1.0, 0.0).astype(BF16)


def weight_blocks(hidden, model, width):
    blocks = [(0, at, model) for at in range(0, hidden, width)]
    return blocks + [(1, at, hidden) for at in range(0, model, width)]


def split_blocks(hidden, model, width):
    blocks = weight_blocks(hidden, model, width)
    count = hidden // width + model // width * EARLY[0] // EARLY[1]
    parts = []
    for part in (blocks[:count], blocks[count:]):
        at, placed = 0, []
        for which, first, rows in part:
            placed.append((which, first, at, rows))
            at += rows
        parts.append((placed, at))
    return parts


def place_kernel(experts, cap, routes_in, gates_in, tok_in, cot_in, in_own, out_own, *refs):
    sent, rows_ref, early, late = refs[:4]
    scratch = refs[4:]
    routes_ref, gates_ref, tok_ref, cot_ref, held_ref, in_ref, out_ref, sems, sent_sems, load_sems, weight_sems = scratch
    tok_rows, width = tok_in.shape
    copies = [
        pltpu.make_async_copy(routes_in, routes_ref, sems.at[0]),
        pltpu.make_async_copy(gates_in, gates_ref, sems.at[1]),
        pltpu.make_async_copy(tok_in, tok_ref, sems.at[2]),
        pltpu.make_async_copy(cot_in, cot_ref, sems.at[3]),
    ]
    for copy in copies:
        copy.start()
    loads = [
        pltpu.make_async_copy(in_own, in_ref, load_sems.at[0]),
        pltpu.make_async_copy(out_own, out_ref, load_sems.at[1]),
    ]
    for copy in loads:
        copy.start()
    copies[0].wait()
    routes = routes_ref[...]
    first, second = routes[0:1, :], routes[1:2, :]
    names = iota((experts, tok_rows), 0)
    hit0, hit1 = names == first, names == second
    either = jnp.where(hit0 | hit1, 1.0, 0.0).astype(BF16)
    earlier = iota((tok_rows, tok_rows), 0) < iota((tok_rows, tok_rows), 1)
    count = dot(either, jnp.where(earlier, 1.0, 0.0).astype(BF16))
    used = cap // HALVES

    def row_of(hit, expert):
        position = jnp.sum(jnp.where(hit, count, 0.0), axis=0, keepdims=True).astype(jnp.int32)
        upper = jnp.where(position >= used, 1, 0)
        return (expert * HALVES + upper) * cap + position - upper * used

    row0, row1 = row_of(hit0, first), row_of(hit1, second)
    rows_ref[0:1, :] = row0
    rows_ref[1:2, :] = row1
    slot = iota((experts * HALVES * cap, tok_rows), 0)
    at_x = (slot == row0) | (slot == row1)
    at0, at1 = slot == row0 + used, slot == row1 + used
    copies[1].wait()
    gates = gates_ref[...]
    gate = jnp.sum(
        jnp.where(at0, gates[0:1, :], 0.0) + jnp.where(at1, gates[1:2, :], 0.0),
        axis=1,
        keepdims=True,
    )
    copies[2].wait()
    copies[3].wait()
    for copy in loads:
        copy.wait()
    weights = []
    for (placed, _), out in zip(split_blocks(*reversed(in_own.shape), width), (early, late)):
        for which, first, at, rows in placed:
            source = (in_ref, out_ref)[which].at[:, pl.ds(first, width)]
            weights.append(
                pltpu.make_async_copy(
                    source, out.at[pl.ds(at, rows), :], weight_sems.at[len(weights)]
                )
            )
            weights[-1].start()
    held_x = dot(mask(at_x), tok_ref[...])
    held_g = dot(mask(at0 | at1), cot_ref[...]) * gate
    held_ref[...] = (held_x + held_g).astype(BF16)
    copies = [
        pltpu.make_async_copy(held_ref, sent.at[index], sent_sems.at[index])
        for index in range(sent.shape[0])
    ]
    for copy in copies:
        copy.start()
    for copy in copies + weights:
        copy.wait()


def sorted_row(at, used, sources):
    group = 4 * used
    scale = -(-(1 << 16) // group)
    source = lax.shift_right_logical(at * scale, 16)
    inner = at - source * group
    block = lax.shift_right_logical(inner * -(-(1 << 16) // used), 16)
    return block * (sources * used) + source * used + inner - block * used


def expert_kernel(used, odd_ref, own, low, high, in_own, out_own, early, late, *rest):
    ret_own, ret_low, ret_high, x_out, g_out, act_ref, dpre_ref, share_out = rest[:8]
    recv_ref, x_ref, g_ref, in0, in1, out0, out1, held_ref, ret_ref, share_ref = rest[8:18]
    recv_sems, weight_sems, ret_sems, kept_sems, share_sems = rest[18:]
    classes, all_rows, width = own.shape
    peers = 2 * classes
    rows = all_rows // 4
    sources = rows // used
    side = classes // 2
    odd = odd_ref[0]

    def columns(index, other):
        place = 2 * index + (1 - odd if other else odd)
        return pl.ds(pl.multiple_of(place * width, width), width)

    moves = [(own, q, columns(q, False)) for q in range(classes)]
    moves += [(low, q, columns(q, True)) for q in range(side)]
    moves += [(high, q, columns(q + side, True)) for q in range(side)]
    arrive = [
        pltpu.make_async_copy(ref.at[q], recv_ref.at[:, cols], recv_sems.at[index])
        for index, (ref, q, cols) in enumerate(moves)
    ]
    load_in = [[pltpu.make_async_copy(in_own, in0, weight_sems.at[0])], []]
    load_out = [[pltpu.make_async_copy(out_own, out0, weight_sems.at[1])], []]
    for (placed, _), source in zip(split_blocks(*reversed(in0.shape), width), (early, late)):
        for which, first, at, size in placed:
            target = (in1, out1)[which].at[:, pl.ds(first, width)]
            index = 2 + len(load_in[1]) + len(load_out[1])
            (load_in, load_out)[which][1].append(
                pltpu.make_async_copy(
                    source.at[pl.ds(at, size), :], target, weight_sems.at[index]
                )
            )
    for copy in arrive + load_in[0] + load_in[1] + load_out[0] + load_out[1]:
        copy.start()
    batch = GROUP if sources % GROUP == 0 else sources
    size = 4 * used * batch
    part_rows = used * batch
    pick = mask(iota((size, size), 0) == sorted_row(iota((1, size), 1), used, batch))
    spread = mask(iota((size, size), 1) == sorted_row(iota((size, 1), 0), used, batch))
    for copy in arrive:
        copy.wait()
    for pair in range(classes):
        cols = slice(pair * 2 * width, (pair + 1) * 2 * width)
        for at_group in range(sources // batch):
            block = dot(pick, recv_ref[at_group * size : (at_group + 1) * size, cols]).astype(BF16)
            here = slice(at_group * part_rows, (at_group + 1) * part_rows)
            for part in range(HALVES):
                at = (part * peers + 2 * pair) * width
                start = part * 2 * part_rows
                x_ref[here, at : at + 2 * width] = block[start : start + part_rows, :]
                start = start + part_rows
                g_ref[here, at : at + 2 * width] = block[start : start + part_rows, :]
    kept = [
        pltpu.make_async_copy(x_ref, x_out, kept_sems.at[0]),
        pltpu.make_async_copy(g_ref, g_out, kept_sems.at[1]),
    ]
    for copy in kept:
        copy.start()

    by_last = ((1,), (1,))
    acts, slopes, dpres = [], [], []
    for group, ref in enumerate((in0, in1)):
        for copy in load_in[group]:
            copy.wait()
        value, slope = gelu_parts(dot(x_ref[...], ref[...]))
        acts.append(value.astype(BF16))
        slopes.append(slope)
        act_ref[group] = acts[group]
    for group, ref in enumerate((out0, out1)):
        for copy in load_out[group]:
            copy.wait()
        dpres.append((dot(g_ref[...], ref[...], by_last) * slopes[group]).astype(BF16))
        dpre_ref[group] = dpres[group]
    leave = []
    for pair in range(classes):
        for part in range(HALVES):
            at = (part * peers + 2 * pair) * width
            cols = slice(at, at + 2 * width)
            given = dot(acts[0], out0[:, cols]) + dot(acts[1], out1[:, cols])
            back = dot(dpres[0], in0[cols, :], by_last) + dot(dpres[1], in1[cols, :], by_last)
            for kind, block in ((0, given), (1, back)):
                block = block.astype(BF16)
                for at_group in range(sources // batch):
                    start = at_group * size + (2 * part + kind) * part_rows
                    here = slice(at_group * part_rows, (at_group + 1) * part_rows)
                    held_ref[start : start + part_rows, :] = block[here, :]
        for at_group in range(sources // batch):
            here = slice(at_group * size, (at_group + 1) * size)
            ret_ref[here, pair * 2 * width : (pair + 1) * 2 * width] = dot(
                spread, held_ref[here, :]
            ).astype(BF16)
        other = ret_low.at[pair] if pair < side else ret_high.at[pair - side]
        leave.append(
            pltpu.make_async_copy(
                ret_ref.at[:, columns(pair, False)], ret_own.at[pair], ret_sems.at[2 * pair]
            )
        )
        leave.append(
            pltpu.make_async_copy(
                ret_ref.at[:, columns(pair, True)], other, ret_sems.at[2 * pair + 1]
            )
        )
        leave[-2].start()
        leave[-1].start()
    over_rows = ((0,), (0,))
    model, hidden = in0.shape
    shares = []

    def share(block, start):
        for index in range(hidden // width):
            at = pl.ds(start(index), hidden)
            share_ref[at, :] = block[:, index * width : (index + 1) * width]
            shares.append(
                pltpu.make_async_copy(
                    share_ref.at[at, :], share_out.at[at, :], share_sems.at[len(shares)]
                )
            )
            shares[-1].start()

    for at in range(0, model, hidden):
        block = dot(x_ref[:, at : at + hidden], dpres[1], over_rows).astype(BF16)
        share(block, lambda index, at=at: index * model + at)
        block = dot(acts[1], g_ref[:, at : at + hidden], over_rows).astype(BF16)
        share(block, lambda index, at=at: hidden // width * model + (at // width + index) * hidden)
    for copy in leave + kept + shares:
        copy.wait()


def gradient_kernel(x_ref, g_ref, act_ref, dpre_ref, sent_ref, grad_in_ref, grad_out_ref):
    over_rows = ((0,), (0,))
    model = x_ref.shape[1]
    hidden, width = dpre_ref.shape[2], sent_ref.shape[1]
    for at in range(0, model, hidden):
        part = dot(x_ref[:, at : at + hidden], dpre_ref[0], over_rows)
        for index in range(hidden // width):
            start = index * model + at
            cols = slice(index * width, (index + 1) * width)
            grad_in_ref[0, at : at + hidden, cols] = (
                part[:, cols] + sent_ref[start : start + hidden, :].astype(F32)
            ).astype(BF16)
        part = dot(act_ref[0], g_ref[:, at : at + hidden], over_rows)
        for index in range(hidden // width):
            start = hidden // width * model + (at // width + index) * hidden
            cols = slice(index * width, (index + 1) * width)
            grad_out_ref[0, :, at + index * width : at + (index + 1) * width] = (
                part[:, cols] + sent_ref[start : start + hidden, :].astype(F32)
            ).astype(BF16)


def add_kernel(own_ref, low_ref, high_ref, out_ref):
    side = low_ref.shape[0]
    for index in range(own_ref.shape[0]):
        ref = low_ref.at[index] if index < side else high_ref.at[index - side]
        out_ref[index] = (own_ref[index].astype(F32) + ref[...].astype(F32)).astype(BF16)


def combine_kernel(used, rows_ref, gates_ref, home_ref, mixed_ref, grad_ref):
    groups, all_rows, _ = home_ref.shape
    tok_rows = mixed_ref.shape[0]
    slot = iota((all_rows, tok_rows), 0)
    row0, row1 = rows_ref[0:1, :], rows_ref[1:2, :]
    diagonal = iota((tok_rows, tok_rows), 0) == iota((tok_rows, tok_rows), 1)

    def column(row):
        return jnp.sum(jnp.where(diagonal, row, 0.0), axis=1, keepdims=True)

    def picked(hit):
        chosen = mask(hit)
        return sum(dot(chosen, home_ref[group], ((0,), (0,))) for group in range(groups))

    mixed = column(gates_ref[0:1, :]) * picked(slot == row0) + column(
        gates_ref[1:2, :]
    ) * picked(slot == row1)
    mixed_ref[...] = mixed.astype(BF16)
    grad_ref[...] = picked((slot == row0 + used) | (slot == row1 + used)).astype(BF16)


def call(kernel, shapes, cost, places, limit, scratch, *args):
    ins, outs = places
    flops, moved = cost
    return pl.pallas_call(
        kernel,
        out_shape=shapes,
        in_specs=[pl.BlockSpec(memory_space=place) for place in ins],
        out_specs=tuple(pl.BlockSpec(memory_space=place) for place in outs),
        scratch_shapes=scratch,
        cost_estimate=pl.CostEstimate(flops=flops, bytes_accessed=moved, transcendentals=0),
        compiler_params=pltpu.CompilerParams(vmem_limit_bytes=limit * 1024 * 1024),
    )(*args)


def struct(*shape, dtype=BF16):
    return jax.ShapeDtypeStruct(shape, dtype)


def body(tokens, cotangent, gates, routes, w_in, w_out):
    experts = lax.axis_size("dp")
    cuts = lax.axis_size("cuts")
    peers = cuts // HALVES
    classes = peers // 2
    side = classes // 2
    tok_rows, width = tokens.shape
    chosen = routes.shape[1]
    cap = 3 * chosen * tok_rows // (2 * experts)
    used = cap // HALVES
    rows = experts * used
    all_rows = 4 * rows
    model = width * cuts
    near, far = pltpu.VMEM, pltpu.HBM
    dma = pltpu.SemaphoreType.DMA
    swap = [(c, (c + peers) % cuts) for c in range(cuts)]
    up = [(c, c // peers * peers + (c + 1) % peers) for c in range(cuts)]
    down = [(d, c) for c, d in up]
    spread = [
        [d * cuts + h * peers + y for y in range(odd, peers, 2) for d in range(experts) for h in range(HALVES)]
        for odd in range(2)
    ]

    def to_partner(value):
        return lax.ppermute(value, "cuts", swap)

    def over_spread(value):
        pieces = value.reshape(classes * all_rows // FOUR, FOUR, width)
        pieces = lax.all_to_all(pieces, ("dp", "cuts"), 0, 0, tiled=True, axis_index_groups=spread)
        return pieces.reshape(classes, all_rows, width)

    in_own, out_own = w_in[0], w_out[0]
    hidden = in_own.shape[1]
    blocks = hidden // width + cuts
    early_rows, late_rows = (part[1] for part in split_blocks(hidden, model, width))
    routes_t, gates_t = routes.T, gates.T
    odd = (lax.axis_index("cuts") % 2).astype(jnp.int32).reshape(1)

    sent, places, early, late = call(
        functools.partial(place_kernel, experts, cap),
        (
            struct(classes, all_rows, width),
            struct(chosen, tok_rows, dtype=jnp.int32),
            struct(early_rows, width),
            struct(late_rows, width),
        ),
        (4 * all_rows * tok_rows * width, 4 * classes * all_rows * width),
        ([far] * 6, [far, near, far, far]),
        56,
        [
            pltpu.VMEM((chosen, tok_rows), jnp.int32),
            pltpu.VMEM((chosen, tok_rows), F32),
            pltpu.VMEM((tok_rows, width), BF16),
            pltpu.VMEM((tok_rows, width), BF16),
            pltpu.VMEM((all_rows, width), BF16),
            pltpu.VMEM((model, hidden), BF16),
            pltpu.VMEM((hidden, model), BF16),
            dma((4,)),
            dma((classes,)),
            dma((2,)),
            dma((blocks,)),
        ],
        routes_t,
        gates_t,
        tokens,
        cotangent,
        in_own,
        out_own,
    )
    early = to_partner(early)
    recv = over_spread(sent)
    recv, early, late = lax.optimization_barrier((recv, early, late))
    low = lax.ppermute(recv[:side], "cuts", up)
    high = lax.ppermute(recv[side:], "cuts", down)
    late = to_partner(late)
    ret_own, ret_low, ret_high, held_x, held_g, active, dpre, sent_grads = call(
        functools.partial(expert_kernel, used),
        (
            struct(classes, all_rows, width),
            struct(side, all_rows, width),
            struct(classes - side, all_rows, width),
            struct(rows, model),
            struct(rows, model),
            struct(2, rows, hidden),
            struct(2, rows, hidden),
            struct(early_rows + late_rows, width),
        ),
        (16 * rows * model * hidden, 12 * rows * model + 8 * model * hidden),
        ([pltpu.SMEM] + [far] * 7, [far] * 5 + [near] * 2 + [far]),
        60,
        [
            pltpu.VMEM((all_rows, peers * width), BF16),
            pltpu.VMEM((rows, model), BF16),
            pltpu.VMEM((rows, model), BF16),
            pltpu.VMEM((model, hidden), BF16),
            pltpu.VMEM((model, hidden), BF16),
            pltpu.VMEM((hidden, model), BF16),
            pltpu.VMEM((hidden, model), BF16),
            pltpu.VMEM((all_rows, 2 * width), BF16),
            pltpu.VMEM((all_rows, peers * width), BF16),
            pltpu.VMEM((early_rows + late_rows, width), BF16),
            dma((peers,)),
            dma((2 + blocks,)),
            dma((peers,)),
            dma((2,)),
            dma((2 * model // hidden * (hidden // width),)),
        ],
        odd,
        recv,
        low,
        high,
        in_own,
        out_own,
        early,
        late,
    )
    from_low = lax.ppermute(ret_low, "cuts", up)
    from_high = lax.ppermute(ret_high, "cuts", down)
    sent_grads = to_partner(sent_grads)
    summed = call(
        add_kernel,
        (struct(classes, all_rows, width),),
        (classes * all_rows * width, 6 * classes * all_rows * width),
        ([near] * 3, [near]),
        16,
        [],
        ret_own,
        from_low,
        from_high,
    )[0]
    home = over_spread(summed)
    grad_in, grad_out = call(
        gradient_kernel,
        (struct(1, model, hidden), struct(1, hidden, model)),
        (8 * rows * model * hidden, 16 * model * hidden),
        ([near] * 5, [near] * 2),
        32,
        [],
        held_x,
        held_g,
        active,
        dpre,
        sent_grads,
    )
    mixed, token_grad = call(
        functools.partial(combine_kernel, used),
        (struct(tok_rows, width), struct(tok_rows, width)),
        (6 * classes * all_rows * tok_rows * width, 2 * classes * all_rows * width),
        ([near] * 3, [near] * 2),
        16,
        [],
        places,
        gates_t,
        home,
    )
    return (mixed, token_grad, grad_in, grad_out)


def solution(mesh):
    in_specs = (
        P("dp", "cuts"),
        P("dp", "cuts"),
        P("dp", None),
        P("dp", None),
        P("dp", None, "cuts"),
        P("dp", "cuts", None),
    )
    out_specs = (P("dp", "cuts"), P("dp", "cuts"), P("dp", None, "cuts"), P("dp", "cuts", None))
    return jax.shard_map(body, mesh=mesh, in_specs=in_specs, out_specs=out_specs, check_vma=False)
```

```python
import functools
import math

import jax
import jax.numpy as jnp
from jax import lax
from jax.experimental import pallas as pl
from jax.experimental.pallas import tpu as pltpu
from jax.sharding import PartitionSpec as P

BF16 = jnp.bfloat16
F32 = jnp.float32
HALVES = 2
EARLY = (1, 2)
GROUP = 8
FOUR = 4


def gelu_parts(pre):
    coef = math.sqrt(2.0 / math.pi)
    inner = coef * (pre + 0.044715 * pre * pre * pre)
    tangent = jnp.tanh(inner)
    value = 0.5 * pre * (1.0 + tangent)
    slope = 0.5 * (1.0 + tangent) + 0.5 * pre * (1.0 - tangent * tangent) * coef * (
        1.0 + 3.0 * 0.044715 * pre * pre
    )
    return (value, slope)


def dot(left, right, dims=((1,), (0,))):
    return lax.dot_general(left, right, (dims, ((), ())), preferred_element_type=F32)


def iota(shape, axis):
    return lax.broadcasted_iota(jnp.int32, shape, axis)


def mask(hit):
    return jnp.where(hit, 1.0, 0.0).astype(BF16)


def weight_blocks(hidden, model, width):
    blocks = [(0, at, model) for at in range(0, hidden, width)]
    return blocks + [(1, at, hidden) for at in range(0, model, width)]


def split_blocks(hidden, model, width):
    blocks = weight_blocks(hidden, model, width)
    count = hidden // width + model // width * EARLY[0] // EARLY[1]
    parts = []
    for part in (blocks[:count], blocks[count:]):
        at, placed = 0, []
        for which, first, rows in part:
            placed.append((which, first, at, rows))
            at += rows
        parts.append((placed, at))
    return parts


def travelling(refs, start, rows):
    early, late = refs
    if start < early.shape[0]:
        return early.at[pl.ds(start, rows), :]
    return late.at[pl.ds(start - early.shape[0], rows), :]


def place_kernel(experts, cap, routes_in, gates_in, tok_in, cot_in, in_own, out_own, *refs):
    sent, rows_ref, early, late = refs[:4]
    scratch = refs[4:]
    routes_ref, gates_ref, tok_ref, cot_ref, held_ref, in_ref, out_ref, sems, sent_sems, load_sems, weight_sems = scratch
    tok_rows, width = tok_in.shape
    copies = [
        pltpu.make_async_copy(routes_in, routes_ref, sems.at[0]),
        pltpu.make_async_copy(gates_in, gates_ref, sems.at[1]),
        pltpu.make_async_copy(tok_in, tok_ref, sems.at[2]),
        pltpu.make_async_copy(cot_in, cot_ref, sems.at[3]),
    ]
    for copy in copies:
        copy.start()
    loads = [
        pltpu.make_async_copy(in_own, in_ref, load_sems.at[0]),
        pltpu.make_async_copy(out_own, out_ref, load_sems.at[1]),
    ]
    for copy in loads:
        copy.start()
    copies[0].wait()
    routes = routes_ref[...]
    first, second = routes[0:1, :], routes[1:2, :]
    names = iota((experts, tok_rows), 0)
    hit0, hit1 = names == first, names == second
    either = jnp.where(hit0 | hit1, 1.0, 0.0).astype(BF16)
    earlier = iota((tok_rows, tok_rows), 0) < iota((tok_rows, tok_rows), 1)
    count = dot(either, jnp.where(earlier, 1.0, 0.0).astype(BF16))
    used = cap // HALVES

    def row_of(hit, expert):
        position = jnp.sum(jnp.where(hit, count, 0.0), axis=0, keepdims=True).astype(jnp.int32)
        upper = jnp.where(position >= used, 1, 0)
        return (expert * HALVES + upper) * cap + position - upper * used

    row0, row1 = row_of(hit0, first), row_of(hit1, second)
    rows_ref[0:1, :] = row0
    rows_ref[1:2, :] = row1
    slot = iota((experts * HALVES * cap, tok_rows), 0)
    at_x = (slot == row0) | (slot == row1)
    at0, at1 = slot == row0 + used, slot == row1 + used
    copies[1].wait()
    gates = gates_ref[...]
    gate = jnp.sum(
        jnp.where(at0, gates[0:1, :], 0.0) + jnp.where(at1, gates[1:2, :], 0.0),
        axis=1,
        keepdims=True,
    )
    copies[2].wait()
    copies[3].wait()
    for copy in loads:
        copy.wait()
    weights = []
    for (placed, _), out in zip(split_blocks(*reversed(in_own.shape), width), (early, late)):
        for which, first, at, rows in placed:
            source = (in_ref, out_ref)[which].at[:, pl.ds(first, width)]
            weights.append(
                pltpu.make_async_copy(
                    source, out.at[pl.ds(at, rows), :], weight_sems.at[len(weights)]
                )
            )
            weights[-1].start()
    held_x = dot(mask(at_x), tok_ref[...])
    held_g = dot(mask(at0 | at1), cot_ref[...]) * gate
    held_ref[...] = (held_x + held_g).astype(BF16)
    copies = [
        pltpu.make_async_copy(held_ref, sent.at[index], sent_sems.at[index])
        for index in range(sent.shape[0])
    ]
    for copy in copies:
        copy.start()
    for copy in copies + weights:
        copy.wait()


def sorted_row(at, used, sources):
    group = 4 * used
    scale = -(-(1 << 16) // group)
    source = lax.shift_right_logical(at * scale, 16)
    inner = at - source * group
    block = lax.shift_right_logical(inner * -(-(1 << 16) // used), 16)
    return block * (sources * used) + source * used + inner - block * used


def expert_kernel(used, odd_ref, own, low, high, in_own, out_own, early, late, *rest):
    ret_own, ret_low, ret_high, x_out, g_out, act_ref, dpre_ref, *share_outs = rest[:9]
    recv_ref, x_ref, g_ref, in0, in1, out0, out1, held_ref, ret_ref, share_ref = rest[9:19]
    recv_sems, weight_sems, ret_sems, kept_sems, share_sems = rest[19:]
    classes, all_rows, width = own.shape
    peers = 2 * classes
    rows = all_rows // 4
    sources = rows // used
    side = classes // 2
    odd = odd_ref[0]

    def columns(index, other):
        place = 2 * index + (1 - odd if other else odd)
        return pl.ds(pl.multiple_of(place * width, width), width)

    moves = [(own, q, columns(q, False)) for q in range(classes)]
    moves += [(low, q, columns(q, True)) for q in range(side)]
    moves += [(high, q, columns(q + side, True)) for q in range(side)]
    arrive = [
        pltpu.make_async_copy(ref.at[q], recv_ref.at[:, cols], recv_sems.at[index])
        for index, (ref, q, cols) in enumerate(moves)
    ]
    load_in = [[pltpu.make_async_copy(in_own, in0, weight_sems.at[0])], []]
    load_out = [[pltpu.make_async_copy(out_own, out0, weight_sems.at[1])], []]
    for (placed, _), source in zip(split_blocks(*reversed(in0.shape), width), (early, late)):
        for which, first, at, size in placed:
            target = (in1, out1)[which].at[:, pl.ds(first, width)]
            index = 2 + len(load_in[1]) + len(load_out[1])
            (load_in, load_out)[which][1].append(
                pltpu.make_async_copy(
                    source.at[pl.ds(at, size), :], target, weight_sems.at[index]
                )
            )
    for copy in arrive + load_in[0] + load_in[1]:
        copy.start()
    batch = GROUP if sources % GROUP == 0 else sources
    size = 4 * used * batch
    part_rows = used * batch
    pick = mask(iota((size, size), 0) == sorted_row(iota((1, size), 1), used, batch))
    spread = mask(iota((size, size), 1) == sorted_row(iota((size, 1), 0), used, batch))
    for copy in arrive:
        copy.wait()
    for copy in load_out[0] + load_out[1]:
        copy.start()
    for pair in range(classes):
        cols = slice(pair * 2 * width, (pair + 1) * 2 * width)
        for at_group in range(sources // batch):
            block = dot(pick, recv_ref[at_group * size : (at_group + 1) * size, cols]).astype(BF16)
            here = slice(at_group * part_rows, (at_group + 1) * part_rows)
            for part in range(HALVES):
                at = (part * peers + 2 * pair) * width
                start = part * 2 * part_rows
                x_ref[here, at : at + 2 * width] = block[start : start + part_rows, :]
                start = start + part_rows
                g_ref[here, at : at + 2 * width] = block[start : start + part_rows, :]
    kept = [
        pltpu.make_async_copy(x_ref, x_out, kept_sems.at[0]),
        pltpu.make_async_copy(g_ref, g_out, kept_sems.at[1]),
    ]

    by_last = ((1,), (1,))
    acts, slopes, dpres = [], [], []
    for group, ref in enumerate((in0, in1)):
        for copy in load_in[group]:
            copy.wait()
        value, slope = gelu_parts(dot(x_ref[...], ref[...]))
        acts.append(value.astype(BF16))
        slopes.append(slope)
        act_ref[group] = acts[group]
    for group, ref in enumerate((out0, out1)):
        for copy in load_out[group]:
            copy.wait()
        dpres.append((dot(g_ref[...], ref[...], by_last) * slopes[group]).astype(BF16))
        dpre_ref[group] = dpres[group]
    for copy in kept:
        copy.start()
    leave = []
    for pair in range(classes):
        for part in range(HALVES):
            at = (part * peers + 2 * pair) * width
            cols = slice(at, at + 2 * width)
            given = dot(acts[0], out0[:, cols]) + dot(acts[1], out1[:, cols])
            back = dot(dpres[0], in0[cols, :], by_last) + dot(dpres[1], in1[cols, :], by_last)
            for kind, block in ((0, given), (1, back)):
                block = block.astype(BF16)
                for at_group in range(sources // batch):
                    start = at_group * size + (2 * part + kind) * part_rows
                    here = slice(at_group * part_rows, (at_group + 1) * part_rows)
                    held_ref[start : start + part_rows, :] = block[here, :]
        for at_group in range(sources // batch):
            here = slice(at_group * size, (at_group + 1) * size)
            ret_ref[here, pair * 2 * width : (pair + 1) * 2 * width] = dot(
                spread, held_ref[here, :]
            ).astype(BF16)
        other = ret_low.at[pair] if pair < side else ret_high.at[pair - side]
        leave.append(
            pltpu.make_async_copy(
                ret_ref.at[:, columns(pair, False)], ret_own.at[pair], ret_sems.at[2 * pair]
            )
        )
        leave.append(
            pltpu.make_async_copy(
                ret_ref.at[:, columns(pair, True)], other, ret_sems.at[2 * pair + 1]
            )
        )
        leave[-2].start()
        leave[-1].start()
    over_rows = ((0,), (0,))
    model, hidden = in0.shape
    shares = []

    def share(block, start):
        for index in range(hidden // width):
            at = pl.ds(start(index), hidden)
            share_ref[at, :] = block[:, index * width : (index + 1) * width]
            target = travelling(share_outs, start(index), hidden)
            shares.append(
                pltpu.make_async_copy(share_ref.at[at, :], target, share_sems.at[len(shares)])
            )
            shares[-1].start()

    for at in range(0, model, hidden):
        block = dot(x_ref[:, at : at + hidden], dpres[1], over_rows).astype(BF16)
        share(block, lambda index, at=at: index * model + at)
        block = dot(acts[1], g_ref[:, at : at + hidden], over_rows).astype(BF16)
        share(block, lambda index, at=at: hidden // width * model + (at // width + index) * hidden)
    for copy in leave + kept + shares:
        copy.wait()


def gradient_kernel(x_ref, g_ref, act_ref, dpre_ref, *refs):
    sent_refs, grad_in_ref, grad_out_ref = refs[:2], refs[2], refs[3]
    over_rows = ((0,), (0,))
    model = x_ref.shape[1]
    hidden, width = dpre_ref.shape[2], sent_refs[0].shape[1]
    for at in range(0, model, hidden):
        part = dot(x_ref[:, at : at + hidden], dpre_ref[0], over_rows)
        for index in range(hidden // width):
            start = index * model + at
            cols = slice(index * width, (index + 1) * width)
            grad_in_ref[0, at : at + hidden, cols] = (
                part[:, cols] + travelling(sent_refs, start, hidden)[...].astype(F32)
            ).astype(BF16)
        part = dot(act_ref[0], g_ref[:, at : at + hidden], over_rows)
        for index in range(hidden // width):
            start = hidden // width * model + (at // width + index) * hidden
            cols = slice(index * width, (index + 1) * width)
            grad_out_ref[0, :, at + index * width : at + (index + 1) * width] = (
                part[:, cols] + travelling(sent_refs, start, hidden)[...].astype(F32)
            ).astype(BF16)


def add_kernel(own_ref, low_ref, high_ref, out_ref):
    side = low_ref.shape[0]
    for index in range(own_ref.shape[0]):
        ref = low_ref.at[index] if index < side else high_ref.at[index - side]
        out_ref[index] = (own_ref[index].astype(F32) + ref[...].astype(F32)).astype(BF16)


def combine_kernel(used, rows_ref, gates_ref, home_ref, mixed_ref, grad_ref):
    groups, all_rows, _ = home_ref.shape
    tok_rows = mixed_ref.shape[0]
    slot = iota((all_rows, tok_rows), 0)
    row0, row1 = rows_ref[0:1, :], rows_ref[1:2, :]
    diagonal = iota((tok_rows, tok_rows), 0) == iota((tok_rows, tok_rows), 1)

    def column(row):
        return jnp.sum(jnp.where(diagonal, row, 0.0), axis=1, keepdims=True)

    def picked(hit):
        chosen = mask(hit)
        return sum(dot(chosen, home_ref[group], ((0,), (0,))) for group in range(groups))

    mixed = column(gates_ref[0:1, :]) * picked(slot == row0) + column(
        gates_ref[1:2, :]
    ) * picked(slot == row1)
    mixed_ref[...] = mixed.astype(BF16)
    grad_ref[...] = picked((slot == row0 + used) | (slot == row1 + used)).astype(BF16)


def call(kernel, shapes, cost, places, limit, scratch, *args):
    ins, outs = places
    flops, moved = cost
    return pl.pallas_call(
        kernel,
        out_shape=shapes,
        in_specs=[pl.BlockSpec(memory_space=place) for place in ins],
        out_specs=tuple(pl.BlockSpec(memory_space=place) for place in outs),
        scratch_shapes=scratch,
        cost_estimate=pl.CostEstimate(flops=flops, bytes_accessed=moved, transcendentals=0),
        compiler_params=pltpu.CompilerParams(vmem_limit_bytes=limit * 1024 * 1024),
    )(*args)


def struct(*shape, dtype=BF16):
    return jax.ShapeDtypeStruct(shape, dtype)


def body(tokens, cotangent, gates, routes, w_in, w_out):
    experts = lax.axis_size("dp")
    cuts = lax.axis_size("cuts")
    peers = cuts // HALVES
    classes = peers // 2
    side = classes // 2
    tok_rows, width = tokens.shape
    chosen = routes.shape[1]
    cap = 3 * chosen * tok_rows // (2 * experts)
    used = cap // HALVES
    rows = experts * used
    all_rows = 4 * rows
    model = width * cuts
    near, far = pltpu.VMEM, pltpu.HBM
    dma = pltpu.SemaphoreType.DMA
    swap = [(c, (c + peers) % cuts) for c in range(cuts)]
    up = [(c, c // peers * peers + (c + 1) % peers) for c in range(cuts)]
    down = [(d, c) for c, d in up]
    spread = [
        [d * cuts + h * peers + y for y in range(odd, peers, 2) for d in range(experts) for h in range(HALVES)]
        for odd in range(2)
    ]

    def to_partner(value):
        return lax.ppermute(value, "cuts", swap)

    def over_spread(value):
        pieces = value.reshape(classes * all_rows // FOUR, FOUR, width)
        pieces = lax.all_to_all(pieces, ("dp", "cuts"), 0, 0, tiled=True, axis_index_groups=spread)
        return pieces.reshape(classes, all_rows, width)

    in_own, out_own = w_in[0], w_out[0]
    hidden = in_own.shape[1]
    blocks = hidden // width + cuts
    early_rows, late_rows = (part[1] for part in split_blocks(hidden, model, width))
    routes_t, gates_t = routes.T, gates.T
    odd = (lax.axis_index("cuts") % 2).astype(jnp.int32).reshape(1)

    sent, places, early, late = call(
        functools.partial(place_kernel, experts, cap),
        (
            struct(classes, all_rows, width),
            struct(chosen, tok_rows, dtype=jnp.int32),
            struct(early_rows, width),
            struct(late_rows, width),
        ),
        (4 * all_rows * tok_rows * width, 4 * classes * all_rows * width),
        ([far] * 6, [far, near, far, far]),
        56,
        [
            pltpu.VMEM((chosen, tok_rows), jnp.int32),
            pltpu.VMEM((chosen, tok_rows), F32),
            pltpu.VMEM((tok_rows, width), BF16),
            pltpu.VMEM((tok_rows, width), BF16),
            pltpu.VMEM((all_rows, width), BF16),
            pltpu.VMEM((model, hidden), BF16),
            pltpu.VMEM((hidden, model), BF16),
            dma((4,)),
            dma((classes,)),
            dma((2,)),
            dma((blocks,)),
        ],
        routes_t,
        gates_t,
        tokens,
        cotangent,
        in_own,
        out_own,
    )
    early, late = to_partner(early), to_partner(late)
    recv = over_spread(sent)
    recv, early = lax.optimization_barrier((recv, early))
    low = lax.ppermute(recv[:side], "cuts", up)
    high = lax.ppermute(recv[side:], "cuts", down)
    ret_own, ret_low, ret_high, held_x, held_g, active, dpre, grads, late_grads = call(
        functools.partial(expert_kernel, used),
        (
            struct(classes, all_rows, width),
            struct(side, all_rows, width),
            struct(classes - side, all_rows, width),
            struct(rows, model),
            struct(rows, model),
            struct(2, rows, hidden),
            struct(2, rows, hidden),
            struct(early_rows, width),
            struct(late_rows, width),
        ),
        (16 * rows * model * hidden, 12 * rows * model + 8 * model * hidden),
        ([pltpu.SMEM] + [far] * 7, [far] * 5 + [near] * 2 + [far] * 2),
        60,
        [
            pltpu.VMEM((all_rows, peers * width), BF16),
            pltpu.VMEM((rows, model), BF16),
            pltpu.VMEM((rows, model), BF16),
            pltpu.VMEM((model, hidden), BF16),
            pltpu.VMEM((model, hidden), BF16),
            pltpu.VMEM((hidden, model), BF16),
            pltpu.VMEM((hidden, model), BF16),
            pltpu.VMEM((all_rows, 2 * width), BF16),
            pltpu.VMEM((all_rows, peers * width), BF16),
            pltpu.VMEM((early_rows + late_rows, width), BF16),
            dma((peers,)),
            dma((2 + blocks,)),
            dma((peers,)),
            dma((2,)),
            dma((2 * model // hidden * (hidden // width),)),
        ],
        odd,
        recv,
        low,
        high,
        in_own,
        out_own,
        early,
        late,
    )
    from_low = lax.ppermute(ret_low, "cuts", up)
    from_high = lax.ppermute(ret_high, "cuts", down)
    grads, late_grads = to_partner(grads), to_partner(late_grads)
    summed = call(
        add_kernel,
        (struct(classes, all_rows, width),),
        (classes * all_rows * width, 6 * classes * all_rows * width),
        ([near] * 3, [near]),
        16,
        [],
        ret_own,
        from_low,
        from_high,
    )[0]
    home = over_spread(summed)
    grad_in, grad_out = call(
        gradient_kernel,
        (struct(1, model, hidden), struct(1, hidden, model)),
        (8 * rows * model * hidden, 16 * model * hidden),
        ([near] * 6, [near] * 2),
        32,
        [],
        held_x,
        held_g,
        active,
        dpre,
        grads,
        late_grads,
    )
    mixed, token_grad = call(
        functools.partial(combine_kernel, used),
        (struct(tok_rows, width), struct(tok_rows, width)),
        (6 * classes * all_rows * tok_rows * width, 2 * classes * all_rows * width),
        ([near] * 3, [near] * 2),
        16,
        [],
        places,
        gates_t,
        home,
    )
    return (mixed, token_grad, grad_in, grad_out)


def solution(mesh):
    in_specs = (
        P("dp", "cuts"),
        P("dp", "cuts"),
        P("dp", None),
        P("dp", None),
        P("dp", None, "cuts"),
        P("dp", "cuts", None),
    )
    out_specs = (P("dp", "cuts"), P("dp", "cuts"), P("dp", None, "cuts"), P("dp", "cuts", None))
    return jax.shard_map(body, mesh=mesh, in_specs=in_specs, out_specs=out_specs, check_vma=False)
```

```python
import functools
import math

import jax
import jax.numpy as jnp
from jax import lax
from jax.experimental import pallas as pl
from jax.experimental.pallas import tpu as pltpu
from jax.sharding import PartitionSpec as P

BF16 = jnp.bfloat16
F32 = jnp.float32
HALVES = 2
EARLY = (1, 2)
GROUP = 8
FOUR = 4


def gelu_parts(pre):
    coef = math.sqrt(2.0 / math.pi)
    inner = coef * (pre + 0.044715 * pre * pre * pre)
    tangent = jnp.tanh(inner)
    value = 0.5 * pre * (1.0 + tangent)
    slope = 0.5 * (1.0 + tangent) + 0.5 * pre * (1.0 - tangent * tangent) * coef * (
        1.0 + 3.0 * 0.044715 * pre * pre
    )
    return (value, slope)


def dot(left, right, dims=((1,), (0,))):
    return lax.dot_general(left, right, (dims, ((), ())), preferred_element_type=F32)


def iota(shape, axis):
    return lax.broadcasted_iota(jnp.int32, shape, axis)


def mask(hit):
    return jnp.where(hit, 1.0, 0.0).astype(BF16)


def weight_blocks(hidden, model, width):
    blocks = [(0, at, model) for at in range(0, hidden, width)]
    return blocks + [(1, at, hidden) for at in range(0, model, width)]


def split_blocks(hidden, model, width):
    blocks = weight_blocks(hidden, model, width)
    count = hidden // width + model // width * EARLY[0] // EARLY[1]
    parts = []
    for part in (blocks[:count], blocks[count:]):
        at, placed = 0, []
        for which, first, rows in part:
            placed.append((which, first, at, rows))
            at += rows
        parts.append((placed, at))
    return parts


def place_kernel(experts, cap, routes_in, gates_in, tok_in, cot_in, in_own, out_own, *refs):
    sent, rows_ref, early, late = refs[:4]
    scratch = refs[4:]
    routes_ref, gates_ref, tok_ref, cot_ref, held_ref, in_ref, out_ref, sems, sent_sems, load_sems, weight_sems = scratch
    tok_rows, width = tok_in.shape
    copies = [
        pltpu.make_async_copy(routes_in, routes_ref, sems.at[0]),
        pltpu.make_async_copy(gates_in, gates_ref, sems.at[1]),
        pltpu.make_async_copy(tok_in, tok_ref, sems.at[2]),
        pltpu.make_async_copy(cot_in, cot_ref, sems.at[3]),
    ]
    for copy in copies:
        copy.start()
    loads = [
        pltpu.make_async_copy(in_own, in_ref, load_sems.at[0]),
        pltpu.make_async_copy(out_own, out_ref, load_sems.at[1]),
    ]
    for copy in loads:
        copy.start()
    copies[0].wait()
    routes = routes_ref[...]
    first, second = routes[0:1, :], routes[1:2, :]
    names = iota((experts, tok_rows), 0)
    hit0, hit1 = names == first, names == second
    either = jnp.where(hit0 | hit1, 1.0, 0.0).astype(BF16)
    earlier = iota((tok_rows, tok_rows), 0) < iota((tok_rows, tok_rows), 1)
    count = dot(either, jnp.where(earlier, 1.0, 0.0).astype(BF16))
    used = cap // HALVES

    def row_of(hit, expert):
        position = jnp.sum(jnp.where(hit, count, 0.0), axis=0, keepdims=True).astype(jnp.int32)
        upper = jnp.where(position >= used, 1, 0)
        return (expert * HALVES + upper) * cap + position - upper * used

    row0, row1 = row_of(hit0, first), row_of(hit1, second)
    rows_ref[0:1, :] = row0
    rows_ref[1:2, :] = row1
    slot = iota((experts * HALVES * cap, tok_rows), 0)
    at_x = (slot == row0) | (slot == row1)
    at0, at1 = slot == row0 + used, slot == row1 + used
    copies[1].wait()
    gates = gates_ref[...]
    gate = jnp.sum(
        jnp.where(at0, gates[0:1, :], 0.0) + jnp.where(at1, gates[1:2, :], 0.0),
        axis=1,
        keepdims=True,
    )
    copies[2].wait()
    copies[3].wait()
    for copy in loads:
        copy.wait()
    weights = []
    for (placed, _), out in zip(split_blocks(*reversed(in_own.shape), width), (early, late)):
        for which, first, at, rows in placed:
            source = (in_ref, out_ref)[which].at[:, pl.ds(first, width)]
            weights.append(
                pltpu.make_async_copy(
                    source, out.at[pl.ds(at, rows), :], weight_sems.at[len(weights)]
                )
            )
            weights[-1].start()
    held_x = dot(mask(at_x), tok_ref[...])
    held_g = dot(mask(at0 | at1), cot_ref[...]) * gate
    held_ref[...] = (held_x + held_g).astype(BF16)
    copies = [
        pltpu.make_async_copy(held_ref, sent.at[index], sent_sems.at[index])
        for index in range(sent.shape[0])
    ]
    for copy in copies:
        copy.start()
    for copy in copies + weights:
        copy.wait()


def sorted_row(at, used, sources):
    group = 4 * used
    scale = -(-(1 << 16) // group)
    source = lax.shift_right_logical(at * scale, 16)
    inner = at - source * group
    block = lax.shift_right_logical(inner * -(-(1 << 16) // used), 16)
    return block * (sources * used) + source * used + inner - block * used


def expert_kernel(used, odd_ref, own, low, high, in_own, out_own, early, late, *rest):
    ret_own, ret_low, ret_high, rows_out, own_ref, other_ref = rest[:6]
    recv_ref, x_ref, g_ref, in0, in1, out0, out1, held_ref, ret_ref = rest[6:15]
    recv_sems, weight_sems, ret_sems, kept_sems = rest[15:]
    classes, all_rows, width = own.shape
    peers = 2 * classes
    rows = all_rows // 4
    sources = rows // used
    side = classes // 2
    odd = odd_ref[0]

    def columns(index, other):
        place = 2 * index + (1 - odd if other else odd)
        return pl.ds(pl.multiple_of(place * width, width), width)

    moves = [(own, q, columns(q, False)) for q in range(classes)]
    moves += [(low, q, columns(q, True)) for q in range(side)]
    moves += [(high, q, columns(q + side, True)) for q in range(side)]
    arrive = [
        pltpu.make_async_copy(ref.at[q], recv_ref.at[:, cols], recv_sems.at[index])
        for index, (ref, q, cols) in enumerate(moves)
    ]
    load_in = [[pltpu.make_async_copy(in_own, in0, weight_sems.at[0])], []]
    load_out = [[pltpu.make_async_copy(out_own, out0, weight_sems.at[1])], []]
    for (placed, _), source in zip(split_blocks(*reversed(in0.shape), width), (early, late)):
        for which, first, at, size in placed:
            target = (in1, out1)[which].at[:, pl.ds(first, width)]
            index = 2 + len(load_in[1]) + len(load_out[1])
            (load_in, load_out)[which][1].append(
                pltpu.make_async_copy(
                    source.at[pl.ds(at, size), :], target, weight_sems.at[index]
                )
            )
    for copy in arrive + load_in[0] + load_in[1]:
        copy.start()
    batch = GROUP if sources % GROUP == 0 else sources
    size = 4 * used * batch
    part_rows = used * batch
    pick = mask(iota((size, size), 0) == sorted_row(iota((1, size), 1), used, batch))
    spread = mask(iota((size, size), 1) == sorted_row(iota((size, 1), 0), used, batch))
    for copy in arrive:
        copy.wait()
    for copy in load_out[0] + load_out[1]:
        copy.start()
    for pair in range(classes):
        cols = slice(pair * 2 * width, (pair + 1) * 2 * width)
        for at_group in range(sources // batch):
            block = dot(pick, recv_ref[at_group * size : (at_group + 1) * size, cols]).astype(BF16)
            here = slice(at_group * part_rows, (at_group + 1) * part_rows)
            for part in range(HALVES):
                at = (part * peers + 2 * pair) * width
                start = part * 2 * part_rows
                x_ref[here, at : at + 2 * width] = block[start : start + part_rows, :]
                start = start + part_rows
                g_ref[here, at : at + 2 * width] = block[start : start + part_rows, :]
    kept = [
        pltpu.make_async_copy(x_ref, rows_out.at[0], kept_sems.at[0]),
        pltpu.make_async_copy(g_ref, rows_out.at[1], kept_sems.at[1]),
    ]

    by_last = ((1,), (1,))
    acts, slopes, dpres = [], [], []
    for group, ref in enumerate((in0, in1)):
        for copy in load_in[group]:
            copy.wait()
        value, slope = gelu_parts(dot(x_ref[...], ref[...]))
        acts.append(value.astype(BF16))
        slopes.append(slope)
        (own_ref, other_ref)[group][0] = acts[group]
    for group, ref in enumerate((out0, out1)):
        for copy in load_out[group]:
            copy.wait()
        dpres.append((dot(g_ref[...], ref[...], by_last) * slopes[group]).astype(BF16))
        (own_ref, other_ref)[group][1] = dpres[group]
    for copy in kept:
        copy.start()
    leave = []
    for pair in range(classes):
        for part in range(HALVES):
            at = (part * peers + 2 * pair) * width
            cols = slice(at, at + 2 * width)
            given = dot(acts[0], out0[:, cols]) + dot(acts[1], out1[:, cols])
            back = dot(dpres[0], in0[cols, :], by_last) + dot(dpres[1], in1[cols, :], by_last)
            for kind, block in ((0, given), (1, back)):
                block = block.astype(BF16)
                for at_group in range(sources // batch):
                    start = at_group * size + (2 * part + kind) * part_rows
                    here = slice(at_group * part_rows, (at_group + 1) * part_rows)
                    held_ref[start : start + part_rows, :] = block[here, :]
        for at_group in range(sources // batch):
            here = slice(at_group * size, (at_group + 1) * size)
            ret_ref[here, pair * 2 * width : (pair + 1) * 2 * width] = dot(
                spread, held_ref[here, :]
            ).astype(BF16)
        other = ret_low.at[pair] if pair < side else ret_high.at[pair - side]
        leave.append(
            pltpu.make_async_copy(
                ret_ref.at[:, columns(pair, False)], ret_own.at[pair], ret_sems.at[2 * pair]
            )
        )
        leave.append(
            pltpu.make_async_copy(
                ret_ref.at[:, columns(pair, True)], other, ret_sems.at[2 * pair + 1]
            )
        )
        leave[-2].start()
        leave[-1].start()
    for copy in leave + kept:
        copy.wait()


def gradient_kernel(rows_ref, other_rows_ref, own_ref, other_ref, grad_in_ref, grad_out_ref):
    over_rows = ((0,), (0,))
    model, hidden = rows_ref.shape[2], own_ref.shape[2]
    for at in range(0, model, hidden):
        cols = slice(at, at + hidden)
        part = dot(rows_ref[0, :, cols], own_ref[1], over_rows)
        part = part + dot(other_rows_ref[0, :, cols], other_ref[1], over_rows)
        grad_in_ref[0, cols, :] = part.astype(BF16)
        part = dot(own_ref[0], rows_ref[1, :, cols], over_rows)
        part = part + dot(other_ref[0], other_rows_ref[1, :, cols], over_rows)
        grad_out_ref[0, :, cols] = part.astype(BF16)


def add_kernel(own_ref, low_ref, high_ref, out_ref):
    side = low_ref.shape[0]
    for index in range(own_ref.shape[0]):
        ref = low_ref.at[index] if index < side else high_ref.at[index - side]
        out_ref[index] = (own_ref[index].astype(F32) + ref[...].astype(F32)).astype(BF16)


def combine_kernel(used, rows_ref, gates_ref, home_ref, mixed_ref, grad_ref):
    groups, all_rows, _ = home_ref.shape
    tok_rows = mixed_ref.shape[0]
    slot = iota((all_rows, tok_rows), 0)
    row0, row1 = rows_ref[0:1, :], rows_ref[1:2, :]
    diagonal = iota((tok_rows, tok_rows), 0) == iota((tok_rows, tok_rows), 1)

    def column(row):
        return jnp.sum(jnp.where(diagonal, row, 0.0), axis=1, keepdims=True)

    def picked(hit):
        chosen = mask(hit)
        return sum(dot(chosen, home_ref[group], ((0,), (0,))) for group in range(groups))

    mixed = column(gates_ref[0:1, :]) * picked(slot == row0) + column(
        gates_ref[1:2, :]
    ) * picked(slot == row1)
    mixed_ref[...] = mixed.astype(BF16)
    grad_ref[...] = picked((slot == row0 + used) | (slot == row1 + used)).astype(BF16)


def call(kernel, shapes, cost, places, limit, scratch, *args):
    ins, outs = places
    flops, moved = cost
    return pl.pallas_call(
        kernel,
        out_shape=shapes,
        in_specs=[pl.BlockSpec(memory_space=place) for place in ins],
        out_specs=tuple(pl.BlockSpec(memory_space=place) for place in outs),
        scratch_shapes=scratch,
        cost_estimate=pl.CostEstimate(flops=flops, bytes_accessed=moved, transcendentals=0),
        compiler_params=pltpu.CompilerParams(vmem_limit_bytes=limit * 1024 * 1024),
    )(*args)


def struct(*shape, dtype=BF16):
    return jax.ShapeDtypeStruct(shape, dtype)


def body(tokens, cotangent, gates, routes, w_in, w_out):
    experts = lax.axis_size("dp")
    cuts = lax.axis_size("cuts")
    peers = cuts // HALVES
    classes = peers // 2
    side = classes // 2
    tok_rows, width = tokens.shape
    chosen = routes.shape[1]
    cap = 3 * chosen * tok_rows // (2 * experts)
    used = cap // HALVES
    rows = experts * used
    all_rows = 4 * rows
    model = width * cuts
    near, far = pltpu.VMEM, pltpu.HBM
    dma = pltpu.SemaphoreType.DMA
    swap = [(c, (c + peers) % cuts) for c in range(cuts)]
    up = [(c, c // peers * peers + (c + 1) % peers) for c in range(cuts)]
    down = [(d, c) for c, d in up]
    spread = [
        [d * cuts + h * peers + y for y in range(odd, peers, 2) for d in range(experts) for h in range(HALVES)]
        for odd in range(2)
    ]

    def to_partner(value):
        return lax.ppermute(value, "cuts", swap)

    def over_spread(value):
        pieces = value.reshape(classes * all_rows // FOUR, FOUR, width)
        pieces = lax.all_to_all(pieces, ("dp", "cuts"), 0, 0, tiled=True, axis_index_groups=spread)
        return pieces.reshape(classes, all_rows, width)

    in_own, out_own = w_in[0], w_out[0]
    hidden = in_own.shape[1]
    blocks = hidden // width + cuts
    early_rows, late_rows = (part[1] for part in split_blocks(hidden, model, width))
    routes_t, gates_t = routes.T, gates.T
    odd = (lax.axis_index("cuts") % 2).astype(jnp.int32).reshape(1)

    sent, places, early, late = call(
        functools.partial(place_kernel, experts, cap),
        (
            struct(classes, all_rows, width),
            struct(chosen, tok_rows, dtype=jnp.int32),
            struct(early_rows, width),
            struct(late_rows, width),
        ),
        (4 * all_rows * tok_rows * width, 4 * classes * all_rows * width),
        ([far] * 6, [far, near, far, far]),
        56,
        [
            pltpu.VMEM((chosen, tok_rows), jnp.int32),
            pltpu.VMEM((chosen, tok_rows), F32),
            pltpu.VMEM((tok_rows, width), BF16),
            pltpu.VMEM((tok_rows, width), BF16),
            pltpu.VMEM((all_rows, width), BF16),
            pltpu.VMEM((model, hidden), BF16),
            pltpu.VMEM((hidden, model), BF16),
            dma((4,)),
            dma((classes,)),
            dma((2,)),
            dma((blocks,)),
        ],
        routes_t,
        gates_t,
        tokens,
        cotangent,
        in_own,
        out_own,
    )
    early, late = to_partner(early), to_partner(late)
    recv = over_spread(sent)
    recv, early = lax.optimization_barrier((recv, early))
    low = lax.ppermute(recv[:side], "cuts", up)
    high = lax.ppermute(recv[side:], "cuts", down)
    ret_own, ret_low, ret_high, held_rows, own_units, other_units = call(
        functools.partial(expert_kernel, used),
        (
            struct(classes, all_rows, width),
            struct(side, all_rows, width),
            struct(classes - side, all_rows, width),
            struct(2, rows, model),
            struct(2, rows, hidden),
            struct(2, rows, hidden),
        ),
        (16 * rows * model * hidden, 12 * rows * model + 8 * model * hidden),
        ([pltpu.SMEM] + [far] * 7, [far] * 4 + [near] * 2),
        60,
        [
            pltpu.VMEM((all_rows, peers * width), BF16),
            pltpu.VMEM((rows, model), BF16),
            pltpu.VMEM((rows, model), BF16),
            pltpu.VMEM((model, hidden), BF16),
            pltpu.VMEM((model, hidden), BF16),
            pltpu.VMEM((hidden, model), BF16),
            pltpu.VMEM((hidden, model), BF16),
            pltpu.VMEM((all_rows, 2 * width), BF16),
            pltpu.VMEM((all_rows, peers * width), BF16),
            dma((peers,)),
            dma((2 + blocks,)),
            dma((peers,)),
            dma((2,)),
        ],
        odd,
        recv,
        low,
        high,
        in_own,
        out_own,
        early,
        late,
    )
    from_low = lax.ppermute(ret_low, "cuts", up)
    from_high = lax.ppermute(ret_high, "cuts", down)
    partner_rows, partner_units = to_partner(held_rows), to_partner(other_units)
    summed = call(
        add_kernel,
        (struct(classes, all_rows, width),),
        (classes * all_rows * width, 6 * classes * all_rows * width),
        ([near] * 3, [near]),
        16,
        [],
        ret_own,
        from_low,
        from_high,
    )[0]
    home = over_spread(summed)
    grad_in, grad_out = call(
        gradient_kernel,
        (struct(1, model, hidden), struct(1, hidden, model)),
        (16 * rows * model * hidden, 16 * model * hidden),
        ([near] * 4, [near] * 2),
        32,
        [],
        held_rows,
        partner_rows,
        own_units,
        partner_units,
    )
    mixed, token_grad = call(
        functools.partial(combine_kernel, used),
        (struct(tok_rows, width), struct(tok_rows, width)),
        (6 * classes * all_rows * tok_rows * width, 2 * classes * all_rows * width),
        ([near] * 3, [near] * 2),
        16,
        [],
        places,
        gates_t,
        home,
    )
    return (mixed, token_grad, grad_in, grad_out)


def solution(mesh):
    in_specs = (
        P("dp", "cuts"),
        P("dp", "cuts"),
        P("dp", None),
        P("dp", None),
        P("dp", None, "cuts"),
        P("dp", "cuts", None),
    )
    out_specs = (P("dp", "cuts"), P("dp", "cuts"), P("dp", None, "cuts"), P("dp", "cuts", None))
    return jax.shard_map(body, mesh=mesh, in_specs=in_specs, out_specs=out_specs, check_vma=False)
```

```python
import functools
import math

import jax
import jax.numpy as jnp
from jax import lax
from jax.experimental import pallas as pl
from jax.experimental.pallas import tpu as pltpu
from jax.sharding import PartitionSpec as P

BF16 = jnp.bfloat16
F32 = jnp.float32
HALVES = 2
EARLY = (1, 2)
PIECES = 4
GROUP = 8
FOUR = 4


def gelu_parts(pre):
    coef = math.sqrt(2.0 / math.pi)
    inner = coef * (pre + 0.044715 * pre * pre * pre)
    tangent = jnp.tanh(inner)
    value = 0.5 * pre * (1.0 + tangent)
    slope = 0.5 * (1.0 + tangent) + 0.5 * pre * (1.0 - tangent * tangent) * coef * (
        1.0 + 3.0 * 0.044715 * pre * pre
    )
    return (value, slope)


def dot(left, right, dims=((1,), (0,))):
    return lax.dot_general(left, right, (dims, ((), ())), preferred_element_type=F32)


def iota(shape, axis):
    return lax.broadcasted_iota(jnp.int32, shape, axis)


def mask(hit):
    return jnp.where(hit, 1.0, 0.0).astype(BF16)


def weight_blocks(hidden, model, width):
    blocks = [(0, at, model) for at in range(0, hidden, width)]
    return blocks + [(1, at, hidden) for at in range(0, model, width)]


def split_blocks(hidden, model, width):
    blocks = weight_blocks(hidden, model, width)
    count = hidden // width + model // width * EARLY[0] // EARLY[1]
    parts = []
    for part in (blocks[:count], blocks[count:]):
        at, placed = 0, []
        for which, first, rows in part:
            placed.append((which, first, at, rows))
            at += rows
        parts.append((placed, at))
    return parts


def in_pieces(source, target, sems, first):
    rows = source.shape[0] // PIECES
    return [
        pltpu.make_async_copy(
            source.at[pl.ds(index * rows, rows), :],
            target.at[pl.ds(index * rows, rows), :],
            sems.at[first + index],
        )
        for index in range(PIECES)
    ]


def place_kernel(experts, cap, routes_in, gates_in, tok_in, cot_in, in_own, out_own, *refs):
    sent, rows_ref, early, late = refs[:4]
    scratch = refs[4:]
    routes_ref, gates_ref, tok_ref, cot_ref, held_ref, in_ref, out_ref, sems, sent_sems, load_sems, weight_sems = scratch
    tok_rows, width = tok_in.shape
    copies = [
        pltpu.make_async_copy(routes_in, routes_ref, sems.at[0]),
        pltpu.make_async_copy(gates_in, gates_ref, sems.at[1]),
        pltpu.make_async_copy(tok_in, tok_ref, sems.at[2]),
        pltpu.make_async_copy(cot_in, cot_ref, sems.at[3]),
    ]
    for copy in copies:
        copy.start()
    loads = in_pieces(in_own, in_ref, load_sems, 0) + in_pieces(out_own, out_ref, load_sems, PIECES)
    for copy in loads:
        copy.start()
    copies[0].wait()
    routes = routes_ref[...]
    first, second = routes[0:1, :], routes[1:2, :]
    names = iota((experts, tok_rows), 0)
    hit0, hit1 = names == first, names == second
    either = jnp.where(hit0 | hit1, 1.0, 0.0).astype(BF16)
    earlier = iota((tok_rows, tok_rows), 0) < iota((tok_rows, tok_rows), 1)
    count = dot(either, jnp.where(earlier, 1.0, 0.0).astype(BF16))
    used = cap // HALVES

    def row_of(hit, expert):
        position = jnp.sum(jnp.where(hit, count, 0.0), axis=0, keepdims=True).astype(jnp.int32)
        upper = jnp.where(position >= used, 1, 0)
        return (expert * HALVES + upper) * cap + position - upper * used

    row0, row1 = row_of(hit0, first), row_of(hit1, second)
    rows_ref[0:1, :] = row0
    rows_ref[1:2, :] = row1
    slot = iota((experts * HALVES * cap, tok_rows), 0)
    at_x = (slot == row0) | (slot == row1)
    at0, at1 = slot == row0 + used, slot == row1 + used
    copies[1].wait()
    gates = gates_ref[...]
    gate = jnp.sum(
        jnp.where(at0, gates[0:1, :], 0.0) + jnp.where(at1, gates[1:2, :], 0.0),
        axis=1,
        keepdims=True,
    )
    copies[2].wait()
    copies[3].wait()
    for copy in loads:
        copy.wait()
    weights = []
    for (placed, _), out in zip(split_blocks(*reversed(in_own.shape), width), (early, late)):
        for which, first, at, rows in placed:
            source = (in_ref, out_ref)[which].at[:, pl.ds(first, width)]
            weights.append(
                pltpu.make_async_copy(
                    source, out.at[pl.ds(at, rows), :], weight_sems.at[len(weights)]
                )
            )
            weights[-1].start()
    held_x = dot(mask(at_x), tok_ref[...])
    held_g = dot(mask(at0 | at1), cot_ref[...]) * gate
    held_ref[...] = (held_x + held_g).astype(BF16)
    copies = [
        pltpu.make_async_copy(held_ref, sent.at[index], sent_sems.at[index])
        for index in range(sent.shape[0])
    ]
    for copy in copies:
        copy.start()
    for copy in copies + weights:
        copy.wait()


def sorted_row(at, used, sources):
    group = 4 * used
    scale = -(-(1 << 16) // group)
    source = lax.shift_right_logical(at * scale, 16)
    inner = at - source * group
    block = lax.shift_right_logical(inner * -(-(1 << 16) // used), 16)
    return block * (sources * used) + source * used + inner - block * used


def expert_kernel(used, odd_ref, own, low, high, in_own, out_own, early, late, *rest):
    ret_own, ret_low, ret_high, rows_out, own_ref = rest[:5]
    recv_ref, x_ref, g_ref, in0, in1, out0, out1, held_ref, ret_ref, other_ref = rest[5:15]
    recv_sems, weight_sems, ret_sems, kept_sems = rest[15:]
    classes, all_rows, width = own.shape
    peers = 2 * classes
    rows = all_rows // 4
    sources = rows // used
    side = classes // 2
    odd = odd_ref[0]

    def columns(index, other):
        place = 2 * index + (1 - odd if other else odd)
        return pl.ds(pl.multiple_of(place * width, width), width)

    moves = [(own, q, columns(q, False)) for q in range(classes)]
    moves += [(low, q, columns(q, True)) for q in range(side)]
    moves += [(high, q, columns(q + side, True)) for q in range(side)]
    arrive = [
        pltpu.make_async_copy(ref.at[q], recv_ref.at[:, cols], recv_sems.at[index])
        for index, (ref, q, cols) in enumerate(moves)
    ]
    load_in = [in_pieces(in_own, in0, weight_sems, 0), []]
    load_out = [in_pieces(out_own, out0, weight_sems, PIECES), []]
    for (placed, _), source in zip(split_blocks(*reversed(in0.shape), width), (early, late)):
        for which, first, at, size in placed:
            target = (in1, out1)[which].at[:, pl.ds(first, width)]
            index = 2 * PIECES + len(load_in[1]) + len(load_out[1])
            (load_in, load_out)[which][1].append(
                pltpu.make_async_copy(
                    source.at[pl.ds(at, size), :], target, weight_sems.at[index]
                )
            )
    for copy in arrive + load_in[0] + load_in[1]:
        copy.start()
    batch = GROUP if sources % GROUP == 0 else sources
    size = 4 * used * batch
    part_rows = used * batch
    pick = mask(iota((size, size), 0) == sorted_row(iota((1, size), 1), used, batch))
    spread = mask(iota((size, size), 1) == sorted_row(iota((size, 1), 0), used, batch))
    for copy in arrive:
        copy.wait()
    for copy in load_out[0] + load_out[1]:
        copy.start()
    for pair in range(classes):
        cols = slice(pair * 2 * width, (pair + 1) * 2 * width)
        for at_group in range(sources // batch):
            block = dot(pick, recv_ref[at_group * size : (at_group + 1) * size, cols]).astype(BF16)
            here = slice(at_group * part_rows, (at_group + 1) * part_rows)
            for part in range(HALVES):
                at = (part * peers + 2 * pair) * width
                start = part * 2 * part_rows
                x_ref[here, at : at + 2 * width] = block[start : start + part_rows, :]
                start = start + part_rows
                g_ref[here, at : at + 2 * width] = block[start : start + part_rows, :]
    model, hidden = in0.shape
    kept = [
        pltpu.make_async_copy(
            ref.at[:, pl.ds(at, model // PIECES)],
            rows_out.at[kind, :, pl.ds(at, model // PIECES)],
            kept_sems.at[kind, at * PIECES // model],
        )
        for kind, ref in enumerate((x_ref, g_ref))
        for at in range(0, model, model // PIECES)
    ]
    kept += [
        pltpu.make_async_copy(
            other_ref.at[kind], rows_out.at[kind, :, pl.ds(model, hidden)], kept_sems.at[kind, PIECES]
        )
        for kind in range(2)
    ]

    by_last = ((1,), (1,))
    acts, slopes, dpres = [], [], []
    for group, ref in enumerate((in0, in1)):
        for copy in load_in[group]:
            copy.wait()
        value, slope = gelu_parts(dot(x_ref[...], ref[...]))
        acts.append(value.astype(BF16))
        slopes.append(slope)
        (own_ref, other_ref)[group][0] = acts[group]
    for group, ref in enumerate((out0, out1)):
        for copy in load_out[group]:
            copy.wait()
        dpres.append((dot(g_ref[...], ref[...], by_last) * slopes[group]).astype(BF16))
        (own_ref, other_ref)[group][1] = dpres[group]
    for copy in kept:
        copy.start()
    leave = []
    for pair in range(classes):
        for part in range(HALVES):
            at = (part * peers + 2 * pair) * width
            cols = slice(at, at + 2 * width)
            given = dot(acts[0], out0[:, cols]) + dot(acts[1], out1[:, cols])
            back = dot(dpres[0], in0[cols, :], by_last) + dot(dpres[1], in1[cols, :], by_last)
            for kind, block in ((0, given), (1, back)):
                block = block.astype(BF16)
                for at_group in range(sources // batch):
                    start = at_group * size + (2 * part + kind) * part_rows
                    here = slice(at_group * part_rows, (at_group + 1) * part_rows)
                    held_ref[start : start + part_rows, :] = block[here, :]
        for at_group in range(sources // batch):
            here = slice(at_group * size, (at_group + 1) * size)
            ret_ref[here, pair * 2 * width : (pair + 1) * 2 * width] = dot(
                spread, held_ref[here, :]
            ).astype(BF16)
        other = ret_low.at[pair] if pair < side else ret_high.at[pair - side]
        leave.append(
            pltpu.make_async_copy(
                ret_ref.at[:, columns(pair, False)], ret_own.at[pair], ret_sems.at[2 * pair]
            )
        )
        leave.append(
            pltpu.make_async_copy(
                ret_ref.at[:, columns(pair, True)], other, ret_sems.at[2 * pair + 1]
            )
        )
        leave[-2].start()
        leave[-1].start()
    for copy in leave + kept:
        copy.wait()


def gradient_kernel(rows_ref, other_ref, own_ref, grad_in_ref, grad_out_ref):
    over_rows = ((0,), (0,))
    hidden = own_ref.shape[2]
    model = rows_ref.shape[2] - hidden
    units = slice(model, model + hidden)
    for at in range(0, model, hidden):
        cols = slice(at, at + hidden)
        part = dot(rows_ref[0, :, cols], own_ref[1], over_rows)
        part = part + dot(other_ref[0, :, cols], other_ref[1, :, units], over_rows)
        grad_in_ref[0, cols, :] = part.astype(BF16)
        part = dot(own_ref[0], rows_ref[1, :, cols], over_rows)
        part = part + dot(other_ref[0, :, units], other_ref[1, :, cols], over_rows)
        grad_out_ref[0, :, cols] = part.astype(BF16)


def add_kernel(own_ref, low_ref, high_ref, out_ref):
    side = low_ref.shape[0]
    for index in range(own_ref.shape[0]):
        ref = low_ref.at[index] if index < side else high_ref.at[index - side]
        out_ref[index] = (own_ref[index].astype(F32) + ref[...].astype(F32)).astype(BF16)


def combine_kernel(used, rows_ref, gates_ref, home_ref, mixed_ref, grad_ref):
    groups, all_rows, _ = home_ref.shape
    tok_rows = mixed_ref.shape[0]
    slot = iota((all_rows, tok_rows), 0)
    row0, row1 = rows_ref[0:1, :], rows_ref[1:2, :]
    diagonal = iota((tok_rows, tok_rows), 0) == iota((tok_rows, tok_rows), 1)

    def column(row):
        return jnp.sum(jnp.where(diagonal, row, 0.0), axis=1, keepdims=True)

    def picked(hit):
        chosen = mask(hit)
        return sum(dot(chosen, home_ref[group], ((0,), (0,))) for group in range(groups))

    mixed = column(gates_ref[0:1, :]) * picked(slot == row0) + column(
        gates_ref[1:2, :]
    ) * picked(slot == row1)
    mixed_ref[...] = mixed.astype(BF16)
    grad_ref[...] = picked((slot == row0 + used) | (slot == row1 + used)).astype(BF16)


def call(kernel, shapes, cost, places, limit, scratch, *args):
    ins, outs = places
    flops, moved = cost
    return pl.pallas_call(
        kernel,
        out_shape=shapes,
        in_specs=[pl.BlockSpec(memory_space=place) for place in ins],
        out_specs=tuple(pl.BlockSpec(memory_space=place) for place in outs),
        scratch_shapes=scratch,
        cost_estimate=pl.CostEstimate(flops=flops, bytes_accessed=moved, transcendentals=0),
        compiler_params=pltpu.CompilerParams(vmem_limit_bytes=limit * 1024 * 1024),
    )(*args)


def struct(*shape, dtype=BF16):
    return jax.ShapeDtypeStruct(shape, dtype)


def body(tokens, cotangent, gates, routes, w_in, w_out):
    experts = lax.axis_size("dp")
    cuts = lax.axis_size("cuts")
    peers = cuts // HALVES
    classes = peers // 2
    side = classes // 2
    tok_rows, width = tokens.shape
    chosen = routes.shape[1]
    cap = 3 * chosen * tok_rows // (2 * experts)
    used = cap // HALVES
    rows = experts * used
    all_rows = 4 * rows
    model = width * cuts
    near, far = pltpu.VMEM, pltpu.HBM
    dma = pltpu.SemaphoreType.DMA
    swap = [(c, (c + peers) % cuts) for c in range(cuts)]
    up = [(c, c // peers * peers + (c + 1) % peers) for c in range(cuts)]
    down = [(d, c) for c, d in up]
    spread = [
        [d * cuts + h * peers + y for y in range(odd, peers, 2) for d in range(experts) for h in range(HALVES)]
        for odd in range(2)
    ]

    def to_partner(value):
        return lax.ppermute(value, "cuts", swap)

    def over_spread(value):
        pieces = value.reshape(classes * all_rows // FOUR, FOUR, width)
        pieces = lax.all_to_all(pieces, ("dp", "cuts"), 0, 0, tiled=True, axis_index_groups=spread)
        return pieces.reshape(classes, all_rows, width)

    in_own, out_own = w_in[0], w_out[0]
    hidden = in_own.shape[1]
    blocks = hidden // width + cuts
    early_rows, late_rows = (part[1] for part in split_blocks(hidden, model, width))
    routes_t, gates_t = routes.T, gates.T
    odd = (lax.axis_index("cuts") % 2).astype(jnp.int32).reshape(1)

    sent, places, early, late = call(
        functools.partial(place_kernel, experts, cap),
        (
            struct(classes, all_rows, width),
            struct(chosen, tok_rows, dtype=jnp.int32),
            struct(early_rows, width),
            struct(late_rows, width),
        ),
        (4 * all_rows * tok_rows * width, 4 * classes * all_rows * width),
        ([far] * 6, [far, near, far, far]),
        56,
        [
            pltpu.VMEM((chosen, tok_rows), jnp.int32),
            pltpu.VMEM((chosen, tok_rows), F32),
            pltpu.VMEM((tok_rows, width), BF16),
            pltpu.VMEM((tok_rows, width), BF16),
            pltpu.VMEM((all_rows, width), BF16),
            pltpu.VMEM((model, hidden), BF16),
            pltpu.VMEM((hidden, model), BF16),
            dma((4,)),
            dma((classes,)),
            dma((2 * PIECES,)),
            dma((blocks,)),
        ],
        routes_t,
        gates_t,
        tokens,
        cotangent,
        in_own,
        out_own,
    )
    early, late = to_partner(early), to_partner(late)
    recv = over_spread(sent)
    recv, early = lax.optimization_barrier((recv, early))
    low = lax.ppermute(recv[:side], "cuts", up)
    high = lax.ppermute(recv[side:], "cuts", down)
    ret_own, ret_low, ret_high, held_rows, own_units = call(
        functools.partial(expert_kernel, used),
        (
            struct(classes, all_rows, width),
            struct(side, all_rows, width),
            struct(classes - side, all_rows, width),
            struct(2, rows, model + hidden),
            struct(2, rows, hidden),
        ),
        (16 * rows * model * hidden, 12 * rows * model + 8 * model * hidden),
        ([pltpu.SMEM] + [far] * 7, [far] * 4 + [near]),
        60,
        [
            pltpu.VMEM((all_rows, peers * width), BF16),
            pltpu.VMEM((rows, model), BF16),
            pltpu.VMEM((rows, model), BF16),
            pltpu.VMEM((model, hidden), BF16),
            pltpu.VMEM((model, hidden), BF16),
            pltpu.VMEM((hidden, model), BF16),
            pltpu.VMEM((hidden, model), BF16),
            pltpu.VMEM((all_rows, 2 * width), BF16),
            pltpu.VMEM((all_rows, peers * width), BF16),
            pltpu.VMEM((2, rows, hidden), BF16),
            dma((peers,)),
            dma((2 * PIECES + blocks,)),
            dma((peers,)),
            dma((2, PIECES + 1)),
        ],
        odd,
        recv,
        low,
        high,
        in_own,
        out_own,
        early,
        late,
    )
    from_low = lax.ppermute(ret_low, "cuts", up)
    from_high = lax.ppermute(ret_high, "cuts", down)
    partner_rows = to_partner(held_rows)
    summed = call(
        add_kernel,
        (struct(classes, all_rows, width),),
        (classes * all_rows * width, 6 * classes * all_rows * width),
        ([near] * 3, [near]),
        16,
        [],
        ret_own,
        from_low,
        from_high,
    )[0]
    home = over_spread(summed)
    grad_in, grad_out = call(
        gradient_kernel,
        (struct(1, model, hidden), struct(1, hidden, model)),
        (16 * rows * model * hidden, 16 * model * hidden),
        ([near] * 3, [near] * 2),
        32,
        [],
        held_rows,
        partner_rows,
        own_units,
    )
    mixed, token_grad = call(
        functools.partial(combine_kernel, used),
        (struct(tok_rows, width), struct(tok_rows, width)),
        (6 * classes * all_rows * tok_rows * width, 2 * classes * all_rows * width),
        ([near] * 3, [near] * 2),
        16,
        [],
        places,
        gates_t,
        home,
    )
    return (mixed, token_grad, grad_in, grad_out)


def solution(mesh):
    in_specs = (
        P("dp", "cuts"),
        P("dp", "cuts"),
        P("dp", None),
        P("dp", None),
        P("dp", None, "cuts"),
        P("dp", "cuts", None),
    )
    out_specs = (P("dp", "cuts"), P("dp", "cuts"), P("dp", None, "cuts"), P("dp", "cuts", None))
    return jax.shard_map(body, mesh=mesh, in_specs=in_specs, out_specs=out_specs, check_vma=False)
```

```python
import functools
import math

import jax
import jax.numpy as jnp
from jax import lax
from jax.experimental import pallas as pl
from jax.experimental.pallas import tpu as pltpu
from jax.sharding import PartitionSpec as P

BF16 = jnp.bfloat16
F32 = jnp.float32
HALVES = 2
EARLY = (1, 1)
PIECES = 4
GROUP = 8
FOUR = 4


def gelu_parts(pre):
    coef = math.sqrt(2.0 / math.pi)
    inner = coef * (pre + 0.044715 * pre * pre * pre)
    tangent = jnp.tanh(inner)
    value = 0.5 * pre * (1.0 + tangent)
    slope = 0.5 * (1.0 + tangent) + 0.5 * pre * (1.0 - tangent * tangent) * coef * (
        1.0 + 3.0 * 0.044715 * pre * pre
    )
    return (value, slope)


def dot(left, right, dims=((1,), (0,))):
    return lax.dot_general(left, right, (dims, ((), ())), preferred_element_type=F32)


def iota(shape, axis):
    return lax.broadcasted_iota(jnp.int32, shape, axis)


def mask(hit):
    return jnp.where(hit, 1.0, 0.0).astype(BF16)


def weight_blocks(hidden, model, width):
    blocks = [(0, at, model) for at in range(0, hidden, width)]
    return blocks + [(1, at, hidden) for at in range(0, model, width)]


def split_blocks(hidden, model, width):
    blocks = weight_blocks(hidden, model, width)
    ins, outs = blocks[: hidden // width], blocks[hidden // width :]
    parts = []
    for part in (ins[: EARLY[0]] + outs[: EARLY[1]], ins[EARLY[0] :] + outs[EARLY[1] :]):
        at, placed = 0, []
        for which, first, rows in part:
            placed.append((which, first, at, rows))
            at += rows
        parts.append((placed, at))
    return parts


def in_pieces(source, target, sems, first):
    rows = source.shape[0] // PIECES
    return [
        pltpu.make_async_copy(
            source.at[pl.ds(index * rows, rows), :],
            target.at[pl.ds(index * rows, rows), :],
            sems.at[first + index],
        )
        for index in range(PIECES)
    ]


def place_kernel(experts, cap, routes_in, gates_in, tok_in, cot_in, in_own, out_own, *refs):
    sent, rows_ref, early, late = refs[:4]
    scratch = refs[4:]
    routes_ref, gates_ref, tok_ref, cot_ref, held_ref, in_ref, out_ref, sems, sent_sems, load_sems, weight_sems = scratch
    tok_rows, width = tok_in.shape
    copies = [
        pltpu.make_async_copy(routes_in, routes_ref, sems.at[0]),
        pltpu.make_async_copy(gates_in, gates_ref, sems.at[1]),
        pltpu.make_async_copy(tok_in, tok_ref, sems.at[2]),
        pltpu.make_async_copy(cot_in, cot_ref, sems.at[3]),
    ]
    for copy in copies:
        copy.start()
    loads = in_pieces(in_own, in_ref, load_sems, 0) + in_pieces(out_own, out_ref, load_sems, PIECES)
    for copy in loads:
        copy.start()
    copies[0].wait()
    routes = routes_ref[...]
    first, second = routes[0:1, :], routes[1:2, :]
    names = iota((experts, tok_rows), 0)
    hit0, hit1 = names == first, names == second
    either = jnp.where(hit0 | hit1, 1.0, 0.0).astype(BF16)
    earlier = iota((tok_rows, tok_rows), 0) < iota((tok_rows, tok_rows), 1)
    count = dot(either, jnp.where(earlier, 1.0, 0.0).astype(BF16))
    used = cap // HALVES

    def row_of(hit, expert):
        position = jnp.sum(jnp.where(hit, count, 0.0), axis=0, keepdims=True).astype(jnp.int32)
        upper = jnp.where(position >= used, 1, 0)
        return (expert * HALVES + upper) * cap + position - upper * used

    row0, row1 = row_of(hit0, first), row_of(hit1, second)
    rows_ref[0:1, :] = row0
    rows_ref[1:2, :] = row1
    slot = iota((experts * HALVES * cap, tok_rows), 0)
    at_x = (slot == row0) | (slot == row1)
    at0, at1 = slot == row0 + used, slot == row1 + used
    copies[1].wait()
    gates = gates_ref[...]
    gate = jnp.sum(
        jnp.where(at0, gates[0:1, :], 0.0) + jnp.where(at1, gates[1:2, :], 0.0),
        axis=1,
        keepdims=True,
    )
    copies[2].wait()
    copies[3].wait()
    for copy in loads:
        copy.wait()
    weights = []
    for (placed, _), out in zip(split_blocks(*reversed(in_own.shape), width), (early, late)):
        for which, first, at, rows in placed:
            source = (in_ref, out_ref)[which].at[:, pl.ds(first, width)]
            weights.append(
                pltpu.make_async_copy(
                    source, out.at[pl.ds(at, rows), :], weight_sems.at[len(weights)]
                )
            )
            weights[-1].start()
    held_x = dot(mask(at_x), tok_ref[...])
    held_g = dot(mask(at0 | at1), cot_ref[...]) * gate
    held_ref[...] = (held_x + held_g).astype(BF16)
    copies = [
        pltpu.make_async_copy(held_ref, sent.at[index], sent_sems.at[index])
        for index in range(sent.shape[0])
    ]
    for copy in copies:
        copy.start()
    for copy in copies + weights:
        copy.wait()


def sorted_row(at, used, sources):
    group = 4 * used
    scale = -(-(1 << 16) // group)
    source = lax.shift_right_logical(at * scale, 16)
    inner = at - source * group
    block = lax.shift_right_logical(inner * -(-(1 << 16) // used), 16)
    return block * (sources * used) + source * used + inner - block * used


def expert_kernel(used, odd_ref, own, low, high, in_own, out_own, in_other, early, late, *rest):
    ret_own, ret_low, ret_high, x_out, g_out, own_ref = rest[:6]
    recv_ref, x_ref, g_ref, in0, in1, out0, out1, held_ref, ret_ref, other_ref = rest[6:16]
    recv_sems, weight_sems, ret_sems, kept_sems = rest[16:]
    classes, all_rows, width = own.shape
    peers = 2 * classes
    rows = all_rows // 4
    sources = rows // used
    side = classes // 2
    odd = odd_ref[0]

    def columns(index, other):
        place = 2 * index + (1 - odd if other else odd)
        return pl.ds(pl.multiple_of(place * width, width), width)

    moves = [(own, q, columns(q, False)) for q in range(classes)]
    moves += [(low, q, columns(q, True)) for q in range(side)]
    moves += [(high, q, columns(q + side, True)) for q in range(side)]
    arrive = [
        pltpu.make_async_copy(ref.at[q], recv_ref.at[:, cols], recv_sems.at[index])
        for index, (ref, q, cols) in enumerate(moves)
    ]
    load_in = [in_pieces(in_own, in0, weight_sems, 0), in_pieces(in_other, in1, weight_sems, PIECES)]
    load_out = [in_pieces(out_own, out0, weight_sems, 2 * PIECES), []]
    for (placed, _), source in zip(split_blocks(*reversed(in0.shape), width), (early, late)):
        for which, first, at, size in placed:
            if which == 1:
                load_out[1].append(
                    pltpu.make_async_copy(
                        source.at[pl.ds(at, size), :],
                        out1.at[:, pl.ds(first, width)],
                        weight_sems.at[3 * PIECES + len(load_out[1])],
                    )
                )
    for copy in arrive + load_in[0] + load_in[1]:
        copy.start()
    batch = GROUP if sources % GROUP == 0 else sources
    size = 4 * used * batch
    part_rows = used * batch
    pick = mask(iota((size, size), 0) == sorted_row(iota((1, size), 1), used, batch))
    spread = mask(iota((size, size), 1) == sorted_row(iota((size, 1), 0), used, batch))
    for copy in arrive:
        copy.wait()
    for copy in load_out[0] + load_out[1]:
        copy.start()
    for pair in range(classes):
        cols = slice(pair * 2 * width, (pair + 1) * 2 * width)
        for at_group in range(sources // batch):
            block = dot(pick, recv_ref[at_group * size : (at_group + 1) * size, cols]).astype(BF16)
            here = slice(at_group * part_rows, (at_group + 1) * part_rows)
            for part in range(HALVES):
                at = (part * peers + 2 * pair) * width
                start = part * 2 * part_rows
                x_ref[here, at : at + 2 * width] = block[start : start + part_rows, :]
                start = start + part_rows
                g_ref[here, at : at + 2 * width] = block[start : start + part_rows, :]
    model, hidden = in0.shape
    kept = [
        pltpu.make_async_copy(
            ref.at[:, pl.ds(at, model // PIECES)],
            out.at[:, pl.ds(at, model // PIECES)],
            kept_sems.at[kind, at * PIECES // model],
        )
        for kind, (ref, out) in enumerate(((x_ref, x_out), (g_ref, g_out)))
        for at in range(0, model, model // PIECES)
    ]
    kept += [
        pltpu.make_async_copy(
            other_ref.at[kind],
            g_out.at[:, pl.ds(model + kind * hidden, hidden)],
            kept_sems.at[kind, PIECES],
        )
        for kind in range(2)
    ]

    by_last = ((1,), (1,))
    acts, slopes, dpres = [], [], []
    for group, ref in enumerate((in0, in1)):
        for copy in load_in[group]:
            copy.wait()
        value, slope = gelu_parts(dot(x_ref[...], ref[...]))
        acts.append(value.astype(BF16))
        slopes.append(slope)
        (own_ref, other_ref)[group][0] = acts[group]
    for group, ref in enumerate((out0, out1)):
        for copy in load_out[group]:
            copy.wait()
        dpres.append((dot(g_ref[...], ref[...], by_last) * slopes[group]).astype(BF16))
        (own_ref, other_ref)[group][1] = dpres[group]
    for copy in kept:
        copy.start()
    leave = []
    for pair in range(classes):
        for part in range(HALVES):
            at = (part * peers + 2 * pair) * width
            cols = slice(at, at + 2 * width)
            given = dot(acts[0], out0[:, cols]) + dot(acts[1], out1[:, cols])
            back = dot(dpres[0], in0[cols, :], by_last) + dot(dpres[1], in1[cols, :], by_last)
            for kind, block in ((0, given), (1, back)):
                block = block.astype(BF16)
                for at_group in range(sources // batch):
                    start = at_group * size + (2 * part + kind) * part_rows
                    here = slice(at_group * part_rows, (at_group + 1) * part_rows)
                    held_ref[start : start + part_rows, :] = block[here, :]
        for at_group in range(sources // batch):
            here = slice(at_group * size, (at_group + 1) * size)
            ret_ref[here, pair * 2 * width : (pair + 1) * 2 * width] = dot(
                spread, held_ref[here, :]
            ).astype(BF16)
        other = ret_low.at[pair] if pair < side else ret_high.at[pair - side]
        leave.append(
            pltpu.make_async_copy(
                ret_ref.at[:, columns(pair, False)], ret_own.at[pair], ret_sems.at[2 * pair]
            )
        )
        leave.append(
            pltpu.make_async_copy(
                ret_ref.at[:, columns(pair, True)], other, ret_sems.at[2 * pair + 1]
            )
        )
        leave[-2].start()
        leave[-1].start()
    for copy in leave + kept:
        copy.wait()


def gradient_kernel(x_ref, g_ref, other_x_ref, other_g_ref, own_ref, grad_in_ref, grad_out_ref):
    over_rows = ((0,), (0,))
    model, hidden = x_ref.shape[1], own_ref.shape[2]
    act = other_g_ref[:, model : model + hidden]
    dpre = other_g_ref[:, model + hidden :]
    for at in range(0, model, hidden):
        cols = slice(at, at + hidden)
        part = dot(x_ref[:, cols], own_ref[1], over_rows)
        part = part + dot(other_x_ref[:, cols], dpre, over_rows)
        grad_in_ref[0, cols, :] = part.astype(BF16)
        part = dot(own_ref[0], g_ref[:, cols], over_rows)
        part = part + dot(act, other_g_ref[:, cols], over_rows)
        grad_out_ref[0, :, cols] = part.astype(BF16)


def add_kernel(own_ref, low_ref, high_ref, out_ref):
    side = low_ref.shape[0]
    for index in range(own_ref.shape[0]):
        ref = low_ref.at[index] if index < side else high_ref.at[index - side]
        out_ref[index] = (own_ref[index].astype(F32) + ref[...].astype(F32)).astype(BF16)


def combine_kernel(used, rows_ref, gates_ref, home_ref, mixed_ref, grad_ref):
    groups, all_rows, width = home_ref.shape
    tok_rows = mixed_ref.shape[0]
    slot = iota((all_rows, tok_rows), 0)
    row0, row1 = rows_ref[0:1, :], rows_ref[1:2, :]
    diagonal = iota((tok_rows, tok_rows), 0) == iota((tok_rows, tok_rows), 1)

    def column(row):
        return jnp.sum(jnp.where(diagonal, row, 0.0), axis=1, keepdims=True)

    total = home_ref[0].astype(F32)
    for group in range(1, groups):
        total = total + home_ref[group].astype(F32)
    high = total.astype(BF16)
    low = (total - high.astype(F32)).astype(BF16)
    hits = (slot == row0, slot == row1, (slot == row0 + used) | (slot == row1 + used))
    chosen = jnp.concatenate([mask(hit) for hit in hits], axis=1)
    picked = dot(chosen, jnp.concatenate([high, low], axis=1), ((0,), (0,)))
    picked = picked[:, :width] + picked[:, width:]
    mixed = (
        column(gates_ref[0:1, :]) * picked[:tok_rows]
        + column(gates_ref[1:2, :]) * picked[tok_rows : 2 * tok_rows]
    )
    mixed_ref[...] = mixed.astype(BF16)
    grad_ref[...] = picked[2 * tok_rows :].astype(BF16)


def call(kernel, shapes, cost, places, limit, scratch, *args):
    ins, outs = places
    flops, moved = cost
    return pl.pallas_call(
        kernel,
        out_shape=shapes,
        in_specs=[pl.BlockSpec(memory_space=place) for place in ins],
        out_specs=tuple(pl.BlockSpec(memory_space=place) for place in outs),
        scratch_shapes=scratch,
        cost_estimate=pl.CostEstimate(flops=flops, bytes_accessed=moved, transcendentals=0),
        compiler_params=pltpu.CompilerParams(vmem_limit_bytes=limit * 1024 * 1024),
    )(*args)


def struct(*shape, dtype=BF16):
    return jax.ShapeDtypeStruct(shape, dtype)


def body(tokens, cotangent, gates, routes, w_in, w_out):
    experts = lax.axis_size("dp")
    cuts = lax.axis_size("cuts")
    peers = cuts // HALVES
    classes = peers // 2
    side = classes // 2
    tok_rows, width = tokens.shape
    chosen = routes.shape[1]
    cap = 3 * chosen * tok_rows // (2 * experts)
    used = cap // HALVES
    rows = experts * used
    all_rows = 4 * rows
    model = width * cuts
    near, far = pltpu.VMEM, pltpu.HBM
    dma = pltpu.SemaphoreType.DMA
    swap = [(c, (c + peers) % cuts) for c in range(cuts)]
    up = [(c, c // peers * peers + (c + 1) % peers) for c in range(cuts)]
    down = [(d, c) for c, d in up]
    spread = [
        [d * cuts + h * peers + y for y in range(odd, peers, 2) for d in range(experts) for h in range(HALVES)]
        for odd in range(2)
    ]

    def to_partner(value):
        return lax.ppermute(value, "cuts", swap)

    def over_spread(value):
        pieces = value.reshape(classes * all_rows // FOUR, FOUR, width)
        pieces = lax.all_to_all(pieces, ("dp", "cuts"), 0, 0, tiled=True, axis_index_groups=spread)
        return pieces.reshape(classes, all_rows, width)

    in_own, out_own = w_in[0], w_out[0]
    hidden = in_own.shape[1]
    blocks = hidden // width + cuts
    early_rows, late_rows = (part[1] for part in split_blocks(hidden, model, width))
    routes_t, gates_t = routes.T, gates.T
    odd = (lax.axis_index("cuts") % 2).astype(jnp.int32).reshape(1)

    sent, places, early, late = call(
        functools.partial(place_kernel, experts, cap),
        (
            struct(classes, all_rows, width),
            struct(chosen, tok_rows, dtype=jnp.int32),
            struct(early_rows, width),
            struct(late_rows, width),
        ),
        (4 * all_rows * tok_rows * width, 4 * classes * all_rows * width),
        ([far] * 6, [far, near, far, far]),
        56,
        [
            pltpu.VMEM((chosen, tok_rows), jnp.int32),
            pltpu.VMEM((chosen, tok_rows), F32),
            pltpu.VMEM((tok_rows, width), BF16),
            pltpu.VMEM((tok_rows, width), BF16),
            pltpu.VMEM((all_rows, width), BF16),
            pltpu.VMEM((model, hidden), BF16),
            pltpu.VMEM((hidden, model), BF16),
            dma((4,)),
            dma((classes,)),
            dma((2 * PIECES,)),
            dma((blocks,)),
        ],
        routes_t,
        gates_t,
        tokens,
        cotangent,
        in_own,
        out_own,
    )
    early, late = lax.optimization_barrier((to_partner(early), late))
    late = to_partner(late)
    recv = over_spread(sent)
    low = lax.ppermute(recv[:side], "cuts", up)
    high = lax.ppermute(recv[side:], "cuts", down)
    early_in = early[: EARLY[0] * model].reshape(EARLY[0], model, width)
    late_in = late[: (hidden // width - EARLY[0]) * model].reshape(-1, model, width)
    in_other = jnp.concatenate([*early_in, *late_in], axis=1)
    ret_own, ret_low, ret_high, held_x, held_g, own_units = call(
        functools.partial(expert_kernel, used),
        (
            struct(classes, all_rows, width),
            struct(side, all_rows, width),
            struct(classes - side, all_rows, width),
            struct(rows, model),
            struct(rows, model + 2 * hidden),
            struct(2, rows, hidden),
        ),
        (16 * rows * model * hidden, 12 * rows * model + 8 * model * hidden),
        ([pltpu.SMEM] + [far] * 8, [far] * 5 + [near]),
        60,
        [
            pltpu.VMEM((all_rows, peers * width), BF16),
            pltpu.VMEM((rows, model), BF16),
            pltpu.VMEM((rows, model), BF16),
            pltpu.VMEM((model, hidden), BF16),
            pltpu.VMEM((model, hidden), BF16),
            pltpu.VMEM((hidden, model), BF16),
            pltpu.VMEM((hidden, model), BF16),
            pltpu.VMEM((all_rows, 2 * width), BF16),
            pltpu.VMEM((all_rows, peers * width), BF16),
            pltpu.VMEM((2, rows, hidden), BF16),
            dma((peers,)),
            dma((3 * PIECES + blocks,)),
            dma((peers,)),
            dma((2, PIECES + 1)),
        ],
        odd,
        recv,
        low,
        high,
        in_own,
        out_own,
        in_other,
        early,
        late,
    )
    from_low = lax.ppermute(ret_low, "cuts", up)
    from_high = lax.ppermute(ret_high, "cuts", down)
    partner_x, sent_g = lax.optimization_barrier((to_partner(held_x), held_g))
    partner_g = to_partner(sent_g)
    summed = call(
        add_kernel,
        (struct(classes, all_rows, width),),
        (classes * all_rows * width, 6 * classes * all_rows * width),
        ([near] * 3, [near]),
        16,
        [],
        ret_own,
        from_low,
        from_high,
    )[0]
    home = over_spread(summed)
    grad_in, grad_out = call(
        gradient_kernel,
        (struct(1, model, hidden), struct(1, hidden, model)),
        (16 * rows * model * hidden, 16 * model * hidden),
        ([near] * 5, [near] * 2),
        32,
        [],
        held_x,
        held_g,
        partner_x,
        partner_g,
        own_units,
    )
    mixed, token_grad = call(
        functools.partial(combine_kernel, used),
        (struct(tok_rows, width), struct(tok_rows, width)),
        (6 * classes * all_rows * tok_rows * width, 2 * classes * all_rows * width),
        ([near] * 3, [near] * 2),
        16,
        [],
        places,
        gates_t,
        home,
    )
    return (mixed, token_grad, grad_in, grad_out)


def solution(mesh):
    in_specs = (
        P("dp", "cuts"),
        P("dp", "cuts"),
        P("dp", None),
        P("dp", None),
        P("dp", None, "cuts"),
        P("dp", "cuts", None),
    )
    out_specs = (P("dp", "cuts"), P("dp", "cuts"), P("dp", None, "cuts"), P("dp", "cuts", None))
    return jax.shard_map(body, mesh=mesh, in_specs=in_specs, out_specs=out_specs, check_vma=False)
```

```python
import functools
import math

import jax
import jax.numpy as jnp
from jax import lax
from jax.experimental import pallas as pl
from jax.experimental.pallas import tpu as pltpu
from jax.sharding import PartitionSpec as P

BF16 = jnp.bfloat16
F32 = jnp.float32
HALVES = 2
EARLY = (1, 3)
PIECES = 4
GROUP = 8
FOUR = 4


def gelu_parts(pre):
    coef = math.sqrt(2.0 / math.pi)
    inner = coef * (pre + 0.044715 * pre * pre * pre)
    tangent = jnp.tanh(inner)
    value = 0.5 * pre * (1.0 + tangent)
    slope = 0.5 * (1.0 + tangent) + 0.5 * pre * (1.0 - tangent * tangent) * coef * (
        1.0 + 3.0 * 0.044715 * pre * pre
    )
    return (value, slope)


def dot(left, right, dims=((1,), (0,))):
    return lax.dot_general(left, right, (dims, ((), ())), preferred_element_type=F32)


def iota(shape, axis):
    return lax.broadcasted_iota(jnp.int32, shape, axis)


def mask(hit):
    return jnp.where(hit, 1.0, 0.0).astype(BF16)


def weight_blocks(hidden, model, width):
    blocks = [(0, at, model) for at in range(0, hidden, width)]
    return blocks + [(1, at, hidden) for at in range(0, model, width)]


def split_blocks(hidden, model, width):
    blocks = weight_blocks(hidden, model, width)
    ins, outs = blocks[: hidden // width], blocks[hidden // width :]
    parts = []
    for part in (ins[: EARLY[0]] + outs[: EARLY[1]], ins[EARLY[0] :] + outs[EARLY[1] :]):
        at, placed = 0, []
        for which, first, rows in part:
            placed.append((which, first, at, rows))
            at += rows
        parts.append((placed, at))
    return parts


def in_pieces(source, target, sems, first):
    rows = source.shape[0] // PIECES
    return [
        pltpu.make_async_copy(
            source.at[pl.ds(index * rows, rows), :],
            target.at[pl.ds(index * rows, rows), :],
            sems.at[first + index],
        )
        for index in range(PIECES)
    ]


def place_kernel(experts, cap, routes_in, gates_in, tok_in, cot_in, in_own, out_own, *refs):
    sent, rows_ref, early, late = refs[:4]
    scratch = refs[4:]
    routes_ref, gates_ref, tok_ref, cot_ref, held_ref, in_ref, out_ref, sems, sent_sems, load_sems, weight_sems = scratch
    tok_rows, width = tok_in.shape
    copies = [
        pltpu.make_async_copy(routes_in, routes_ref, sems.at[0]),
        pltpu.make_async_copy(gates_in, gates_ref, sems.at[1]),
        pltpu.make_async_copy(tok_in, tok_ref, sems.at[2]),
        pltpu.make_async_copy(cot_in, cot_ref, sems.at[3]),
    ]
    for copy in copies:
        copy.start()
    loads = in_pieces(in_own, in_ref, load_sems, 0) + in_pieces(out_own, out_ref, load_sems, PIECES)
    for copy in loads:
        copy.start()
    copies[0].wait()
    routes = routes_ref[...]
    first, second = routes[0:1, :], routes[1:2, :]
    names = iota((experts, tok_rows), 0)
    hit0, hit1 = names == first, names == second
    either = jnp.where(hit0 | hit1, 1.0, 0.0).astype(BF16)
    earlier = iota((tok_rows, tok_rows), 0) < iota((tok_rows, tok_rows), 1)
    count = dot(either, jnp.where(earlier, 1.0, 0.0).astype(BF16))
    used = cap // HALVES

    def row_of(hit, expert):
        position = jnp.sum(jnp.where(hit, count, 0.0), axis=0, keepdims=True).astype(jnp.int32)
        upper = jnp.where(position >= used, 1, 0)
        return (expert * HALVES + upper) * cap + position - upper * used

    row0, row1 = row_of(hit0, first), row_of(hit1, second)
    rows_ref[0:1, :] = row0
    rows_ref[1:2, :] = row1
    slot = iota((experts * HALVES * cap, tok_rows), 0)
    at_x = (slot == row0) | (slot == row1)
    at0, at1 = slot == row0 + used, slot == row1 + used
    copies[1].wait()
    gates = gates_ref[...]
    gate = jnp.sum(
        jnp.where(at0, gates[0:1, :], 0.0) + jnp.where(at1, gates[1:2, :], 0.0),
        axis=1,
        keepdims=True,
    )
    copies[2].wait()
    copies[3].wait()
    for copy in loads:
        copy.wait()
    weights = []
    for (placed, _), out in zip(split_blocks(*reversed(in_own.shape), width), (early, late)):
        for which, first, at, rows in placed:
            source = (in_ref, out_ref)[which].at[:, pl.ds(first, width)]
            weights.append(
                pltpu.make_async_copy(
                    source, out.at[pl.ds(at, rows), :], weight_sems.at[len(weights)]
                )
            )
            weights[-1].start()
    held_x = dot(mask(at_x), tok_ref[...])
    held_g = dot(mask(at0 | at1), cot_ref[...]) * gate
    held_ref[...] = (held_x + held_g).astype(BF16)
    copies = [
        pltpu.make_async_copy(held_ref, sent.at[index], sent_sems.at[index])
        for index in range(sent.shape[0])
    ]
    for copy in copies:
        copy.start()
    for copy in copies + weights:
        copy.wait()


def sorted_row(at, used, sources):
    group = 4 * used
    scale = -(-(1 << 16) // group)
    source = lax.shift_right_logical(at * scale, 16)
    inner = at - source * group
    block = lax.shift_right_logical(inner * -(-(1 << 16) // used), 16)
    return block * (sources * used) + source * used + inner - block * used


def expert_kernel(used, odd_ref, own, low, high, in_own, out_own, in_other, early, late, *rest):
    ret_own, ret_low, ret_high, rows_out, own_ref = rest[:5]
    recv_ref, x_ref, g_ref, in0, in1, out0, out1, held_ref, ret_ref, other_ref = rest[5:15]
    recv_sems, weight_sems, ret_sems, kept_sems = rest[15:]
    classes, all_rows, width = own.shape
    peers = 2 * classes
    rows = all_rows // 4
    sources = rows // used
    side = classes // 2
    odd = odd_ref[0]

    def columns(index, other):
        place = 2 * index + (1 - odd if other else odd)
        return pl.ds(pl.multiple_of(place * width, width), width)

    moves = [(own, q, columns(q, False)) for q in range(classes)]
    moves += [(low, q, columns(q, True)) for q in range(side)]
    moves += [(high, q, columns(q + side, True)) for q in range(side)]
    arrive = [
        pltpu.make_async_copy(ref.at[q], recv_ref.at[:, cols], recv_sems.at[index])
        for index, (ref, q, cols) in enumerate(moves)
    ]
    load_in = [in_pieces(in_own, in0, weight_sems, 0), in_pieces(in_other, in1, weight_sems, PIECES)]
    load_out = [in_pieces(out_own, out0, weight_sems, 2 * PIECES), []]
    for (placed, _), source in zip(split_blocks(*reversed(in0.shape), width), (early, late)):
        for which, first, at, size in placed:
            if which == 1:
                load_out[1].append(
                    pltpu.make_async_copy(
                        source.at[pl.ds(at, size), :],
                        out1.at[:, pl.ds(first, width)],
                        weight_sems.at[3 * PIECES + len(load_out[1])],
                    )
                )
    for copy in arrive + load_in[0] + load_in[1]:
        copy.start()
    batch = GROUP if sources % GROUP == 0 else sources
    size = 4 * used * batch
    part_rows = used * batch
    pick = mask(iota((size, size), 0) == sorted_row(iota((1, size), 1), used, batch))
    spread = mask(iota((size, size), 1) == sorted_row(iota((size, 1), 0), used, batch))
    for copy in arrive:
        copy.wait()
    for copy in load_out[0] + load_out[1]:
        copy.start()
    for pair in range(classes):
        cols = slice(pair * 2 * width, (pair + 1) * 2 * width)
        for at_group in range(sources // batch):
            block = dot(pick, recv_ref[at_group * size : (at_group + 1) * size, cols]).astype(BF16)
            here = slice(at_group * part_rows, (at_group + 1) * part_rows)
            for part in range(HALVES):
                at = (part * peers + 2 * pair) * width
                start = part * 2 * part_rows
                x_ref[here, at : at + 2 * width] = block[start : start + part_rows, :]
                start = start + part_rows
                g_ref[here, at : at + 2 * width] = block[start : start + part_rows, :]
    model, hidden = in0.shape
    kept = [
        pltpu.make_async_copy(
            ref.at[:, pl.ds(at, model // PIECES)],
            rows_out.at[kind, :, pl.ds(at, model // PIECES)],
            kept_sems.at[kind, at * PIECES // model],
        )
        for kind, ref in enumerate((x_ref, g_ref))
        for at in range(0, model, model // PIECES)
    ]
    kept += [
        pltpu.make_async_copy(
            other_ref.at[kind],
            rows_out.at[kind, :, pl.ds(model, hidden)],
            kept_sems.at[kind, PIECES],
        )
        for kind in range(2)
    ]

    by_last = ((1,), (1,))
    acts, slopes, dpres = [], [], []
    for group, ref in enumerate((in0, in1)):
        for copy in load_in[group]:
            copy.wait()
        value, slope = gelu_parts(dot(x_ref[...], ref[...]))
        acts.append(value.astype(BF16))
        slopes.append(slope)
        (own_ref, other_ref)[group][0] = acts[group]
    for group, ref in enumerate((out0, out1)):
        for copy in load_out[group]:
            copy.wait()
        dpres.append((dot(g_ref[...], ref[...], by_last) * slopes[group]).astype(BF16))
        (own_ref, other_ref)[group][1] = dpres[group]
    for copy in kept:
        copy.start()
    leave = []
    for pair in range(classes):
        for part in range(HALVES):
            at = (part * peers + 2 * pair) * width
            cols = slice(at, at + 2 * width)
            given = dot(acts[0], out0[:, cols]) + dot(acts[1], out1[:, cols])
            back = dot(dpres[0], in0[cols, :], by_last) + dot(dpres[1], in1[cols, :], by_last)
            for kind, block in ((0, given), (1, back)):
                block = block.astype(BF16)
                for at_group in range(sources // batch):
                    start = at_group * size + (2 * part + kind) * part_rows
                    here = slice(at_group * part_rows, (at_group + 1) * part_rows)
                    held_ref[start : start + part_rows, :] = block[here, :]
        for at_group in range(sources // batch):
            here = slice(at_group * size, (at_group + 1) * size)
            ret_ref[here, pair * 2 * width : (pair + 1) * 2 * width] = dot(
                spread, held_ref[here, :]
            ).astype(BF16)
        other = ret_low.at[pair] if pair < side else ret_high.at[pair - side]
        leave.append(
            pltpu.make_async_copy(
                ret_ref.at[:, columns(pair, False)], ret_own.at[pair], ret_sems.at[2 * pair]
            )
        )
        leave.append(
            pltpu.make_async_copy(
                ret_ref.at[:, columns(pair, True)], other, ret_sems.at[2 * pair + 1]
            )
        )
        leave[-2].start()
        leave[-1].start()
    for copy in leave + kept:
        copy.wait()


def gradient_kernel(rows_ref, other_ref, own_ref, grad_in_ref, grad_out_ref):
    over_rows = ((0,), (0,))
    hidden = own_ref.shape[2]
    model = rows_ref.shape[2] - hidden
    units = slice(model, model + hidden)
    for at in range(0, model, hidden):
        cols = slice(at, at + hidden)
        part = dot(rows_ref[0, :, cols], own_ref[1], over_rows)
        part = part + dot(other_ref[0, :, cols], other_ref[1, :, units], over_rows)
        grad_in_ref[0, cols, :] = part.astype(BF16)
        part = dot(own_ref[0], rows_ref[1, :, cols], over_rows)
        part = part + dot(other_ref[0, :, units], other_ref[1, :, cols], over_rows)
        grad_out_ref[0, :, cols] = part.astype(BF16)


def add_kernel(own_ref, low_ref, high_ref, out_ref):
    side = low_ref.shape[0]
    for index in range(own_ref.shape[0]):
        ref = low_ref.at[index] if index < side else high_ref.at[index - side]
        out_ref[index] = (own_ref[index].astype(F32) + ref[...].astype(F32)).astype(BF16)


def combine_kernel(used, rows_ref, gates_ref, home_ref, mixed_ref, grad_ref):
    groups, all_rows, width = home_ref.shape
    tok_rows = mixed_ref.shape[0]
    slot = iota((all_rows, tok_rows), 0)
    row0, row1 = rows_ref[0:1, :], rows_ref[1:2, :]
    diagonal = iota((tok_rows, tok_rows), 0) == iota((tok_rows, tok_rows), 1)

    def column(row):
        return jnp.sum(jnp.where(diagonal, row, 0.0), axis=1, keepdims=True)

    total = home_ref[0].astype(F32)
    for group in range(1, groups):
        total = total + home_ref[group].astype(F32)
    high = total.astype(BF16)
    low = (total - high.astype(F32)).astype(BF16)
    hits = (slot == row0, slot == row1, (slot == row0 + used) | (slot == row1 + used))
    chosen = jnp.concatenate([mask(hit) for hit in hits], axis=1)
    picked = dot(chosen, jnp.concatenate([high, low], axis=1), ((0,), (0,)))
    picked = picked[:, :width] + picked[:, width:]
    mixed = (
        column(gates_ref[0:1, :]) * picked[:tok_rows]
        + column(gates_ref[1:2, :]) * picked[tok_rows : 2 * tok_rows]
    )
    mixed_ref[...] = mixed.astype(BF16)
    grad_ref[...] = picked[2 * tok_rows :].astype(BF16)


def call(kernel, shapes, cost, places, limit, scratch, *args):
    ins, outs = places
    flops, moved = cost
    return pl.pallas_call(
        kernel,
        out_shape=shapes,
        in_specs=[pl.BlockSpec(memory_space=place) for place in ins],
        out_specs=tuple(pl.BlockSpec(memory_space=place) for place in outs),
        scratch_shapes=scratch,
        cost_estimate=pl.CostEstimate(flops=flops, bytes_accessed=moved, transcendentals=0),
        compiler_params=pltpu.CompilerParams(vmem_limit_bytes=limit * 1024 * 1024),
    )(*args)


def struct(*shape, dtype=BF16):
    return jax.ShapeDtypeStruct(shape, dtype)


def body(tokens, cotangent, gates, routes, w_in, w_out):
    experts = lax.axis_size("dp")
    cuts = lax.axis_size("cuts")
    peers = cuts // HALVES
    classes = peers // 2
    side = classes // 2
    tok_rows, width = tokens.shape
    chosen = routes.shape[1]
    cap = 3 * chosen * tok_rows // (2 * experts)
    used = cap // HALVES
    rows = experts * used
    all_rows = 4 * rows
    model = width * cuts
    near, far = pltpu.VMEM, pltpu.HBM
    dma = pltpu.SemaphoreType.DMA
    swap = [(c, (c + peers) % cuts) for c in range(cuts)]
    up = [(c, c // peers * peers + (c + 1) % peers) for c in range(cuts)]
    down = [(d, c) for c, d in up]
    spread = [
        [d * cuts + h * peers + y for y in range(odd, peers, 2) for d in range(experts) for h in range(HALVES)]
        for odd in range(2)
    ]

    def to_partner(value):
        return lax.ppermute(value, "cuts", swap)

    def over_spread(value):
        pieces = value.reshape(classes * all_rows // FOUR, FOUR, width)
        pieces = lax.all_to_all(pieces, ("dp", "cuts"), 0, 0, tiled=True, axis_index_groups=spread)
        return pieces.reshape(classes, all_rows, width)

    in_own, out_own = w_in[0], w_out[0]
    hidden = in_own.shape[1]
    blocks = hidden // width + cuts
    early_rows, late_rows = (part[1] for part in split_blocks(hidden, model, width))
    routes_t, gates_t = routes.T, gates.T
    odd = (lax.axis_index("cuts") % 2).astype(jnp.int32).reshape(1)

    sent, places, early, late = call(
        functools.partial(place_kernel, experts, cap),
        (
            struct(classes, all_rows, width),
            struct(chosen, tok_rows, dtype=jnp.int32),
            struct(early_rows, width),
            struct(late_rows, width),
        ),
        (4 * all_rows * tok_rows * width, 4 * classes * all_rows * width),
        ([far] * 6, [far, near, far, far]),
        56,
        [
            pltpu.VMEM((chosen, tok_rows), jnp.int32),
            pltpu.VMEM((chosen, tok_rows), F32),
            pltpu.VMEM((tok_rows, width), BF16),
            pltpu.VMEM((tok_rows, width), BF16),
            pltpu.VMEM((all_rows, width), BF16),
            pltpu.VMEM((model, hidden), BF16),
            pltpu.VMEM((hidden, model), BF16),
            dma((4,)),
            dma((classes,)),
            dma((2 * PIECES,)),
            dma((blocks,)),
        ],
        routes_t,
        gates_t,
        tokens,
        cotangent,
        in_own,
        out_own,
    )
    early, late = lax.optimization_barrier((to_partner(early), late))
    late = to_partner(late)
    recv = over_spread(sent)
    low = lax.ppermute(recv[:side], "cuts", up)
    high = lax.ppermute(recv[side:], "cuts", down)
    early_in = early[: EARLY[0] * model].reshape(EARLY[0], model, width)
    late_in = late[: (hidden // width - EARLY[0]) * model].reshape(-1, model, width)
    in_other = jnp.concatenate([*early_in, *late_in], axis=1)
    ret_own, ret_low, ret_high, held_rows, own_units = call(
        functools.partial(expert_kernel, used),
        (
            struct(classes, all_rows, width),
            struct(side, all_rows, width),
            struct(classes - side, all_rows, width),
            struct(2, rows, model + hidden),
            struct(2, rows, hidden),
        ),
        (16 * rows * model * hidden, 12 * rows * model + 8 * model * hidden),
        ([pltpu.SMEM] + [far] * 8, [far] * 4 + [near]),
        60,
        [
            pltpu.VMEM((all_rows, peers * width), BF16),
            pltpu.VMEM((rows, model), BF16),
            pltpu.VMEM((rows, model), BF16),
            pltpu.VMEM((model, hidden), BF16),
            pltpu.VMEM((model, hidden), BF16),
            pltpu.VMEM((hidden, model), BF16),
            pltpu.VMEM((hidden, model), BF16),
            pltpu.VMEM((all_rows, 2 * width), BF16),
            pltpu.VMEM((all_rows, peers * width), BF16),
            pltpu.VMEM((2, rows, hidden), BF16),
            dma((peers,)),
            dma((3 * PIECES + blocks,)),
            dma((peers,)),
            dma((2, PIECES + 1)),
        ],
        odd,
        recv,
        low,
        high,
        in_own,
        out_own,
        in_other,
        early,
        late,
    )
    from_low = lax.ppermute(ret_low, "cuts", up)
    from_high = lax.ppermute(ret_high, "cuts", down)
    partner_rows = to_partner(held_rows)
    summed = call(
        add_kernel,
        (struct(classes, all_rows, width),),
        (classes * all_rows * width, 6 * classes * all_rows * width),
        ([near] * 3, [near]),
        16,
        [],
        ret_own,
        from_low,
        from_high,
    )[0]
    home = over_spread(summed)
    grad_in, grad_out = call(
        gradient_kernel,
        (struct(1, model, hidden), struct(1, hidden, model)),
        (16 * rows * model * hidden, 16 * model * hidden),
        ([near] * 3, [near] * 2),
        32,
        [],
        held_rows,
        partner_rows,
        own_units,
    )
    mixed, token_grad = call(
        functools.partial(combine_kernel, used),
        (struct(tok_rows, width), struct(tok_rows, width)),
        (6 * classes * all_rows * tok_rows * width, 2 * classes * all_rows * width),
        ([near] * 3, [near] * 2),
        16,
        [],
        places,
        gates_t,
        home,
    )
    return (mixed, token_grad, grad_in, grad_out)


def solution(mesh):
    in_specs = (
        P("dp", "cuts"),
        P("dp", "cuts"),
        P("dp", None),
        P("dp", None),
        P("dp", None, "cuts"),
        P("dp", "cuts", None),
    )
    out_specs = (P("dp", "cuts"), P("dp", "cuts"), P("dp", None, "cuts"), P("dp", "cuts", None))
    return jax.shard_map(body, mesh=mesh, in_specs=in_specs, out_specs=out_specs, check_vma=False)
```
